32 devices in a mesh: grp: 1, pen: 16 (over z, y, core), dep: 2 (over x), chan: 1.
Axes of the slice: x: 2, y: 2, z: 4, core: 2. Of those that a mesh axis runs over, the one named last changes fastest.
Arguments:
- misfit: float32 [6, 2048, 2048], P(('grp', 'chan'), ('pen', 'dep')), may hold values from -6 to 6
- kernel_spec: bfloat16 [6, 2, 2048, 2048], P('chan', None, ('pen', 'dep')), may hold values from -2.5 to 2.5
- model_vec: float32 [2, 16, 3072, 128], P(('grp', 'dep', 'chan'), 'pen'), may hold values from -1 to 1
- weight_vec: bfloat16 [2, 16, 3072, 128], P(('grp', 'dep', 'chan'), 'pen'), may hold values from 0.19921875 to 2
- active_list: int32 [2, 16, 2048], P(('grp', 'dep', 'chan'), 'pen'), may hold values from 0 to 2047, as said below
- send_counts: int32 [2, 16, 16], P(('grp', 'dep', 'chan'), 'pen'), may hold values from 0 to 192, as said below
Outputs:
- gradient: float32 [2, 2048, 2048], P(('grp', 'dep', 'chan'), 'pen')
- model_new: float32 [2, 16, 3072, 128], P(('grp', 'dep', 'chan'), 'pen')
- predicted: float32 [6, 2048, 2048], P(('grp', 'chan'), ('pen', 'dep'))
The draws below stay inside these ranges and needn't reach their ends.
Inputs may be any that keep to these rules, and one draw needn't show every extreme that they name: For each layer and band, active_list is a permutation of the 2048 block ids: the active blocks in increasing order, then the others in increasing order; the number of active blocks equals the sum of send_counts over owners, and every active block of a layer is active in all deeper layers. `send_counts`: each entry is at most 192, reached in every draw; the counts of a band sum to its number of active blocks.
All inputs are finite; a program needn't handle non-finite values.
Results may differ from the reference program's by a relative error of at most 0.0003.
Values sent between devices are 32-bit elements; how exact they have to be, the bound alone decides.
No kernel may reach another device: no remote copies, remote signals or barrier semaphores. Data moves between devices by JAX's collectives and lax.ppermute only.
A program may use at most 128 MiB of HBM per device.

```python
import math
import jax
import jax.numpy as jnp
from jax import lax

N = 2048
CH = 6
LAYERS = 2
BLK_DEV = 2048
CAP = 192
OWN = 3072
N_PEN = 16


def topography_counts(key):
    base_key = jax.random.fold_in(key, 17)
    key_height, key_order, key_room = jax.random.split(base_key, 3)
    height = jax.random.randint(key_height, (N_PEN, BLK_DEV), 0, LAYERS)
    depth_index = jnp.arange(LAYERS, dtype=jnp.int32)[:, None, None]
    active = (depth_index >= height[None]).astype(jnp.int32)
    listing = jnp.argsort(1 - active, axis=-1, stable=True).astype(jnp.int32)
    active_total = jnp.sum(active, axis=-1)
    scores = jax.random.randint(key_order, (LAYERS, N_PEN, N_PEN), 0, 1 << 20) * N_PEN + jnp.arange(N_PEN, dtype=jnp.int32)
    owner_order = jnp.argsort(scores, axis=-1).astype(jnp.int32)
    room_left = jax.random.randint(key_room, (LAYERS, N_PEN, N_PEN), BLK_DEV // N_PEN, CAP + 1)
    room_left = room_left.at[:, :, 0].set(CAP)
    room_ends = jnp.cumsum(room_left, axis=-1)
    taken = jnp.clip(active_total[..., None] - (room_ends - room_left), 0, room_left)
    inverse_order = jnp.argsort(owner_order, axis=-1)
    counts = jnp.take_along_axis(taken, inverse_order, axis=-1).astype(jnp.int32)
    return (listing, counts)


def draw_active_list(key, part):
    return topography_counts(key)[0]


def draw_send_counts(key, part):
    return topography_counts(key)[1]


def levels(key, shape, cuts, low, largest):
    def one(dim, blocks):
        heights = jax.random.uniform(jax.random.fold_in(jax.random.fold_in(key, 6), dim), (blocks,), jnp.float32, low / len(cuts), largest / len(cuts))
        return jnp.repeat(jnp.exp(heights), shape[dim] // blocks).reshape((-1,) + (1,) * (len(shape) - dim - 1))

    level = one(*cuts[0])
    for cut in cuts[1:]:
        level = level * one(*cut)
    return level


def bell_draw(rng, shape, width, bound, cuts=(), kind=jnp.bfloat16):
    result = jax.random.normal(rng, shape, jnp.float32) * width
    if len(cuts) > 0:
        result = levels(rng, shape, cuts, -0.22, 0.18) * result
    return jnp.clip(result, min=-bound, max=bound).astype(kind)


def setup_inputs(seed: int = 0, part: int = 0) -> dict:
    key_list = jax.random.split(jax.random.key(seed), 7)
    part_splits = jax.random.split(jax.random.fold_in(key_list[6], part), 7)
    misfit = bell_draw(part_splits[0], (CH, N, N), 1.0, 6.0, ((1, 32),), jnp.float32)
    kernel_spec = bell_draw(key_list[1], (CH, LAYERS, N, N), 0.4, 2.5, ((2, 32),))
    model_vec = jnp.clip(jax.random.uniform(part_splits[2], (LAYERS, N_PEN, OWN, 128), jnp.float32, -1.0, 1.0) * levels(part_splits[2], (LAYERS, N_PEN, OWN, 128), ((0, 2), (1, 16)), -0.4, 0.0), -1.0, 1.0)
    weight_vec = jnp.clip(jnp.exp(math.log(2.0) - 2.306499 * jax.random.uniform(part_splits[3], (LAYERS, N_PEN, OWN, 128), jnp.float32) ** levels(part_splits[3], (LAYERS, N_PEN, OWN, 128), ((0, 2), (1, 16)), -0.2, 0.2)), 0.19921875, 2.0).astype(jnp.bfloat16)
    active_list = draw_active_list(jax.random.fold_in(jax.random.fold_in(key_list[6], part), 71), part)
    send_counts = draw_send_counts(jax.random.fold_in(jax.random.fold_in(key_list[6], part), 71), part)
    return {"misfit": misfit, "kernel_spec": kernel_spec, "model_vec": model_vec, "weight_vec": weight_vec, "active_list": active_list, "send_counts": send_counts}


step_size = 0.5


def reference(misfit, kernel_spec, model_vec, weight_vec, active_list, send_counts):
    channel_ids = jnp.arange(CH, dtype=jnp.int32)
    imag_flags = (channel_ids == 2) | (channel_ids == 4)
    spectra = jnp.fft.fft2(misfit)
    rotated = jnp.where(imag_flags[:, None, None], -1j * spectra, spectra)

    def adjoint_layer(layer_index):
        kernels = jnp.swapaxes(lax.dynamic_index_in_dim(kernel_spec, layer_index, 1, keepdims=False), -1, -2).astype(jnp.float32)
        total_hat = jnp.sum(kernels * rotated, axis=0)
        return jnp.real(jnp.fft.ifft2(total_hat)).astype(jnp.float32)

    gradient = lax.map(adjoint_layer, jnp.arange(LAYERS, dtype=jnp.int32))

    slot_index = jnp.arange(CAP, dtype=jnp.int32)
    source_ids = jnp.arange(N_PEN, dtype=jnp.int32)[:, None, None]
    owner_ids = jnp.arange(N_PEN, dtype=jnp.int32)[None, :, None]

    def owner_layer(layer_index):
        grad_blocks = gradient[layer_index].reshape(N_PEN, BLK_DEV, 128)
        counts = send_counts[layer_index]
        listing = active_list[layer_index]
        slot_valid = slot_index[None, None, :] < counts[:, :, None]
        starts = jnp.cumsum(counts, axis=1) - counts
        in_list = jnp.minimum(starts[:, :, None] + slot_index, BLK_DEV - 1)
        block_ids = listing[source_ids, in_list]
        values = jnp.where(slot_valid[..., None], grad_blocks[source_ids, block_ids], 0.0)
        begins = jnp.cumsum(counts, axis=0) - counts
        places = begins[:, :, None] + slot_index
        safe_places = jnp.minimum(places, OWN - 1)
        current = model_vec[layer_index]
        scales = weight_vec[layer_index].astype(jnp.float32)
        updated = jnp.clip(current[owner_ids, safe_places] - step_size * scales[owner_ids, safe_places] * values, -1.0, 1.0)
        new_vec = current.at[owner_ids, jnp.where(slot_valid, places, OWN)].set(updated, mode="drop")
        model_grid = jnp.zeros((N_PEN, BLK_DEV, 128), jnp.float32)
        model_grid = model_grid.at[source_ids, jnp.where(slot_valid, block_ids, BLK_DEV)].set(updated, mode="drop")
        return new_vec, model_grid.reshape(N, N)

    model_new, model_grids = lax.map(owner_layer, jnp.arange(LAYERS, dtype=jnp.int32))
    model_hat = jnp.fft.fft2(model_grids)

    def forward_channel(channel_index):
        kernels = jnp.swapaxes(lax.dynamic_index_in_dim(kernel_spec, channel_index, 0, keepdims=False), -1, -2).astype(jnp.float32)
        total_hat = jnp.sum(kernels * model_hat, axis=0)
        turned_hat = jnp.where(imag_flags[channel_index], 1j * total_hat, total_hat)
        return jnp.real(jnp.fft.ifft2(turned_hat)).astype(jnp.float32)

    predicted = lax.map(forward_channel, channel_ids)
    return (gradient, model_new, predicted)
```

```python
import functools
import math

import jax
import jax.numpy as jnp
import ml_dtypes
import numpy as np
from jax import lax
from jax.experimental import pallas as pl
from jax.experimental.pallas import tpu as pltpu
from jax.sharding import PartitionSpec as P

inner_radix = 128
step_size = 0.5
highest = lax.Precision.HIGHEST
letters_free = "cdefghij"


def unit_table(length, direction):
    indices = jnp.arange(length, dtype=jnp.int32)
    phases = indices[:, None] * indices[None, :] % length
    angles = 2.0 * math.pi / length * phases.astype(jnp.float32)
    return (jnp.cos(angles), direction * jnp.sin(angles))


def twiddle_table(outer_size, inner_size, direction):
    length = outer_size * inner_size
    phases = (
        jnp.arange(outer_size, dtype=jnp.int32)[:, None]
        * jnp.arange(inner_size, dtype=jnp.int32)[None, :]
        % length
    )
    angles = 2.0 * math.pi / length * phases.astype(jnp.float32)
    return (jnp.cos(angles), direction * jnp.sin(angles))


def contract(formula, operand, tables, real_only):
    product_one = jnp.einsum(formula, operand[0], tables[0], precision=highest)
    if operand[1] is None:
        return (product_one, jnp.einsum(formula, operand[0], tables[1], precision=highest))
    real_value = product_one - jnp.einsum(formula, operand[1], tables[1], precision=highest)
    if real_only:
        return (real_value, None)
    imag_value = jnp.einsum(formula, operand[0], tables[1], precision=highest) + jnp.einsum(
        formula, operand[1], tables[0], precision=highest
    )
    return (real_value, imag_value)


def transform(operand, dimension, direction, real_only):
    full_shape = operand[0].shape
    length = full_shape[dimension]
    inner_size = min(inner_radix, length)
    outer_size = length // inner_size
    split_shape = full_shape[:dimension] + (outer_size, inner_size) + full_shape[dimension + 1 :]
    leading = letters_free[:dimension]
    trailing = letters_free[dimension : len(full_shape) - 1]
    pieces = tuple((None if member is None else member.reshape(split_shape) for member in operand))
    sectioned = contract(
        leading + "ab" + trailing + ",ak->" + leading + "kb" + trailing,
        pieces,
        unit_table(outer_size, direction),
        False,
    )
    twist_real, twist_imag = twiddle_table(outer_size, inner_size, direction)
    twist_shape = (outer_size, inner_size) + (1,) * len(trailing)
    twist_real = twist_real.reshape(twist_shape)
    twist_imag = twist_imag.reshape(twist_shape)
    rotated = (
        sectioned[0] * twist_real - sectioned[1] * twist_imag,
        sectioned[0] * twist_imag + sectioned[1] * twist_real,
    )
    factor = 1.0 / length if direction > 0 else 1.0
    if len(trailing) == 0:
        result = contract(
            leading + "kb,bm->" + leading + "km",
            rotated,
            unit_table(inner_size, direction),
            real_only,
        )
        return tuple(
            (
                (
                    None
                    if member is None
                    else jnp.swapaxes(member, -1, -2).reshape(full_shape) * factor
                )
                for member in result
            )
        )
    result = contract(
        leading + "kb" + trailing + ",bm->" + leading + "mk" + trailing,
        rotated,
        unit_table(inner_size, direction),
        real_only,
    )
    return tuple(
        (None if member is None else member.reshape(full_shape) * factor for member in result)
    )


def exclusive_sum(counts):
    places = jnp.arange(counts.shape[0], dtype=jnp.int32)
    return jnp.sum(jnp.where(places[None, :] < places[:, None], counts[None, :], 0), axis=1)


def imag_channels(chan_place, chan_width):
    channel_ids = chan_place * chan_width + jnp.arange(chan_width, dtype=jnp.int32)
    return ((channel_ids == 2) | (channel_ids == 4))[:, None, None]


def channel_weighted(kernel_view, along):
    total = None
    for channel in range(kernel_view.shape[0]):
        kernel_now = kernel_view[channel].astype(jnp.float32)
        term = kernel_now * along[channel][None, None]
        total = term if total is None else total + term
    return total.reshape(-1, along.shape[1], along.shape[2])


def layer_weighted(kernel_view, grouped):
    ordered = jnp.swapaxes(grouped, 0, 1)
    outputs = []
    for channel in range(kernel_view.shape[0]):
        products = kernel_view[channel].astype(jnp.float32) * ordered
        outputs.append(jnp.sum(products, axis=(0, 1)))
    return jnp.stack(outputs)


def local_general(misfit, kernel_spec, model_vec, weight_vec, active_list, send_counts):
    pen_count = lax.axis_size("pen")
    dep_count = lax.axis_size("dep")
    chan_count = lax.axis_size("chan")
    chan_width, band_width, grid_width = misfit.shape
    column_width = kernel_spec.shape[2]
    kernel_view = kernel_spec.reshape(chan_width, dep_count, chan_count, column_width, grid_width)
    turned = imag_channels(lax.axis_index("chan"), chan_width)
    spectra_real, spectra_imag = transform((misfit, None), 2, -1.0, False)
    columns = (
        lax.all_to_all(spectra_real, ("pen", "dep"), split_axis=2, concat_axis=1, tiled=True),
        lax.all_to_all(spectra_imag, ("pen", "dep"), split_axis=2, concat_axis=1, tiled=True),
    )
    columns = (jnp.swapaxes(columns[0], 1, 2), jnp.swapaxes(columns[1], 1, 2))
    misfit_hat = transform(columns, 2, -1.0, False)
    along_real = jnp.where(turned, misfit_hat[1], misfit_hat[0])
    along_imag = jnp.where(turned, -misfit_hat[0], misfit_hat[1])
    partial_real = channel_weighted(kernel_view, along_real)
    partial_imag = channel_weighted(kernel_view, along_imag)
    fields = transform((partial_real, partial_imag), 2, 1.0, False)
    outgoing = tuple(
        (
            member.reshape(dep_count, chan_count, column_width, pen_count, -1)
            .transpose(3, 0, 1, 4, 2)
            .reshape(pen_count * dep_count, chan_count, -1, column_width)
            for member in fields
        )
    )
    arrived = (
        lax.all_to_all(outgoing[0], ("pen", "dep"), split_axis=0, concat_axis=3, tiled=True),
        lax.all_to_all(outgoing[1], ("pen", "dep"), split_axis=0, concat_axis=3, tiled=True),
    )
    real_fields = transform(arrived, 3, 1.0, True)[0]
    gradient = lax.psum_scatter(real_fields, "chan", scatter_dimension=1, tiled=True).reshape(
        1, -1, grid_width
    )
    blocks = gradient.reshape(-1, 128)
    block_count = blocks.shape[0]
    owner_length = model_vec.shape[2]
    slot_cap = owner_length // pen_count
    counts = send_counts.reshape(pen_count)
    starts = exclusive_sum(counts)
    slot_index = jnp.arange(slot_cap, dtype=jnp.int32)
    slot_valid = slot_index[None, :] < counts[:, None]
    in_list = jnp.minimum(starts[:, None] + slot_index[None, :], block_count - 1)
    listing = active_list.reshape(block_count)
    block_ids = listing[in_list]
    outgoing_blocks = jnp.where(slot_valid[:, :, None], blocks[block_ids], 0.0)
    incoming, arrived_counts = (
        lax.all_to_all(outgoing_blocks, "pen", split_axis=0, concat_axis=0, tiled=True),
        lax.all_to_all(counts.astype(jnp.float32), "pen", split_axis=0, concat_axis=0, tiled=True),
    )
    source_counts = arrived_counts.astype(jnp.int32)
    begins = exclusive_sum(source_counts)
    filled = slot_index[None, :] < source_counts[:, None]
    places = begins[:, None] + slot_index[None, :]
    safe_places = jnp.minimum(places, owner_length - 1)
    current = model_vec.reshape(owner_length, 128)
    scales = weight_vec.reshape(owner_length, 128)
    updated = jnp.clip(
        current[safe_places] - step_size * scales[safe_places].astype(jnp.float32) * incoming,
        -1.0,
        1.0,
    )
    targets = jnp.where(filled, places, owner_length)
    model_new = current.at[targets].set(updated, mode="drop").reshape(model_vec.shape)
    returned = lax.all_to_all(updated, "pen", split_axis=0, concat_axis=0, tiled=True)
    drop_ids = jnp.where(slot_valid, block_ids, block_count)
    model_grid = jnp.zeros((block_count, 128), jnp.float32).at[drop_ids].set(returned, mode="drop")
    model_grid = model_grid.reshape(-1, grid_width)
    surface_field = transform((model_grid, None), 1, -1.0, False)
    moved_columns = (
        lax.all_to_all(surface_field[0], ("pen", "dep"), split_axis=1, concat_axis=0, tiled=True),
        lax.all_to_all(surface_field[1], ("pen", "dep"), split_axis=1, concat_axis=0, tiled=True),
    )
    ordered = tuple(
        (
            member.reshape(pen_count, dep_count, -1, column_width)
            .transpose(1, 3, 0, 2)
            .reshape(dep_count, column_width, grid_width)
            for member in moved_columns
        )
    )
    model_hat = transform(ordered, 2, -1.0, False)
    layers_all = (
        lax.all_gather(model_hat[0], "chan", axis=0, tiled=True),
        lax.all_gather(model_hat[1], "chan", axis=0, tiled=True),
    )
    grouped = tuple(
        (member.reshape(chan_count, dep_count, column_width, grid_width) for member in layers_all)
    )
    summed_real = layer_weighted(kernel_view, grouped[0])
    summed_imag = layer_weighted(kernel_view, grouped[1])
    data_real = jnp.where(turned, -summed_imag, summed_real)
    data_imag = jnp.where(turned, summed_real, summed_imag)
    surface_rows = transform((data_real, data_imag), 2, 1.0, False)
    rows_back = (
        lax.all_to_all(surface_rows[0], ("pen", "dep"), split_axis=2, concat_axis=1, tiled=True),
        lax.all_to_all(surface_rows[1], ("pen", "dep"), split_axis=2, concat_axis=1, tiled=True),
    )
    predicted = jnp.swapaxes(transform(rows_back, 1, 1.0, True)[0], 1, 2)
    return (gradient, model_new, predicted)


RADIX = 16
LANES = 128
f32 = jnp.float32
bf16 = jnp.bfloat16


def two_terms(table):
    high = table.astype(ml_dtypes.bfloat16)
    low = (table - high.astype(np.float64)).astype(ml_dtypes.bfloat16)
    return (high, low)


def row_frequencies(n, devices, width):
    device = np.arange(devices)[:, None]
    column = np.arange(width // 2)[None, :]
    return width * device + 2 * column + (device >= devices // 2)


@functools.cache
def row_tables(n, devices):
    width = n // devices
    freq = row_frequencies(n, devices, width).reshape(devices // 4, 1, LANES)
    y = np.arange(n // 2)[None, :, None]
    angle = 2.0 * math.pi / n * (freq * y % n)
    real, imag = np.cos(angle), -np.sin(angle)
    imag[0, :, 0] = 1.0 - 2.0 * (np.arange(n // 2) % 2)
    forward = np.concatenate([real, imag], axis=2)
    inverse = 2.0 * forward
    inverse[0, :, 0] *= 0.5
    inverse[0, :, LANES] *= 0.5
    inverse = inverse.swapaxes(1, 2) / float(n) ** 2
    return (two_terms(forward), two_terms(inverse))


@functools.cache
def column_tables():
    k = np.arange(RADIX)[:, None, None]
    m = np.arange(LANES)[None, :, None]
    b = np.arange(LANES)[None, None, :]
    n = RADIX * LANES
    angle = 2.0 * math.pi / n * ((16 * b * m + b * k) % n)
    real, sine = np.cos(angle), np.sin(angle)
    forward = np.concatenate(
        [np.concatenate([real, sine], axis=2), np.concatenate([-sine, real], axis=2)], axis=1
    )
    return (two_terms(forward), two_terms(forward.swapaxes(1, 2)))


def split(value):
    high = value.astype(bf16)
    return high, (value - high.astype(f32)).astype(bf16)


def dot(a, b):
    return jnp.dot(a, b, preferred_element_type=f32)


def dot3(left, right):
    return dot(left[0], right[0]) + (dot(left[0], right[1]) + dot(left[1], right[0]))


def turn(value, shift):
    shift %= LANES
    return value if shift == 0 else pltpu.roll(value, shift, value.ndim - 1)


def lane_of(shape):
    return lax.broadcasted_iota(jnp.int32, shape, len(shape) - 1)


def quad_transpose(parts):
    lane = lane_of(parts[0].shape)
    low, even = lane < 64, lane % 64 < 32
    a, b, c, d = parts
    a, c = jnp.where(low, a, turn(c, 64)), jnp.where(low, turn(a, 64), c)
    b, d = jnp.where(low, b, turn(d, 64)), jnp.where(low, turn(b, 64), d)
    a, b = jnp.where(even, a, turn(b, 32)), jnp.where(even, turn(a, 96), b)
    c, d = jnp.where(even, c, turn(d, 32)), jnp.where(even, turn(c, 96), d)
    return [a, b, c, d]


def radix4(x, sign):
    (r0, i0), (r1, i1), (r2, i2), (r3, i3) = x
    ar, ai, br, bi = r0 + r2, i0 + i2, r0 - r2, i0 - i2
    cr, ci, dr, di = r1 + r3, i1 + i3, r1 - r3, i1 - i3
    if sign < 0:
        turned = (di, -dr)
    else:
        turned = (-di, dr)
    return [
        (ar + cr, ai + ci),
        (br + turned[0], bi + turned[1]),
        (ar - cr, ai - ci),
        (br - turned[0], bi - turned[1]),
    ]


def radix16(x, sign):
    inner = [radix4([x[4 * a1 + a0] for a1 in range(4)], sign) for a0 in range(4)]
    outputs = [None] * RADIX
    for k0 in range(4):
        column = []
        for a0 in range(4):
            re, im = inner[a0][k0]
            power = a0 * k0 % RADIX
            if power == 4:
                re, im = (im, -re) if sign < 0 else (-im, re)
            elif power == 2 or power == 6:
                scale = math.sqrt(0.5)
                c = scale if power == 2 else -scale
                if sign < 0:
                    re, im = re * c + im * scale, im * c - re * scale
                else:
                    re, im = re * c - im * scale, im * c + re * scale
            elif power != 0:
                c = math.cos(2.0 * math.pi * power / RADIX)
                s = sign * math.sin(2.0 * math.pi * power / RADIX)
                re, im = re * c - im * s, re * s + im * c
            column.append((re, im))
        for k1, value in enumerate(radix4(column, sign)):
            outputs[4 * k1 + k0] = value
    return outputs


def forward_blocks(load, work):
    @pl.loop(0, LANES // 8)
    def _(step):
        first = pl.multiple_of(step * 8, 8)
        outputs = radix16([load(a, first) for a in range(RADIX)], -1)
        for k, (re, im) in enumerate(outputs):
            work[k, pl.ds(first, 8), :] = re
            work[k, pl.ds(first + LANES, 8), :] = im


def inverse_blocks(work, store):
    @pl.loop(0, LANES // 8)
    def _(step):
        first = pl.multiple_of(step * 8, 8)
        inputs = [
            (work[k, pl.ds(first, 8), :], work[k, pl.ds(first + LANES, 8), :]) for k in range(RADIX)
        ]
        for a, (re, im) in enumerate(radix16(inputs, 1)):
            store(a, first, re, im)


def column_product(tables, k, value):
    return dot3((tables[0][k], tables[1][k]), split(value))


def part_kernel(flags, spec, sent, kept, wide):
    wide[...] = spec[0].astype(f32)
    upper = flags[0]
    half = kept.shape[1]
    for i in range(half):
        sent[0, half - 1 - i : half - i, :] = wide[pl.ds(2 * i + 1 - upper, 1), :]
        kept[0, i : i + 1, :] = wide[pl.ds(2 * i + upper, 1), :]


def part_spec(flags, spec):
    count, width, n = spec.shape
    half = width // 2
    block = pl.BlockSpec((1, half, n), lambda s: (s, 0, 0))
    return pl.pallas_call(
        part_kernel,
        grid=(count,),
        out_shape=[jax.ShapeDtypeStruct((count, half, n), f32)] * 2,
        in_specs=[
            pl.BlockSpec(memory_space=pltpu.SMEM),
            pl.BlockSpec((1, width, n), lambda s: (s, 0, 0)),
        ],
        out_specs=[block, block],
        scratch_shapes=[pltpu.VMEM((width, n), f32)],
        name="part_spec",
    )(flags, spec)


TILE_ROWS = {0: (0, 0), 1: (0, 32), 2: (0, 64), 3: (0, 96), 4: (1, 0), 5: (1, 32)}
EDGE_LANES = {4: 64, 0: 65, 2: 66, 5: 96, 1: 97, 3: 98}


def pair_kernel(flags, kept, got, edge, pairs_a, pairs_b, own, mirror, room, rows):
    k = pl.program_id(0)
    n = own.shape[1]

    @pl.when(k == 0)
    def _():
        first, upper = flags[1], flags[0]
        for layer in range(2):
            for channel in range(6):
                line = 2 * channel + layer
                weight = -0.5 if channel in (2, 4) else 0.5
                tile, place = TILE_ROWS[channel]
                base = (2 * layer + tile) * LANES + place
                own[base : base + 32, :] = (kept[line] * 0.5).astype(bf16)
                room[0:1, :] = jnp.where(first == 1, kept[line, 0:1, :], edge[line])
                room[1:33, :] = got[line]
                mirror[base : base + 32, :] = (
                    jnp.where(upper == 1, room[1:33, :], room[0:32, :]) * weight
                ).astype(bf16)
            base = (2 * layer + 1) * LANES + 64
            for target, weights in ((own, (0.5, 0.5)), (mirror, (0.5, -0.5))):
                rows[...] = jnp.zeros_like(rows)
                for channel, lane in EDGE_LANES.items():
                    weight = weights[1] if channel in (2, 4) else weights[0]
                    rows[lane - 64 : lane - 63, :] = edge[2 * channel + layer] * weight
                target[base : base + 64, :] = rows[...].astype(bf16)

    lane = lax.broadcasted_iota(jnp.int32, (LANES, n), 1)
    wanted = RADIX * lax.broadcasted_iota(jnp.int32, (LANES, n), 0) + k
    contract_last = (((1,), (1,)), ((), ()))
    total = lax.dot_general(
        (lane == wanted).astype(f32).astype(bf16), own[...], contract_last, preferred_element_type=f32
    ) + lax.dot_general(
        (lane == lax.rem(n - wanted, n)).astype(f32).astype(bf16),
        mirror[...],
        contract_last,
        preferred_element_type=f32,
    )
    for layer in range(2):
        pairs_a[layer] = total[:, 2 * layer * LANES : (2 * layer + 1) * LANES]
        pairs_b[layer] = total[:, (2 * layer + 1) * LANES : (2 * layer + 2) * LANES]


def pair_spec(flags, kept, got, edge):
    count, half, n = kept.shape
    whole = pl.BlockSpec((count, half, n), lambda k: (0, 0, 0))
    out = pl.BlockSpec((2, LANES, LANES), lambda k: (0, k, 0))
    return pl.pallas_call(
        pair_kernel,
        grid=(RADIX,),
        out_shape=[jax.ShapeDtypeStruct((2, n, LANES), f32)] * 2,
        in_specs=[
            pl.BlockSpec(memory_space=pltpu.SMEM),
            whole,
            whole,
            pl.BlockSpec((count, 1, n), lambda k: (0, 0, 0)),
        ],
        out_specs=[out, out],
        scratch_shapes=[
            pltpu.VMEM((4 * LANES, n), bf16),
            pltpu.VMEM((4 * LANES, n), bf16),
            pltpu.VMEM((40, n), f32),
            pltpu.VMEM((64, n), f32),
        ],
        compiler_params=pltpu.CompilerParams(vmem_limit_bytes=44 << 20),
        name="pair_spec",
    )(flags, kept, got, edge)


def misfit_rows_kernel(misfit, high, low, out_a, out_b, halves_high, halves_low):
    s = pl.program_id(0)
    channels, rows, n = misfit.shape

    @pl.when(s == 0)
    def _():
        value = misfit[...].reshape(channels * rows, n)
        first, second = value[:, : n // 2], value[:, n // 2 :]
        for index, combined in enumerate((first + second, first - second)):
            halves_high[index], halves_low[index] = split(combined)

    side = s // (pl.num_programs(0) // 2)
    result = dot3((halves_high[side], halves_low[side]), (high[0], low[0]))
    real = [result[rows * c : rows * (c + 1), :LANES] for c in range(channels)]
    imag = [result[rows * c : rows * (c + 1), LANES:] for c in range(channels)]
    parts = (quad_transpose(real[:4]), quad_transpose(imag[:4]))
    for index in range(4):
        out_a[index, :, :LANES] = parts[0][index]
        out_a[index, :, LANES:] = parts[1][index]
    for index, value in enumerate(quad_transpose([real[4], real[5], imag[4], imag[5]])):
        out_b[index] = value


def misfit_rows(misfit, tables, devices):
    channels, rows, n = misfit.shape
    table = pl.BlockSpec((1, n // 2, 2 * LANES), lambda s: (s, 0, 0))
    return pl.pallas_call(
        misfit_rows_kernel,
        grid=(devices // 4,),
        out_shape=[
            jax.ShapeDtypeStruct((devices, rows, 2 * LANES), f32),
            jax.ShapeDtypeStruct((devices, rows, LANES), f32),
        ],
        in_specs=[pl.BlockSpec((channels, rows, n), lambda s: (0, 0, 0)), table, table],
        out_specs=[
            pl.BlockSpec((4, rows, 2 * LANES), lambda s: (s, 0, 0)),
            pl.BlockSpec((4, rows, LANES), lambda s: (s, 0, 0)),
        ],
        scratch_shapes=[pltpu.VMEM((2, channels * rows, n // 2), bf16)] * 2,
        compiler_params=pltpu.CompilerParams(vmem_limit_bytes=40 << 20),
        name="misfit_rows",
    )(misfit, *tables)


def inverse_step(lhs, high, low, sums):
    s = pl.program_id(0)
    steps = pl.num_programs(0)
    product = dot3(split(lhs), (high[0], low[0]))
    side = s // (steps // 2)
    fresh = s % (steps // 2) == 0

    @pl.when(fresh)
    def _():
        sums[side] = product

    @pl.when(jnp.logical_not(fresh))
    def _():
        sums[side] += product


def predicted_kernel_b(spectra, high, low, out, sums):
    rows, n = out.shape[1:]
    c4r, c5r, c4i, c5i = quad_transpose([spectra[index] for index in range(4)])
    lhs = jnp.concatenate(
        [jnp.concatenate([c4r, c4i], axis=1), jnp.concatenate([c5r, c5i], axis=1)], axis=0
    )
    inverse_step(lhs, high, low, sums)

    @pl.when(pl.program_id(0) == pl.num_programs(0) - 1)
    def _():
        for channel in range(2):
            even, odd = sums[0, channel * rows : (channel + 1) * rows], sums[1, channel * rows : (channel + 1) * rows]
            out[channel, :, : n // 2] = even + odd
            out[channel, :, n // 2 :] = even - odd


def predicted_kernel_a(spectra, high, low, before, out, sums):
    rows, n = out.shape[1:]
    real = quad_transpose([spectra[index, :, :LANES] for index in range(4)])
    imag = quad_transpose([spectra[index, :, LANES:] for index in range(4)])
    lhs = jnp.concatenate(
        [jnp.concatenate(pair, axis=1) for pair in zip(real, imag)], axis=0
    )
    inverse_step(lhs, high, low, sums)

    @pl.when(pl.program_id(0) == pl.num_programs(0) - 1)
    def _():
        for channel in range(4):
            even, odd = sums[0, channel * rows : (channel + 1) * rows], sums[1, channel * rows : (channel + 1) * rows]
            out[channel, :, : n // 2] = even + odd
            out[channel, :, n // 2 :] = even - odd


def predicted_rows(spectra, tables, before, n):
    devices, rows, lanes = spectra.shape
    table = pl.BlockSpec((1, 2 * LANES, n // 2), lambda s: (s, 0, 0))
    chunk = pl.BlockSpec((4, rows, lanes), lambda s: (s, 0, 0))
    channels = 2 if before is None else 4
    return pl.pallas_call(
        predicted_kernel_b if before is None else predicted_kernel_a,
        grid=(devices // 4,),
        out_shape=jax.ShapeDtypeStruct((6, rows, n), f32),
        in_specs=[chunk, table, table] + ([] if before is None else [pl.BlockSpec(memory_space=pl.ANY)]),
        out_specs=pl.BlockSpec((channels, rows, n), lambda s: (2 if before is None else 0, 0, 0)),
        scratch_shapes=[pltpu.VMEM((2, channels * rows, n // 2), f32)],
        input_output_aliases={} if before is None else {3: 0},
        compiler_params=pltpu.CompilerParams(vmem_limit_bytes=32 << 20),
        name="predicted_rows_b" if before is None else "predicted_rows_a",
    )(spectra, *tables, *([] if before is None else [before]))


def write_sum(total, layer0, layer1):
    return jnp.where(lane_of(total.shape) < 64, layer0, layer1)


def adjoint_kernel_a(flags, spectra, pairs, high, low, sums, edges, work):
    first = flags[1] == 1
    lane8 = lane_of((8, LANES))
    packed = jnp.logical_and(lane8 % 32 == 0, first)

    def load(a, row):
        real = spectra[pl.ds(a * LANES + row, 8), :LANES]
        imag = spectra[pl.ds(a * LANES + row, 8), LANES:]
        edges[pl.ds(a * LANES + row, 8), :] = jnp.where(
            (lane8 == 65) | (lane8 == 97), turn(imag, 65), turn(imag, 2)
        )
        return (real, jnp.where(packed, 0.0, imag))

    forward_blocks(load, work)
    lane = lane_of((LANES, LANES))
    turned = lane // 32 == 2

    @pl.loop(0, RADIX)
    def _(k):
        spectrum = column_product((high, low), k, work[k])
        real, imag = spectrum[:LANES], spectrum[LANES:]
        real, imag = jnp.where(turned, imag, real), jnp.where(turned, -real, imag)
        row = pl.multiple_of(k * LANES, LANES)
        for index, value in enumerate((real, imag)):
            v0, v1 = value * pairs[0, pl.ds(row, LANES), :], value * pairs[1, pl.ds(row, LANES), :]
            both = jnp.where(lane < 64, v0 + turn(v0, 64), v1 + turn(v1, 64))
            sums[index, pl.ds(row, LANES), :] = both + turn(both, 96)


def adjoint_columns_a(flags, spectra, pairs, tables):
    n = spectra.shape[0]
    return pl.pallas_call(
        adjoint_kernel_a,
        out_shape=[
            jax.ShapeDtypeStruct((2, n, LANES), f32),
            jax.ShapeDtypeStruct((n, LANES), f32),
        ],
        in_specs=[pl.BlockSpec(memory_space=pltpu.SMEM)] + [pl.BlockSpec(memory_space=pltpu.VMEM)] * 4,
        scratch_shapes=[pltpu.VMEM((RADIX, 2 * LANES, LANES), f32)],
        compiler_params=pltpu.CompilerParams(vmem_limit_bytes=32 << 20),
        name="adjoint_columns_a",
    )(flags, spectra, pairs, *tables)


def adjoint_kernel_b(flags, spectra, edges, sums, pairs, high, low, high_i, low_i, out, work, fields):
    first = flags[1] == 1
    lane8 = lane_of((8, LANES))
    packed = jnp.logical_and(lane8 % 32 == 0, first)
    main = lane8 < 64
    here = (lane8 == 64) | (lane8 == 96)
    moved = (lane8 == 65) | (lane8 == 66) | (lane8 == 97) | (lane8 == 98)

    def load(a, row):
        value = spectra[pl.ds(a * LANES + row, 8), :]
        edge = edges[pl.ds(a * LANES + row, 8), :]
        real = jnp.where(main | here, value, jnp.where(moved, edge, 0.0))
        imag = jnp.where(main, jnp.where(packed, 0.0, turn(value, 64)), 0.0)
        return (real, imag)

    forward_blocks(load, work)
    lane = lane_of((LANES, LANES))
    turned = (lane < 32) | (lane == 64) | (lane == 66)
    low_main = lane < 32
    high_main = (lane >= 64) & (lane < 96)

    @pl.loop(0, RADIX)
    def _(k):
        spectrum = column_product((high, low), k, work[k])
        real, imag = spectrum[:LANES], spectrum[LANES:]
        real, imag = jnp.where(turned, imag, real), jnp.where(turned, -real, imag)
        row = pl.multiple_of(k * LANES, LANES)
        parts = []
        for index, value in enumerate((real, imag)):
            t0, t1 = (value * pairs[layer, pl.ds(row, LANES), :] for layer in range(2))
            t0, t1 = t0 + turn(t0, 96), t1 + turn(t1, 96)
            e0, e1 = (t + turn(t, 127) + turn(t, 126) for t in (t0, t1))
            total = sums[index, pl.ds(row, LANES), :]
            parts.append(
                jnp.where(
                    low_main,
                    total + t0,
                    jnp.where(
                        high_main,
                        total + turn(t1, 64),
                        jnp.where(
                            lane == 32, turn(e0, 96), jnp.where(lane == 96, turn(e1, 32), 0.0)
                        ),
                    ),
                )
            )
        work[k] = column_product((high_i, low_i), k, jnp.concatenate(parts, axis=0))

    def store(a, row, real, imag):
        edge = turn(real, 96)
        fields[0, pl.ds(a * LANES + row, 8), :] = real
        fields[1, pl.ds(a * LANES + row, 8), :] = jnp.where(
            jnp.logical_and(lane8 % 64 == 0, first), edge, imag
        )

    inverse_blocks(work, store)
    lane64 = lane_of((64, LANES))
    for band in range(RADIX):
        pieces = [
            fields[part, band * LANES + 64 * side : band * LANES + 64 * side + 64, :]
            for part in range(2)
            for side in range(2)
        ]
        for layer in range(2):
            shifted = [turn(piece, 32 * q - 64 * layer) for q, piece in enumerate(pieces)]
            out[2 * band + layer] = jnp.where(
                lane64 < 32,
                shifted[0],
                jnp.where(lane64 < 64, shifted[1], jnp.where(lane64 < 96, shifted[2], shifted[3])),
            )


def adjoint_columns_b(flags, spectra, edges, sums, pairs, tables, inverse_tables):
    n = spectra.shape[0]
    return pl.pallas_call(
        adjoint_kernel_b,
        out_shape=jax.ShapeDtypeStruct((2 * RADIX, 64, LANES), f32),
        in_specs=[pl.BlockSpec(memory_space=pltpu.SMEM)] + [pl.BlockSpec(memory_space=pltpu.VMEM)] * 8,
        scratch_shapes=[
            pltpu.VMEM((RADIX, 2 * LANES, LANES), f32),
            pltpu.VMEM((2, n, LANES), f32),
        ],
        compiler_params=pltpu.CompilerParams(vmem_limit_bytes=40 << 20),
        name="adjoint_columns_b",
    )(flags, spectra, edges, sums, pairs, *tables, *inverse_tables)


def forward_kernel_b(flags, moved, pairs, high, low, high_i, low_i, out, edges, model, work, fields):
    first = flags[1] == 1
    lane64 = lane_of((64, LANES))
    low_main = lane64 < 32
    high_main = (lane64 >= 64) & (lane64 < 96)
    edge_lane = (lane64 == 32) | (lane64 == 96)
    for band in range(RADIX):
        value0, value1 = moved[2 * band], moved[2 * band + 1]

        def pick(q):
            return jnp.where(
                low_main,
                turn(value0, -32 * q),
                jnp.where(high_main, turn(value1, 64 - 32 * q), 0.0),
            )

        for side in range(2):
            real, imag = pick(side), pick(2 + side)
            row = band * LANES + 64 * side
            fields[0, row : row + 64, :] = jnp.where(edge_lane, turn(imag, 32), real)
            fields[1, row : row + 64, :] = jnp.where(
                jnp.logical_and(lane64 % 64 == 0, first), 0.0, imag
            )

    def load(a, row):
        return tuple(fields[part, pl.ds(a * LANES + row, 8), :] for part in range(2))

    forward_blocks(load, work)
    lane = lane_of((LANES, LANES))
    turned = (lane < 32) | (lane == 64) | (lane == 66)

    @pl.loop(0, RADIX)
    def _(k):
        spectrum = column_product((high, low), k, work[k])
        row = pl.multiple_of(k * LANES, LANES)
        totals = []
        for part in range(2):
            value = spectrum[part * LANES : (part + 1) * LANES]
            spread = []
            for layer in range(2):
                main = jnp.where(lane < 32, turn(value, -64 * layer), 0.0)
                main = main + turn(main, 32)
                main = main + turn(main, 64)
                model[layer, part, pl.ds(row, LANES), :] = main
                at = 32 + 64 * layer
                edge = jnp.broadcast_to(value[:, at : at + 1], value.shape)
                spread.append(jnp.where(lane < 64, main, edge))
            totals.append(
                spread[0] * pairs[0, pl.ds(row, LANES), :] + spread[1] * pairs[1, pl.ds(row, LANES), :]
            )
        real, imag = totals
        real, imag = jnp.where(turned, -imag, real), jnp.where(turned, real, imag)
        work[k] = column_product((high_i, low_i), k, jnp.concatenate([real, imag], axis=0))

    lane8 = lane_of((8, LANES))

    def store(a, row, real, imag):
        imag = jnp.where(jnp.logical_and(lane8 % 32 == 0, first), turn(real, 64), imag)
        out[pl.ds(a * LANES + row, 8), :] = jnp.where(lane8 < 64, real, turn(imag, 64))
        edges[pl.ds(a * LANES + row, 8), :] = real

    inverse_blocks(work, store)


def forward_columns_b(flags, moved, pairs, tables, inverse_tables, n):
    return pl.pallas_call(
        forward_kernel_b,
        out_shape=[
            jax.ShapeDtypeStruct((n, LANES), f32),
            jax.ShapeDtypeStruct((n, LANES), f32),
            jax.ShapeDtypeStruct((2, 2, n, LANES), f32),
        ],
        in_specs=[pl.BlockSpec(memory_space=pltpu.SMEM)] + [pl.BlockSpec(memory_space=pltpu.VMEM)] * 6,
        scratch_shapes=[
            pltpu.VMEM((RADIX, 2 * LANES, LANES), f32),
            pltpu.VMEM((2, n, LANES), f32),
        ],
        compiler_params=pltpu.CompilerParams(vmem_limit_bytes=40 << 20),
        name="forward_columns_b",
    )(flags, moved, pairs, *tables, *inverse_tables)


def forward_kernel_a(flags, model, edges, pairs, high_i, low_i, out, work):
    first = flags[1] == 1
    lane = lane_of((LANES, LANES))
    turned = lane // 32 == 2

    @pl.loop(0, RADIX)
    def _(k):
        row = pl.multiple_of(k * LANES, LANES)
        real, imag = (
            model[0, part, pl.ds(row, LANES), :] * pairs[0, pl.ds(row, LANES), :]
            + model[1, part, pl.ds(row, LANES), :] * pairs[1, pl.ds(row, LANES), :]
            for part in range(2)
        )
        real, imag = jnp.where(turned, -imag, real), jnp.where(turned, real, imag)
        work[k] = column_product((high_i, low_i), k, jnp.concatenate([real, imag], axis=0))

    lane8 = lane_of((8, LANES))
    packed = jnp.logical_and(lane8 % 32 == 0, first)

    def store(a, row, real, imag):
        edge = edges[pl.ds(a * LANES + row, 8), :]
        edge = jnp.where(lane8 < 64, turn(edge, 63), turn(edge, 126))
        out[pl.ds(a * LANES + row, 8), :LANES] = real
        out[pl.ds(a * LANES + row, 8), LANES:] = jnp.where(packed, edge, imag)

    inverse_blocks(work, store)


def forward_columns_a(flags, model, edges, pairs, inverse_tables):
    n = edges.shape[0]
    return pl.pallas_call(
        forward_kernel_a,
        out_shape=jax.ShapeDtypeStruct((n, 2 * LANES), f32),
        in_specs=[pl.BlockSpec(memory_space=pltpu.SMEM)] + [pl.BlockSpec(memory_space=pltpu.VMEM)] * 5,
        scratch_shapes=[pltpu.VMEM((RADIX, 2 * LANES, LANES), f32)],
        compiler_params=pltpu.CompilerParams(vmem_limit_bytes=32 << 20),
        name="forward_columns_a",
    )(flags, model, edges, pairs, *inverse_tables)


def block_row(block, rows):
    return (block % RADIX) * rows + block // RADIX


def gradient_kernel(counts, listing, spectra, high, low, gradient, outgoing, sums, blocks, compact):
    rows, n = gradient.shape
    parts = quad_transpose([spectra[index] for index in range(4)])
    lhs = jnp.concatenate(
        [jnp.concatenate([parts[0], parts[1]], axis=0), jnp.concatenate([parts[2], parts[3]], axis=0)],
        axis=1,
    )
    inverse_step(lhs, high, low, sums)

    @pl.when(pl.program_id(0) == pl.num_programs(0) - 1)
    def _():
        gradient[:, : n // 2] = sums[0] + sums[1]
        gradient[:, n // 2 :] = sums[0] - sums[1]
        for q in range(RADIX):
            blocks[q * rows : (q + 1) * rows, :] = gradient[:, q * LANES : (q + 1) * LANES]
        owners = outgoing.shape[0]
        cap = outgoing.shape[1]
        total = lax.fori_loop(0, owners, lambda o, t: t + counts[o], jnp.int32(0))

        @pl.loop(0, lax.div(total + 7, 8))
        def _(step):
            for index in range(8):
                at = step * 8 + index
                compact[pl.ds(at, 1), :] = blocks[pl.ds(block_row(listing[at], rows), 1), :]

        offset = 0
        for o in range(owners):
            outgoing[o] = compact[pl.ds(offset, cap), :]
            offset = offset + counts[o]


def gradient_rows(counts, listing, spectra, tables, rows, n, cap):
    devices = spectra.shape[0]
    owners = counts.shape[0]
    smem = pl.BlockSpec(memory_space=pltpu.SMEM)
    table = pl.BlockSpec((1, 2 * LANES, n // 2), lambda s: (s, 0, 0))
    block_count = listing.shape[0]
    return pl.pallas_call(
        gradient_kernel,
        grid=(devices // 4,),
        out_shape=[
            jax.ShapeDtypeStruct((rows, n), f32),
            jax.ShapeDtypeStruct((owners, cap, LANES), f32),
        ],
        in_specs=[
            smem,
            smem,
            pl.BlockSpec((4, rows // 2, LANES), lambda s: (s, 0, 0)),
            table,
            table,
        ],
        out_specs=[
            pl.BlockSpec((rows, n), lambda s: (0, 0)),
            pl.BlockSpec((owners, cap, LANES), lambda s: (0, 0, 0)),
        ],
        scratch_shapes=[
            pltpu.VMEM((2, rows, n // 2), f32),
            pltpu.VMEM((block_count, LANES), f32),
            pltpu.VMEM((block_count + cap, LANES), f32),
        ],
        compiler_params=pltpu.CompilerParams(vmem_limit_bytes=32 << 20),
        name="gradient_rows",
    )(counts, listing, spectra, *tables)


def owner_kernel(counts, incoming, current, weights, model_new, updated, room, scales):
    sources, cap, _ = incoming.shape
    length = current.shape[0]
    room[:length, :] = current[...]
    room[length:, :] = jnp.zeros_like(room[length:, :])
    scales[:length, :] = weights[...].astype(f32) * step_size
    scales[length:, :] = jnp.zeros_like(scales[length:, :])
    row = lax.broadcasted_iota(jnp.int32, (cap, LANES), 0)
    begin = 0
    for p in range(sources):
        count = counts[p]
        before = room[pl.ds(begin, cap), :]
        after = jnp.clip(before - scales[pl.ds(begin, cap), :] * incoming[p], -1.0, 1.0)
        updated[p] = after
        room[pl.ds(begin, cap), :] = jnp.where(row < count, after, before)
        begin = begin + count
    model_new[...] = room[:length, :]


def owner_update(counts, incoming, current, weights):
    sources, cap, _ = incoming.shape
    length = current.shape[0]
    return pl.pallas_call(
        owner_kernel,
        out_shape=[
            jax.ShapeDtypeStruct((length, LANES), f32),
            jax.ShapeDtypeStruct((sources, cap, LANES), f32),
        ],
        in_specs=[pl.BlockSpec(memory_space=pltpu.SMEM)] + [pl.BlockSpec(memory_space=pltpu.VMEM)] * 3,
        scratch_shapes=[pltpu.VMEM((length + cap, LANES), f32)] * 2,
        compiler_params=pltpu.CompilerParams(vmem_limit_bytes=24 << 20),
        name="owner_update",
    )(counts, incoming, current, weights)


def model_rows_kernel(counts, listing, returned, high, low, out, compact, grid, halves_high, halves_low):
    s = pl.program_id(0)
    owners, cap, _ = returned.shape
    rows = halves_high.shape[1]

    @pl.when(s == 0)
    def _():
        grid[...] = jnp.zeros_like(grid)
        offset = 0
        for o in range(owners):
            compact[pl.ds(offset, cap), :] = returned[o]
            offset = offset + counts[o]
        total = offset

        @pl.loop(0, lax.div(total, 8))
        def _(step):
            for index in range(8):
                at = step * 8 + index
                grid[pl.ds(block_row(listing[at], rows), 1), :] = compact[pl.ds(at, 1), :]

        @pl.loop(lax.div(total, 8) * 8, total)
        def _(at):
            grid[pl.ds(block_row(listing[at], rows), 1), :] = compact[pl.ds(at, 1), :]

        half = RADIX // 2
        for q in range(half):
            first = grid[q * rows : (q + 1) * rows, :]
            second = grid[(q + half) * rows : (q + half + 1) * rows, :]
            for index, combined in enumerate((first + second, first - second)):
                top, rest = split(combined)
                halves_high[index, :, q * LANES : (q + 1) * LANES] = top
                halves_low[index, :, q * LANES : (q + 1) * LANES] = rest

    side = s // (pl.num_programs(0) // 2)
    result = dot3((halves_high[side], halves_low[side]), (high[0], low[0]))
    half = rows // 2
    parts = quad_transpose(
        [result[:half, :LANES], result[half:, :LANES], result[:half, LANES:], result[half:, LANES:]]
    )
    for index in range(4):
        out[index] = parts[index]


def model_rows(counts, listing, returned, tables, rows, n, devices):
    owners, cap, _ = returned.shape
    block_count = listing.shape[0]
    smem = pl.BlockSpec(memory_space=pltpu.SMEM)
    table = pl.BlockSpec((1, n // 2, 2 * LANES), lambda s: (s, 0, 0))
    return pl.pallas_call(
        model_rows_kernel,
        grid=(devices // 4,),
        out_shape=jax.ShapeDtypeStruct((devices, rows // 2, LANES), f32),
        in_specs=[
            smem,
            smem,
            pl.BlockSpec((owners, cap, LANES), lambda s: (0, 0, 0)),
            table,
            table,
        ],
        out_specs=pl.BlockSpec((4, rows // 2, LANES), lambda s: (s, 0, 0)),
        scratch_shapes=[
            pltpu.VMEM((block_count + cap, LANES), f32),
            pltpu.VMEM((block_count, LANES), f32),
            pltpu.VMEM((2, rows, n // 2), bf16),
            pltpu.VMEM((2, rows, n // 2), bf16),
        ],
        compiler_params=pltpu.CompilerParams(vmem_limit_bytes=32 << 20),
        name="model_rows",
    )(counts, listing, returned, *tables)


def swap_all(value, axes):
    return lax.all_to_all(value, axes, split_axis=0, concat_axis=0, tiled=True)


def local_paired(misfit, kernel_spec, model_vec, weight_vec, active_list, send_counts):
    both = ("pen", "dep")
    pen_count = lax.axis_size("pen")
    devices = pen_count * lax.axis_size("dep")
    channels, rows, n = misfit.shape
    band = n // pen_count
    forward_np, inverse_np = row_tables(n, devices)
    row_forward, row_inverse = tuple(map(jnp.asarray, forward_np)), tuple(map(jnp.asarray, inverse_np))
    forward_np, inverse_np = column_tables()
    col_forward, col_inverse = tuple(map(jnp.asarray, forward_np)), tuple(map(jnp.asarray, inverse_np))
    me = lax.axis_index(both)
    half = devices // 2
    flags = jnp.stack([(me >= half).astype(jnp.int32), (me == 0).astype(jnp.int32)])
    counts = send_counts.reshape(pen_count)
    listing = active_list.reshape(-1)
    owner_length = model_vec.shape[2]
    cap = owner_length // pen_count

    spec = kernel_spec.reshape((-1,) + kernel_spec.shape[2:])
    sent, kept = part_spec(flags, spec)
    got = lax.ppermute(sent, both, [(d, devices - 1 - d) for d in range(devices)])
    edge = lax.ppermute(
        spec[:, 0:1, :].astype(f32), both, [(d, (devices - d) % half) for d in range(half, devices)]
    )
    source_counts = swap_all(counts, "pen")

    chunk_a, chunk_b = misfit_rows(misfit, row_forward, devices)
    columns_a = swap_all(chunk_a, both).reshape(n, 2 * LANES)
    columns_b = swap_all(chunk_b, both).reshape(n, LANES)
    pairs_a, pairs_b = pair_spec(flags, kept, got, edge)
    sums, edges = adjoint_columns_a(flags, columns_a, pairs_a, col_forward)
    fields = adjoint_columns_b(flags, columns_b, edges, sums, pairs_b, col_forward, col_inverse)
    gradient, outgoing = gradient_rows(
        counts, listing, swap_all(fields, both), row_inverse, band, n, cap
    )
    incoming = swap_all(outgoing, "pen")
    model_new, updated = owner_update(
        source_counts,
        incoming,
        model_vec.reshape(owner_length, LANES),
        weight_vec.reshape(owner_length, LANES),
    )
    returned = swap_all(updated, "pen")
    model_chunks = model_rows(counts, listing, returned, row_forward, band, n, devices)
    out_b, edges, model = forward_columns_b(
        flags, swap_all(model_chunks, both), pairs_b, col_forward, col_inverse, n
    )
    back_b = swap_all(out_b.reshape(devices, rows, LANES), both)
    out_a = forward_columns_a(flags, model, edges, pairs_a, col_inverse)
    back_a = swap_all(out_a.reshape(devices, rows, 2 * LANES), both)
    predicted = predicted_rows(back_b, row_inverse, None, n)
    predicted = predicted_rows(back_a, row_inverse, predicted, n)
    return (gradient[None], model_new.reshape(model_vec.shape), predicted)


def local(misfit, kernel_spec, model_vec, weight_vec, active_list, send_counts):
    sizes = tuple(lax.axis_size(name) for name in ("pen", "dep", "chan"))
    if sizes == (16, 2, 1) and misfit.shape == (6, 64, RADIX * LANES) and kernel_spec.shape[1] == 2:
        plan = local_paired
    else:
        plan = local_general
    return plan(misfit, kernel_spec, model_vec, weight_vec, active_list, send_counts)


def solution(mesh):
    return jax.shard_map(
        local,
        mesh=mesh,
        in_specs=(
            P(("grp", "chan"), ("pen", "dep"), None),
            P("chan", None, ("pen", "dep"), None),
            P(("grp", "dep", "chan"), "pen", None, None),
            P(("grp", "dep", "chan"), "pen", None, None),
            P(("grp", "dep", "chan"), "pen", None),
            P(("grp", "dep", "chan"), "pen", None),
        ),
        out_specs=(
            P(("grp", "dep", "chan"), "pen", None),
            P(("grp", "dep", "chan"), "pen", None, None),
            P(("grp", "chan"), ("pen", "dep"), None),
        ),
        check_vma=False,
    )
```

```python
import functools
import math

import jax
import jax.numpy as jnp
import ml_dtypes
import numpy as np
from jax import lax
from jax.experimental import pallas as pl
from jax.experimental.pallas import tpu as pltpu
from jax.sharding import PartitionSpec as P

inner_radix = 128
step_size = 0.5
highest = lax.Precision.HIGHEST
letters_free = "cdefghij"


def unit_table(length, direction):
    indices = jnp.arange(length, dtype=jnp.int32)
    phases = indices[:, None] * indices[None, :] % length
    angles = 2.0 * math.pi / length * phases.astype(jnp.float32)
    return (jnp.cos(angles), direction * jnp.sin(angles))


def twiddle_table(outer_size, inner_size, direction):
    length = outer_size * inner_size
    phases = (
        jnp.arange(outer_size, dtype=jnp.int32)[:, None]
        * jnp.arange(inner_size, dtype=jnp.int32)[None, :]
        % length
    )
    angles = 2.0 * math.pi / length * phases.astype(jnp.float32)
    return (jnp.cos(angles), direction * jnp.sin(angles))


def contract(formula, operand, tables, real_only):
    product_one = jnp.einsum(formula, operand[0], tables[0], precision=highest)
    if operand[1] is None:
        return (product_one, jnp.einsum(formula, operand[0], tables[1], precision=highest))
    real_value = product_one - jnp.einsum(formula, operand[1], tables[1], precision=highest)
    if real_only:
        return (real_value, None)
    imag_value = jnp.einsum(formula, operand[0], tables[1], precision=highest) + jnp.einsum(
        formula, operand[1], tables[0], precision=highest
    )
    return (real_value, imag_value)


def transform(operand, dimension, direction, real_only):
    full_shape = operand[0].shape
    length = full_shape[dimension]
    inner_size = min(inner_radix, length)
    outer_size = length // inner_size
    split_shape = full_shape[:dimension] + (outer_size, inner_size) + full_shape[dimension + 1 :]
    leading = letters_free[:dimension]
    trailing = letters_free[dimension : len(full_shape) - 1]
    pieces = tuple((None if member is None else member.reshape(split_shape) for member in operand))
    sectioned = contract(
        leading + "ab" + trailing + ",ak->" + leading + "kb" + trailing,
        pieces,
        unit_table(outer_size, direction),
        False,
    )
    twist_real, twist_imag = twiddle_table(outer_size, inner_size, direction)
    twist_shape = (outer_size, inner_size) + (1,) * len(trailing)
    twist_real = twist_real.reshape(twist_shape)
    twist_imag = twist_imag.reshape(twist_shape)
    rotated = (
        sectioned[0] * twist_real - sectioned[1] * twist_imag,
        sectioned[0] * twist_imag + sectioned[1] * twist_real,
    )
    factor = 1.0 / length if direction > 0 else 1.0
    if len(trailing) == 0:
        result = contract(
            leading + "kb,bm->" + leading + "km",
            rotated,
            unit_table(inner_size, direction),
            real_only,
        )
        return tuple(
            (
                (
                    None
                    if member is None
                    else jnp.swapaxes(member, -1, -2).reshape(full_shape) * factor
                )
                for member in result
            )
        )
    result = contract(
        leading + "kb" + trailing + ",bm->" + leading + "mk" + trailing,
        rotated,
        unit_table(inner_size, direction),
        real_only,
    )
    return tuple(
        (None if member is None else member.reshape(full_shape) * factor for member in result)
    )


def exclusive_sum(counts):
    places = jnp.arange(counts.shape[0], dtype=jnp.int32)
    return jnp.sum(jnp.where(places[None, :] < places[:, None], counts[None, :], 0), axis=1)


def imag_channels(chan_place, chan_width):
    channel_ids = chan_place * chan_width + jnp.arange(chan_width, dtype=jnp.int32)
    return ((channel_ids == 2) | (channel_ids == 4))[:, None, None]


def channel_weighted(kernel_view, along):
    total = None
    for channel in range(kernel_view.shape[0]):
        kernel_now = kernel_view[channel].astype(jnp.float32)
        term = kernel_now * along[channel][None, None]
        total = term if total is None else total + term
    return total.reshape(-1, along.shape[1], along.shape[2])


def layer_weighted(kernel_view, grouped):
    ordered = jnp.swapaxes(grouped, 0, 1)
    outputs = []
    for channel in range(kernel_view.shape[0]):
        products = kernel_view[channel].astype(jnp.float32) * ordered
        outputs.append(jnp.sum(products, axis=(0, 1)))
    return jnp.stack(outputs)


def local_general(misfit, kernel_spec, model_vec, weight_vec, active_list, send_counts):
    pen_count = lax.axis_size("pen")
    dep_count = lax.axis_size("dep")
    chan_count = lax.axis_size("chan")
    chan_width, band_width, grid_width = misfit.shape
    column_width = kernel_spec.shape[2]
    kernel_view = kernel_spec.reshape(chan_width, dep_count, chan_count, column_width, grid_width)
    turned = imag_channels(lax.axis_index("chan"), chan_width)
    spectra_real, spectra_imag = transform((misfit, None), 2, -1.0, False)
    columns = (
        lax.all_to_all(spectra_real, ("pen", "dep"), split_axis=2, concat_axis=1, tiled=True),
        lax.all_to_all(spectra_imag, ("pen", "dep"), split_axis=2, concat_axis=1, tiled=True),
    )
    columns = (jnp.swapaxes(columns[0], 1, 2), jnp.swapaxes(columns[1], 1, 2))
    misfit_hat = transform(columns, 2, -1.0, False)
    along_real = jnp.where(turned, misfit_hat[1], misfit_hat[0])
    along_imag = jnp.where(turned, -misfit_hat[0], misfit_hat[1])
    partial_real = channel_weighted(kernel_view, along_real)
    partial_imag = channel_weighted(kernel_view, along_imag)
    fields = transform((partial_real, partial_imag), 2, 1.0, False)
    outgoing = tuple(
        (
            member.reshape(dep_count, chan_count, column_width, pen_count, -1)
            .transpose(3, 0, 1, 4, 2)
            .reshape(pen_count * dep_count, chan_count, -1, column_width)
            for member in fields
        )
    )
    arrived = (
        lax.all_to_all(outgoing[0], ("pen", "dep"), split_axis=0, concat_axis=3, tiled=True),
        lax.all_to_all(outgoing[1], ("pen", "dep"), split_axis=0, concat_axis=3, tiled=True),
    )
    real_fields = transform(arrived, 3, 1.0, True)[0]
    gradient = lax.psum_scatter(real_fields, "chan", scatter_dimension=1, tiled=True).reshape(
        1, -1, grid_width
    )
    blocks = gradient.reshape(-1, 128)
    block_count = blocks.shape[0]
    owner_length = model_vec.shape[2]
    slot_cap = owner_length // pen_count
    counts = send_counts.reshape(pen_count)
    starts = exclusive_sum(counts)
    slot_index = jnp.arange(slot_cap, dtype=jnp.int32)
    slot_valid = slot_index[None, :] < counts[:, None]
    in_list = jnp.minimum(starts[:, None] + slot_index[None, :], block_count - 1)
    listing = active_list.reshape(block_count)
    block_ids = listing[in_list]
    outgoing_blocks = jnp.where(slot_valid[:, :, None], blocks[block_ids], 0.0)
    incoming, arrived_counts = (
        lax.all_to_all(outgoing_blocks, "pen", split_axis=0, concat_axis=0, tiled=True),
        lax.all_to_all(counts.astype(jnp.float32), "pen", split_axis=0, concat_axis=0, tiled=True),
    )
    source_counts = arrived_counts.astype(jnp.int32)
    begins = exclusive_sum(source_counts)
    filled = slot_index[None, :] < source_counts[:, None]
    places = begins[:, None] + slot_index[None, :]
    safe_places = jnp.minimum(places, owner_length - 1)
    current = model_vec.reshape(owner_length, 128)
    scales = weight_vec.reshape(owner_length, 128)
    updated = jnp.clip(
        current[safe_places] - step_size * scales[safe_places].astype(jnp.float32) * incoming,
        -1.0,
        1.0,
    )
    targets = jnp.where(filled, places, owner_length)
    model_new = current.at[targets].set(updated, mode="drop").reshape(model_vec.shape)
    returned = lax.all_to_all(updated, "pen", split_axis=0, concat_axis=0, tiled=True)
    drop_ids = jnp.where(slot_valid, block_ids, block_count)
    model_grid = jnp.zeros((block_count, 128), jnp.float32).at[drop_ids].set(returned, mode="drop")
    model_grid = model_grid.reshape(-1, grid_width)
    surface_field = transform((model_grid, None), 1, -1.0, False)
    moved_columns = (
        lax.all_to_all(surface_field[0], ("pen", "dep"), split_axis=1, concat_axis=0, tiled=True),
        lax.all_to_all(surface_field[1], ("pen", "dep"), split_axis=1, concat_axis=0, tiled=True),
    )
    ordered = tuple(
        (
            member.reshape(pen_count, dep_count, -1, column_width)
            .transpose(1, 3, 0, 2)
            .reshape(dep_count, column_width, grid_width)
            for member in moved_columns
        )
    )
    model_hat = transform(ordered, 2, -1.0, False)
    layers_all = (
        lax.all_gather(model_hat[0], "chan", axis=0, tiled=True),
        lax.all_gather(model_hat[1], "chan", axis=0, tiled=True),
    )
    grouped = tuple(
        (member.reshape(chan_count, dep_count, column_width, grid_width) for member in layers_all)
    )
    summed_real = layer_weighted(kernel_view, grouped[0])
    summed_imag = layer_weighted(kernel_view, grouped[1])
    data_real = jnp.where(turned, -summed_imag, summed_real)
    data_imag = jnp.where(turned, summed_real, summed_imag)
    surface_rows = transform((data_real, data_imag), 2, 1.0, False)
    rows_back = (
        lax.all_to_all(surface_rows[0], ("pen", "dep"), split_axis=2, concat_axis=1, tiled=True),
        lax.all_to_all(surface_rows[1], ("pen", "dep"), split_axis=2, concat_axis=1, tiled=True),
    )
    predicted = jnp.swapaxes(transform(rows_back, 1, 1.0, True)[0], 1, 2)
    return (gradient, model_new, predicted)


RADIX = 16
LANES = 128
TILES = (((0, 0), (1, 32), (2, 64), (3, 96)), ((4, 0), (5, 64)))
EDGES = ((4, 32), (0, 33), (1, 34), (5, 96), (2, 97), (3, 98))
f32 = jnp.float32
bf16 = jnp.bfloat16


def two_terms(table):
    high = table.astype(ml_dtypes.bfloat16)
    low = (table - high.astype(np.float64)).astype(ml_dtypes.bfloat16)
    return (high, low)


def row_frequencies(n, devices, width):
    device = np.arange(devices)[:, None]
    column = np.arange(width // 2)[None, :]
    return width * device + 2 * column + (device >= devices // 2)


@functools.cache
def row_tables(n, devices):
    width = n // devices
    freq = row_frequencies(n, devices, width).reshape(devices // 4, 1, LANES)
    y = np.arange(n // 2)[None, :, None]
    angle = 2.0 * math.pi / n * (freq * y % n)
    real, imag = np.cos(angle), -np.sin(angle)
    imag[0, :, 0] = 1.0 - 2.0 * (np.arange(n // 2) % 2)
    forward = np.concatenate([real, imag], axis=2)
    inverse = 2.0 * forward
    inverse[0, :, 0] *= 0.5
    inverse[0, :, LANES] *= 0.5
    inverse = inverse.swapaxes(1, 2) / float(n) ** 2
    return (two_terms(forward), two_terms(inverse))


@functools.cache
def column_tables():
    k = np.arange(RADIX)[:, None, None]
    m = np.arange(LANES)[None, :, None]
    b = np.arange(LANES)[None, None, :]
    n = RADIX * LANES
    angle = 2.0 * math.pi / n * ((16 * b * m + b * k) % n)
    real, sine = np.cos(angle), np.sin(angle)
    forward = np.concatenate(
        [np.concatenate([real, sine], axis=2), np.concatenate([-sine, real], axis=2)], axis=1
    )
    return (two_terms(forward), two_terms(forward.swapaxes(1, 2)))


@functools.cache
def lane_tables():
    edges = [lane for _, lane in EDGES]
    fold = np.zeros((2, LANES, LANES))
    spread = np.zeros((LANES, 2, LANES))
    for layer in range(2):
        for _, lane in TILES[1]:
            for i in range(32):
                fold[layer, lane + i, 64 * layer + i] = 1.0
                spread[64 * layer + i, layer, lane + i] = 1.0
        fold[layer, edges, 64 * layer + 32] = 1.0
        spread[64 * layer + 32, layer, edges] = 1.0
    fold = np.concatenate([fold[0], fold[0], fold[1], fold[1]])
    spread = np.tile(spread.reshape(LANES, 2 * LANES), (2, 1))
    return (fold.astype(ml_dtypes.bfloat16), spread.astype(ml_dtypes.bfloat16))


def split(value):
    high = value.astype(bf16)
    return high, (value - high.astype(f32)).astype(bf16)


def dot(a, b):
    return jnp.dot(a, b, preferred_element_type=f32)


def dot3(left, right):
    return dot(left[0], right[0]) + (dot(left[0], right[1]) + dot(left[1], right[0]))


def turn(value, shift):
    shift %= LANES
    return value if shift == 0 else pltpu.roll(value, shift, value.ndim - 1)


def lane_of(shape):
    return lax.broadcasted_iota(jnp.int32, shape, len(shape) - 1)


def quad_transpose(parts):
    lane = lane_of(parts[0].shape)
    low, even = lane < 64, lane % 64 < 32
    a, b, c, d = parts
    a, c = jnp.where(low, a, turn(c, 64)), jnp.where(low, turn(a, 64), c)
    b, d = jnp.where(low, b, turn(d, 64)), jnp.where(low, turn(b, 64), d)
    a, b = jnp.where(even, a, turn(b, 32)), jnp.where(even, turn(a, 96), b)
    c, d = jnp.where(even, c, turn(d, 32)), jnp.where(even, turn(c, 96), d)
    return [a, b, c, d]


def radix4(x, sign):
    (r0, i0), (r1, i1), (r2, i2), (r3, i3) = x
    ar, ai, br, bi = r0 + r2, i0 + i2, r0 - r2, i0 - i2
    cr, ci, dr, di = r1 + r3, i1 + i3, r1 - r3, i1 - i3
    if sign < 0:
        turned = (di, -dr)
    else:
        turned = (-di, dr)
    return [
        (ar + cr, ai + ci),
        (br + turned[0], bi + turned[1]),
        (ar - cr, ai - ci),
        (br - turned[0], bi - turned[1]),
    ]


def radix16(x, sign):
    inner = [radix4([x[4 * a1 + a0] for a1 in range(4)], sign) for a0 in range(4)]
    outputs = [None] * RADIX
    for k0 in range(4):
        column = []
        for a0 in range(4):
            re, im = inner[a0][k0]
            power = a0 * k0 % RADIX
            if power == 4:
                re, im = (im, -re) if sign < 0 else (-im, re)
            elif power == 2 or power == 6:
                scale = math.sqrt(0.5)
                c = scale if power == 2 else -scale
                if sign < 0:
                    re, im = re * c + im * scale, im * c - re * scale
                else:
                    re, im = re * c - im * scale, im * c + re * scale
            elif power != 0:
                c = math.cos(2.0 * math.pi * power / RADIX)
                s = sign * math.sin(2.0 * math.pi * power / RADIX)
                re, im = re * c - im * s, re * s + im * c
            column.append((re, im))
        for k1, value in enumerate(radix4(column, sign)):
            outputs[4 * k1 + k0] = value
    return outputs


def forward_blocks(load, work):
    @pl.loop(0, LANES // 8)
    def _(step):
        first = pl.multiple_of(step * 8, 8)
        outputs = radix16([load(a, first) for a in range(RADIX)], -1)
        for k, (re, im) in enumerate(outputs):
            work[k, pl.ds(first, 8), :] = re
            work[k, pl.ds(first + LANES, 8), :] = im


def inverse_blocks(work, store):
    @pl.loop(0, LANES // 8)
    def _(step):
        first = pl.multiple_of(step * 8, 8)
        inputs = [
            (work[k, pl.ds(first, 8), :], work[k, pl.ds(first + LANES, 8), :]) for k in range(RADIX)
        ]
        for a, (re, im) in enumerate(radix16(inputs, 1)):
            store(a, first, re, im)


def column_product(tables, value):
    high, low = split(value)
    wide = dot(tables[0], jnp.concatenate([high, low], axis=1))
    return wide[:, :LANES] + wide[:, LANES:] + dot(tables[1], high)


def choose_rows(wanted, value):
    columns = lax.broadcasted_iota(jnp.int32, (wanted.shape[0], value.shape[0]), 1)
    return dot((columns == wanted).astype(f32).astype(bf16), value)


def part_kernel(flags, spec, sent):
    half = sent.shape[1]
    wanted = 2 * (half - 1 - lax.broadcasted_iota(jnp.int32, (half, 2 * half), 0)) + 1 - flags[0]
    for line in range(sent.shape[0]):
        sent[line] = choose_rows(wanted, spec[line])


def part_spec(flags, spec, begin, end):
    count, width, n = spec.shape
    half = width // 2
    step = 2
    return pl.pallas_call(
        part_kernel,
        grid=((end - begin) // step,),
        out_shape=pltpu.HBM((end - begin, half, n), f32),
        in_specs=[
            pl.BlockSpec(memory_space=pltpu.SMEM),
            pl.BlockSpec((step, width, n), lambda s: (s + begin // step, 0, 0)),
        ],
        out_specs=pl.BlockSpec((step, half, n), lambda s: (s, 0, 0)),
        name="part_spec",
    )(flags, in_hbm(spec))


def pair_kernel(flags, spec, got_a, got_b, edge, pairs, own, mirror, room, own_t, mirror_t):
    step = pl.program_id(0)
    layer = lax.rem(step, 2)
    upper, first = flags[0], flags[1]
    half = got_a.shape[1]
    n = spec.shape[2]
    wanted = 2 * lax.broadcasted_iota(jnp.int32, (half, 2 * half), 0) + upper

    def weight(channel):
        return -0.5 if channel in (2, 4) else 0.5

    for tile in range(2):

        @pl.when(lax.div(step, 2) == tile)
        def _():
            if tile == 1:
                own[...] = jnp.zeros_like(own)
                mirror[...] = jnp.zeros_like(mirror)
                for channel, lane in EDGES:
                    row = edge[2 * channel + layer]
                    own[lane : lane + 1, :] = row * 0.5
                    mirror[lane : lane + 1, :] = row * weight(channel)
            for channel, lane in TILES[tile]:
                line = 2 * channel + layer
                kept = choose_rows(wanted, spec[line])
                own[lane : lane + half, :] = kept * 0.5
                room[0:1, :] = jnp.where(first == 1, kept[0:1, :], edge[line])
                room[1 : 1 + half, :] = got_a[line] if tile == 0 else got_b[line - 8]
                mirror[lane : lane + half, :] = (
                    jnp.where(upper == 1, room[1 : 1 + half, :], room[0:half, :]) * weight(channel)
                )

    for block in range(n // LANES):
        here = slice(block * LANES, (block + 1) * LANES)
        own_t[here, :] = jnp.transpose(own[:, here])
        mirror_t[here, :] = jnp.transpose(mirror[:, here])
    row = lax.broadcasted_iota(jnp.int32, (LANES, LANES), 0)
    for k in range(RADIX):
        wanted_k = LANES - 1 - row if k > 0 else (LANES - row) & (LANES - 1)
        other = mirror_t[pl.ds((RADIX - k) % RADIX, LANES, stride=RADIX), :]
        pairs[0, k * LANES : (k + 1) * LANES, :] = own_t[
            pl.ds(k, LANES, stride=RADIX), :
        ] + choose_rows(wanted_k, other.astype(bf16))


def pair_spec(flags, spec, got_a, got_b, edge):
    count, width, n = spec.shape
    single = pl.Buffered(1)
    return pl.pallas_call(
        pair_kernel,
        grid=(4,),
        out_shape=pltpu.HBM((4, n, LANES), f32),
        in_specs=[
            pl.BlockSpec(memory_space=pltpu.SMEM),
            pl.BlockSpec((count, width, n), lambda s: (0, 0, 0), pipeline_mode=single),
            pl.BlockSpec(got_a.shape, lambda s: (0, 0, 0), pipeline_mode=single),
            pl.BlockSpec(got_b.shape, lambda s: (0, 0, 0), pipeline_mode=single),
            pl.BlockSpec((count, 1, n), lambda s: (0, 0, 0)),
        ],
        out_specs=pl.BlockSpec((1, n, LANES), lambda s: (s, 0, 0)),
        scratch_shapes=[
            pltpu.VMEM((LANES, n), f32),
            pltpu.VMEM((LANES, n), f32),
            pltpu.VMEM((40, n), f32),
            pltpu.VMEM((n, LANES), f32),
            pltpu.VMEM((n, LANES), f32),
        ],
        compiler_params=pltpu.CompilerParams(vmem_limit_bytes=24 << 20),
        cost_estimate=pl.CostEstimate(flops=0, bytes_accessed=60_000_000, transcendentals=0),
        name="pair_spec",
    )(flags, in_hbm(spec), in_hbm(got_a), in_hbm(got_b), edge)


def misfit_rows_kernel(misfit, high, low, out_a, out_b, halves_high, halves_low):
    s = pl.program_id(0)
    channels, rows, n = misfit.shape

    @pl.when(s == 0)
    def _():
        value = misfit[...].reshape(channels * rows, n)
        first, second = value[:, : n // 2], value[:, n // 2 :]
        for index, combined in enumerate((first + second, first - second)):
            halves_high[index], halves_low[index] = split(combined)

    side = s // (pl.num_programs(0) // 2)
    result = dot3((halves_high[side], halves_low[side]), (high[0], low[0]))
    real = [result[rows * c : rows * (c + 1), :LANES] for c in range(channels)]
    imag = [result[rows * c : rows * (c + 1), LANES:] for c in range(channels)]
    parts = (quad_transpose(real[:4]), quad_transpose(imag[:4]))
    for index in range(4):
        out_a[index, :, :LANES] = parts[0][index]
        out_a[index, :, LANES:] = parts[1][index]
    for index, value in enumerate(quad_transpose([real[4], imag[4], real[5], imag[5]])):
        out_b[index] = value


def misfit_rows(misfit, tables, devices):
    channels, rows, n = misfit.shape
    table = pl.BlockSpec((1, n // 2, 2 * LANES), lambda s: (s, 0, 0))
    return pl.pallas_call(
        misfit_rows_kernel,
        grid=(devices // 4,),
        out_shape=[
            jax.ShapeDtypeStruct((devices, rows, 2 * LANES), f32),
            jax.ShapeDtypeStruct((devices, rows, LANES), f32),
        ],
        in_specs=[pl.BlockSpec((channels, rows, n), lambda s: (0, 0, 0)), table, table],
        out_specs=[
            pl.BlockSpec((4, rows, 2 * LANES), lambda s: (s, 0, 0)),
            pl.BlockSpec((4, rows, LANES), lambda s: (s, 0, 0)),
        ],
        scratch_shapes=[pltpu.VMEM((2, channels * rows, n // 2), bf16)] * 2,
        compiler_params=pltpu.CompilerParams(vmem_limit_bytes=22 << 20),
        name="misfit_rows",
    )(misfit, *tables)


AHEAD = 3


def inverse_step(lhs, table, sums, held, arrived):
    s = pl.program_id(0)
    steps = pl.num_programs(0)

    def fetch(step):
        return pltpu.make_async_copy(table.at[step], held.at[step], arrived.at[step])

    @pl.when(s == 0)
    def _():
        for step in range(AHEAD):
            fetch(step).start()

    fetch(s).wait()

    @pl.when(s + AHEAD < steps)
    def _():
        fetch(s + AHEAD).start()

    product = dot3(split(lhs), (held[s, 0], held[s, 1]))
    side = s // (steps // 2)
    fresh = s % (steps // 2) == 0

    @pl.when(fresh)
    def _():
        sums[side] = product

    @pl.when(jnp.logical_not(fresh))
    def _():
        sums[side] += product


def inverse_scratch(rows, n, steps):
    return [
        pltpu.VMEM((2, rows, n // 2), f32),
        pltpu.VMEM((steps, 2, 2 * LANES, n // 2), bf16),
        pltpu.SemaphoreType.DMA((steps,)),
    ]


def finish_channels(out, sums, channels):
    rows, n = out.shape[1:]

    @pl.when(pl.program_id(0) == pl.num_programs(0) - 1)
    def _():
        for channel in range(channels):
            here = slice(channel * rows, (channel + 1) * rows)
            out[channel, :, : n // 2] = sums[0, here] + sums[1, here]
            out[channel, :, n // 2 :] = sums[0, here] - sums[1, here]


def predicted_kernel_b(spectra, table, out, sums, held, arrived):
    c4r, c4i, c5r, c5i = quad_transpose([spectra[index] for index in range(4)])
    lhs = jnp.concatenate(
        [jnp.concatenate([c4r, c4i], axis=1), jnp.concatenate([c5r, c5i], axis=1)], axis=0
    )
    inverse_step(lhs, table, sums, held, arrived)
    finish_channels(out, sums, 2)


def predicted_kernel_a(spectra, table, before, out, sums, held, arrived):
    real = quad_transpose([spectra[index, :, :LANES] for index in range(4)])
    imag = quad_transpose([spectra[index, :, LANES:] for index in range(4)])
    lhs = jnp.concatenate([jnp.concatenate(pair, axis=1) for pair in zip(real, imag)], axis=0)
    inverse_step(lhs, table, sums, held, arrived)
    finish_channels(out, sums, 4)


def predicted_rows(spectra, table, before, n):
    devices, rows, lanes = spectra.shape
    hbm = pl.BlockSpec(memory_space=pltpu.HBM)
    channels = 2 if before is None else 4
    return pl.pallas_call(
        predicted_kernel_b if before is None else predicted_kernel_a,
        grid=(devices // 4,),
        out_shape=jax.ShapeDtypeStruct((6, rows, n), f32),
        in_specs=[pl.BlockSpec((4, rows, lanes), lambda s: (s, 0, 0)), hbm] + ([] if before is None else [hbm]),
        out_specs=pl.BlockSpec((channels, rows, n), lambda s: (2 if before is None else 0, 0, 0)),
        scratch_shapes=inverse_scratch(channels * rows, n, devices // 4),
        input_output_aliases={} if before is None else {2: 0},
        compiler_params=pltpu.CompilerParams(vmem_limit_bytes=26 << 20),
        name="predicted_rows_b" if before is None else "predicted_rows_a",
    )(spectra, in_hbm(table), *([] if before is None else [before]))


GROUPS = 4


def started(*copies):
    made = [pltpu.make_async_copy(*copy) for copy in copies]
    for copy in made:
        copy.start()
    return made


def group_rows(group):
    size = RADIX // GROUPS * LANES
    return pl.ds(group * size, size)


def group_steps(group):
    return pl.ds(group * (RADIX // GROUPS), RADIX // GROUPS)


def in_group(group):
    return range(group * (RADIX // GROUPS), (group + 1) * (RADIX // GROUPS))


def pair_copies(pairs, tile, held, arrived, group):
    here = group_rows(group)
    return (pairs.at[pl.ds(2 * tile, 2), here], held.at[:, here], arrived.at[group])


def table_copies(table, held, arrived, group):
    here = group_steps(group)
    return (table.at[here], held.at[here], arrived.at[group])


def table_product(table, k, value):
    return column_product((table[k, 0], table[k, 1]), value)


TABLE = pltpu.VMEM((RADIX, 2, 2 * LANES, 2 * LANES), bf16)
WORK = pltpu.VMEM((RADIX, 2 * LANES, LANES), f32)
SIGNALS = pltpu.SemaphoreType.DMA((GROUPS,))


def pairs_like(n):
    return pltpu.VMEM((2, n, LANES), f32)


def turn_phase(channel_lanes, real, imag, sign):
    if sign < 0:
        return jnp.where(channel_lanes, imag, real), jnp.where(channel_lanes, -real, imag)
    return jnp.where(channel_lanes, -imag, real), jnp.where(channel_lanes, real, imag)


def adjoint_kernel_a(
    flags, spectra, pairs, table, sums, edges, work, here, held_pairs, held_table, got, got_pairs, got_table
):
    first = flags[1] == 1
    read = started((spectra, here, got.at[0]))
    later = [
        started(pair_copies(pairs, 0, held_pairs, got_pairs, g), table_copies(table, held_table, got_table, g))
        for g in range(GROUPS)
    ]
    lane8 = lane_of((8, LANES))
    packed = jnp.logical_and(lane8 % 32 == 0, first)
    read[0].wait()

    def load(a, row):
        real = here[pl.ds(a * LANES + row, 8), :LANES]
        imag = here[pl.ds(a * LANES + row, 8), LANES:]
        edges[pl.ds(a * LANES + row, 8), :] = jnp.where(lane8 % 64 == 33, turn(imag, 33), turn(imag, 2))
        return (real, jnp.where(packed, 0.0, imag))

    forward_blocks(load, work)
    lane = lane_of((LANES, LANES))
    turned = lane // 32 == 2
    for group in range(GROUPS):
        for copy in later[group]:
            copy.wait()
        for k in in_group(group):
            spectrum = table_product(held_table, k, work[k])
            real, imag = turn_phase(turned, spectrum[:LANES], spectrum[LANES:], -1)
            row = slice(k * LANES, (k + 1) * LANES)
            for index, value in enumerate((real, imag)):
                v0, v1 = value * held_pairs[0, row, :], value * held_pairs[1, row, :]
                both = jnp.where(lane < 64, v0, turn(v1, 64)) + jnp.where(lane < 64, turn(v0, 64), v1)
                sums[index, row, :] = both + turn(both, 96)


def adjoint_columns_a(flags, spectra, pairs, table):
    n = spectra.shape[0]
    hbm = pl.BlockSpec(memory_space=pltpu.HBM)
    return pl.pallas_call(
        adjoint_kernel_a,
        out_shape=[
            jax.ShapeDtypeStruct((2, n, LANES), f32),
            jax.ShapeDtypeStruct((n, LANES), f32),
        ],
        in_specs=[pl.BlockSpec(memory_space=pltpu.SMEM), hbm, hbm, hbm],
        scratch_shapes=[
            WORK,
            pltpu.VMEM((n, 2 * LANES), f32),
            pairs_like(n),
            TABLE,
            pltpu.SemaphoreType.DMA((1,)),
            SIGNALS,
            SIGNALS,
        ],
        compiler_params=pltpu.CompilerParams(vmem_limit_bytes=24 << 20),
        cost_estimate=pl.CostEstimate(flops=0, bytes_accessed=20_000_000, transcendentals=0),
        name="adjoint_columns_a",
    )(flags, in_hbm(spectra), in_hbm(pairs), in_hbm(table))


def adjoint_kernel_b(
    flags, spectra, edges, sums, fold, pairs, table, table_i, out,
    work, here, held_pairs, held_table, held_table_i, fields, chunks, got, got_pairs, got_table, got_table_i, left,
):
    first = flags[1] == 1
    read = started((spectra, here, got.at[0]))
    later = [
        started(
            table_copies(table, held_table, got_table, g),
            pair_copies(pairs, 1, held_pairs, got_pairs, g),
        )
        for g in range(GROUPS)
    ]
    last = [started(table_copies(table_i, held_table_i, got_table_i, g))[0] for g in range(GROUPS)]
    lane8 = lane_of((8, LANES))
    main = lane8 % 64 < 32
    packed = jnp.logical_and(lane8 % 64 == 0, first)
    in_place = lane8 % 64 == 32
    packed_edge = jnp.logical_and(in_place, first)
    moved = (lane8 % 64 == 33) | (lane8 % 64 == 34)
    read[0].wait()

    def load(a, row):
        value = here[pl.ds(a * LANES + row, 8), :]
        edge = edges[pl.ds(a * LANES + row, 8), :]
        real = jnp.where(main | in_place, value, jnp.where(moved, edge, 0.0))
        imag = jnp.where(jnp.logical_and(main, jnp.logical_not(packed)), turn(value, 96), 0.0)
        return (real, imag)

    forward_blocks(load, work)
    lane = lane_of((LANES, LANES))
    turned = (lane <= 32) | (lane == 97)
    on_main = lane % 64 < 32
    for group in range(GROUPS):
        for copy in later[group][:2]:
            copy.wait()
        for k in in_group(group):
            spectrum = table_product(held_table, k, work[k])
            row = slice(k * LANES, (k + 1) * LANES)
            parts = []
            for value in turn_phase(turned, spectrum[:LANES], spectrum[LANES:], -1):
                terms = split(value * held_pairs[0, row, :]) + split(value * held_pairs[1, row, :])
                parts.append(jnp.concatenate(terms, axis=1))
            folded = dot(jnp.concatenate(parts, axis=0), fold[...])
            for index in range(2):
                half = slice(index * LANES, (index + 1) * LANES)
                work[k, half] = folded[half] + jnp.where(on_main, sums[index, row, :], 0.0)
    for group in range(GROUPS):
        last[group].wait()
        for k in in_group(group):
            work[k] = table_product(held_table_i, k, work[k])

    def store(a, row, real, imag):
        fields[pl.ds(a * LANES + row, 8), :] = jnp.where(main | packed_edge, real, turn(imag, 32))

    inverse_blocks(work, store)
    lane64 = lane_of((64, LANES))
    leaving = []
    for band in range(RADIX):
        upper, lower = (fields[band * LANES + side : band * LANES + side + 64, :] for side in (0, 64))
        chunks[2 * band] = jnp.where(lane64 < 64, upper, turn(lower, 64))
        chunks[2 * band + 1] = jnp.where(lane64 < 64, turn(upper, 64), lower)
        if band % 4 == 3:
            part = pl.ds(2 * (band - 3), 8)
            leaving += started((chunks.at[part], out.at[part], left.at[band // 4]))
    for copy in leaving:
        copy.wait()


def adjoint_columns_b(flags, spectra, edges, sums, pairs, table, table_i):
    n = spectra.shape[0]
    hbm = pl.BlockSpec(memory_space=pltpu.HBM)
    vmem = pl.BlockSpec(memory_space=pltpu.VMEM)
    chunks = (2 * RADIX, 64, LANES)
    return pl.pallas_call(
        adjoint_kernel_b,
        out_shape=pltpu.HBM(chunks, f32),
        in_specs=[pl.BlockSpec(memory_space=pltpu.SMEM), hbm, vmem, vmem, vmem, hbm, hbm, hbm],
        out_specs=hbm,
        scratch_shapes=[
            WORK,
            pltpu.VMEM((n, LANES), f32),
            pairs_like(n),
            TABLE,
            TABLE,
            pltpu.VMEM((n, LANES), f32),
            pltpu.VMEM(chunks, f32),
            pltpu.SemaphoreType.DMA((1,)),
            SIGNALS,
            SIGNALS,
            SIGNALS,
            SIGNALS,
        ],
        compiler_params=pltpu.CompilerParams(vmem_limit_bytes=30 << 20),
        cost_estimate=pl.CostEstimate(flops=0, bytes_accessed=20_000_000, transcendentals=0),
        name="adjoint_columns_b",
    )(flags, in_hbm(spectra), edges, sums, jnp.asarray(lane_tables()[0]), in_hbm(pairs), in_hbm(table), in_hbm(table_i))


def forward_kernel_b(
    flags, moved, spread, pairs, table, table_i, out, edges, model,
    work, here, held_pairs, held_table, held_table_i, fields, chunk, held_model, held_edges,
    got, got_pairs, got_table, got_table_i, left,
):
    first = flags[1] == 1
    read = started((moved, here, got.at[0]))
    later = [
        started(
            table_copies(table, held_table, got_table, g),
            pair_copies(pairs, 1, held_pairs, got_pairs, g),
        )
        for g in range(GROUPS)
    ]
    last = [started(table_copies(table_i, held_table_i, got_table_i, g))[0] for g in range(GROUPS)]
    lane64 = lane_of((64, LANES))
    main64 = lane64 % 64 < 32
    packed64 = jnp.logical_and(lane64 % 64 == 0, first)
    read[0].wait()
    for band in range(RADIX):
        value0, value1 = here[2 * band], here[2 * band + 1]
        sides = (
            jnp.where(lane64 < 64, value0, turn(value1, 64)),
            jnp.where(lane64 < 64, turn(value0, 64), value1),
        )
        for side, value in enumerate(sides):
            row = band * LANES + 64 * side
            fields[0, row : row + 64, :] = value
            fields[1, row : row + 64, :] = jnp.where(
                jnp.logical_and(main64, jnp.logical_not(packed64)), turn(value, 96), 0.0
            )

    def load(a, row):
        return tuple(fields[part, pl.ds(a * LANES + row, 8), :] for part in range(2))

    forward_blocks(load, work)
    lane = lane_of((LANES, LANES))
    turned = (lane <= 32) | (lane == 97)
    for group in range(GROUPS):
        for copy in later[group]:
            copy.wait()
        for k in in_group(group):
            spectrum = table_product(held_table, k, work[k])
            held_model[k] = spectrum
            row = slice(k * LANES, (k + 1) * LANES)
            both = dot(jnp.concatenate(split(spectrum), axis=1), spread[...])
            totals = [
                both[part * LANES : (part + 1) * LANES, :LANES] * held_pairs[0, row, :]
                + both[part * LANES : (part + 1) * LANES, LANES:] * held_pairs[1, row, :]
                for part in range(2)
            ]
            work[k, :LANES], work[k, LANES:] = turn_phase(turned, *totals, 1)
    leaving = started((held_model, model, left.at[1]))
    for group in range(GROUPS):
        last[group].wait()
        for k in in_group(group):
            work[k] = table_product(held_table_i, k, work[k])

    lane8 = lane_of((8, LANES))
    main = lane8 % 64 < 32
    packed = jnp.logical_and(lane8 % 64 == 32, first)

    def store(a, row, real, imag):
        chunk[pl.ds(a * LANES + row, 8), :] = jnp.where(
            jnp.logical_or(main, packed), real, turn(imag, 32)
        )
        held_edges[pl.ds(a * LANES + row, 8), :] = real

    inverse_blocks(work, store)
    leaving += started((chunk, out, left.at[0]), (held_edges, edges, left.at[2]))
    for copy in leaving:
        copy.wait()


def forward_columns_b(flags, moved, pairs, table, table_i, n):
    hbm = pl.BlockSpec(memory_space=pltpu.HBM)
    return pl.pallas_call(
        forward_kernel_b,
        out_shape=[
            pltpu.HBM((n, LANES), f32),
            pltpu.HBM((n, LANES), f32),
            pltpu.HBM((RADIX, 2 * LANES, LANES), f32),
        ],
        in_specs=[
            pl.BlockSpec(memory_space=pltpu.SMEM),
            hbm,
            pl.BlockSpec(memory_space=pltpu.VMEM),
            hbm,
            hbm,
            hbm,
        ],
        out_specs=[hbm, hbm, hbm],
        scratch_shapes=[
            WORK,
            pltpu.VMEM(moved.shape, f32),
            pairs_like(n),
            TABLE,
            TABLE,
            pairs_like(n),
            pltpu.VMEM((n, LANES), f32),
            WORK,
            pltpu.VMEM((n, LANES), f32),
            pltpu.SemaphoreType.DMA((1,)),
            SIGNALS,
            SIGNALS,
            SIGNALS,
            pltpu.SemaphoreType.DMA((3,)),
        ],
        compiler_params=pltpu.CompilerParams(vmem_limit_bytes=34 << 20),
        cost_estimate=pl.CostEstimate(flops=0, bytes_accessed=20_000_000, transcendentals=0),
        name="forward_columns_b",
    )(flags, in_hbm(moved), jnp.asarray(lane_tables()[1]), in_hbm(pairs), in_hbm(table), in_hbm(table_i))


def forward_kernel_a(
    flags, model, edges, pairs, table_i, out,
    work, held_model, held_edges, held_pairs, held_table_i, chunk, got, got_pairs, got_table_i, left,
):
    first = flags[1] == 1
    later = [
        started(
            (model.at[group_steps(g)], held_model.at[group_steps(g)], got.at[g]),
            pair_copies(pairs, 0, held_pairs, got_pairs, g),
            table_copies(table_i, held_table_i, got_table_i, g),
        )
        for g in range(GROUPS)
    ]
    edges_read = started((edges, held_edges, left.at[1]))
    lane = lane_of((LANES, LANES))
    turned = lane // 32 == 2

    def spread(value):
        swapped = turn(value, 64)
        both = (jnp.where(lane < 64, value, swapped), jnp.where(lane < 64, swapped, value))
        return [jnp.where(lane % 64 < 32, layer, turn(layer, 32)) for layer in both]

    for group in range(GROUPS):
        for copy in later[group]:
            copy.wait()
        for k in in_group(group):
            row = slice(k * LANES, (k + 1) * LANES)
            totals = []
            for part in range(2):
                layers = spread(held_model[k, part * LANES : (part + 1) * LANES, :])
                totals.append(layers[0] * held_pairs[0, row, :] + layers[1] * held_pairs[1, row, :])
            real, imag = turn_phase(turned, *totals, 1)
            work[k] = table_product(held_table_i, k, jnp.concatenate([real, imag], axis=0))

    lane8 = lane_of((8, LANES))
    packed = jnp.logical_and(lane8 % 32 == 0, first)

    def store(a, row, real, imag):
        edge = held_edges[pl.ds(a * LANES + row, 8), :]
        edge = jnp.where(lane8 % 64 < 32, turn(edge, 95), turn(edge, 126))
        chunk[pl.ds(a * LANES + row, 8), :LANES] = real
        chunk[pl.ds(a * LANES + row, 8), LANES:] = jnp.where(packed, edge, imag)

    edges_read[0].wait()
    inverse_blocks(work, store)
    for copy in started((chunk, out, left.at[0])):
        copy.wait()


def forward_columns_a(flags, model, edges, pairs, table_i):
    n = edges.shape[0]
    hbm = pl.BlockSpec(memory_space=pltpu.HBM)
    return pl.pallas_call(
        forward_kernel_a,
        out_shape=pltpu.HBM((n, 2 * LANES), f32),
        in_specs=[pl.BlockSpec(memory_space=pltpu.SMEM), hbm, hbm, hbm, hbm],
        out_specs=hbm,
        scratch_shapes=[
            WORK,
            WORK,
            pltpu.VMEM((n, LANES), f32),
            pairs_like(n),
            TABLE,
            pltpu.VMEM((n, 2 * LANES), f32),
            SIGNALS,
            SIGNALS,
            SIGNALS,
            pltpu.SemaphoreType.DMA((2,)),
        ],
        compiler_params=pltpu.CompilerParams(vmem_limit_bytes=26 << 20),
        cost_estimate=pl.CostEstimate(flops=0, bytes_accessed=16_000_000, transcendentals=0),
        name="forward_columns_a",
    )(flags, in_hbm(model), in_hbm(edges), in_hbm(pairs), in_hbm(table_i))


def gradient_kernel(
    counts, listing, spectra, table, gradient, outgoing, sums, held, arrived, blocks, compact
):
    rows, n = gradient.shape
    parts = quad_transpose([spectra[index] for index in range(4)])
    lhs = jnp.concatenate(
        [jnp.concatenate([parts[0], parts[2]], axis=0), jnp.concatenate([parts[1], parts[3]], axis=0)],
        axis=1,
    )
    inverse_step(lhs, table, sums, held, arrived)

    @pl.when(pl.program_id(0) == pl.num_programs(0) - 1)
    def _():
        gradient[:, : n // 2] = sums[0] + sums[1]
        gradient[:, n // 2 :] = sums[0] - sums[1]
        for q in range(RADIX):
            blocks[q * rows : (q + 1) * rows, :] = gradient[:, q * LANES : (q + 1) * LANES]
        owners = outgoing.shape[0]
        cap = outgoing.shape[1]
        total = lax.fori_loop(0, owners, lambda o, t: t + counts[o], jnp.int32(0))

        @pl.loop(0, lax.div(total + 7, 8))
        def _(step):
            for index in range(8):
                at = step * 8 + index
                compact[pl.ds(at, 1), :] = blocks[pl.ds(listing[at], 1), :]

        offset = 0
        for o in range(owners):
            outgoing[o] = compact[pl.ds(offset, cap), :]
            offset = offset + counts[o]


def gradient_rows(counts, listing, spectra, table, rows, n, cap):
    devices = spectra.shape[0]
    owners = counts.shape[0]
    smem = pl.BlockSpec(memory_space=pltpu.SMEM)
    block_count = listing.shape[0]
    return pl.pallas_call(
        gradient_kernel,
        grid=(devices // 4,),
        out_shape=[
            jax.ShapeDtypeStruct((rows, n), f32),
            jax.ShapeDtypeStruct((owners, cap, LANES), f32),
        ],
        in_specs=[
            smem,
            smem,
            pl.BlockSpec((4, rows // 2, LANES), lambda s: (s, 0, 0)),
            pl.BlockSpec(memory_space=pltpu.HBM),
        ],
        out_specs=[
            pl.BlockSpec((rows, n), lambda s: (0, 0)),
            pl.BlockSpec((owners, cap, LANES), lambda s: (0, 0, 0)),
        ],
        scratch_shapes=inverse_scratch(rows, n, devices // 4)
        + [
            pltpu.VMEM((block_count, LANES), f32),
            pltpu.VMEM((block_count + cap, LANES), f32),
        ],
        compiler_params=pltpu.CompilerParams(vmem_limit_bytes=26 << 20),
        name="gradient_rows",
    )(counts, listing, spectra, in_hbm(table))


def owner_segments(counts, incoming, current, weights, room, scales, keep):
    sources, cap, _ = incoming.shape
    length = current.shape[0]
    room[:length, :] = current[...]
    room[length:, :] = jnp.zeros_like(room[length:, :])
    scales[:length, :] = weights[...].astype(f32) * step_size
    scales[length:, :] = jnp.zeros_like(scales[length:, :])
    begin = 0
    for p in range(sources):
        before = room[pl.ds(begin, cap), :]
        after = jnp.clip(before - scales[pl.ds(begin, cap), :] * incoming[p], -1.0, 1.0)
        keep(p, begin, before, after)
        begin = begin + counts[p]


def owner_send_kernel(counts, incoming, current, weights, updated, room, scales):
    def keep(p, begin, before, after):
        updated[p] = after

    owner_segments(counts, incoming, current, weights, room, scales, keep)


def owner_keep_kernel(counts, incoming, current, weights, model_new, room, scales):
    row = lax.broadcasted_iota(jnp.int32, incoming.shape[1:], 0)

    def keep(p, begin, before, after):
        room[pl.ds(begin, before.shape[0]), :] = jnp.where(row < counts[p], after, before)

    owner_segments(counts, incoming, current, weights, room, scales, keep)
    model_new[...] = room[: current.shape[0], :]


def owner_call(kernel, name, shape, counts, incoming, current, weights):
    sources, cap, _ = incoming.shape
    length = current.shape[0]
    return pl.pallas_call(
        kernel,
        out_shape=jax.ShapeDtypeStruct(shape, f32),
        in_specs=[pl.BlockSpec(memory_space=pltpu.SMEM)] + [pl.BlockSpec(memory_space=pltpu.VMEM)] * 3,
        scratch_shapes=[pltpu.VMEM((length + cap, LANES), f32)] * 2,
        compiler_params=pltpu.CompilerParams(vmem_limit_bytes=16 << 20),
        name=name,
    )(counts, incoming, current, weights)


def copy_kernel(source, target):
    target[...] = source[...]


def copied(value):
    return pl.pallas_call(
        copy_kernel,
        out_shape=jax.ShapeDtypeStruct(value.shape, value.dtype),
        compiler_params=pltpu.CompilerParams(vmem_limit_bytes=8 << 20),
        name="copied",
    )(value)


def model_rows_kernel(counts, listing, returned, high, low, out, compact, grid, halves_high, halves_low):
    s = pl.program_id(0)
    owners, cap, _ = returned.shape
    rows = halves_high.shape[1]

    @pl.when(s == 0)
    def _():
        grid[...] = jnp.zeros_like(grid)
        offset = 0
        for o in range(owners):
            compact[pl.ds(offset, cap), :] = returned[o]
            offset = offset + counts[o]
        total = offset

        @pl.loop(0, lax.div(total, 8))
        def _(step):
            for index in range(8):
                at = step * 8 + index
                grid[pl.ds(listing[at], 1), :] = compact[pl.ds(at, 1), :]

        @pl.loop(lax.div(total, 8) * 8, total)
        def _(at):
            grid[pl.ds(listing[at], 1), :] = compact[pl.ds(at, 1), :]

        half = RADIX // 2
        for q in range(half):
            first = grid[q * rows : (q + 1) * rows, :]
            second = grid[(q + half) * rows : (q + half + 1) * rows, :]
            for index, combined in enumerate((first + second, first - second)):
                top, rest = split(combined)
                halves_high[index, :, q * LANES : (q + 1) * LANES] = top
                halves_low[index, :, q * LANES : (q + 1) * LANES] = rest

    side = s // (pl.num_programs(0) // 2)
    result = dot3((halves_high[side], halves_low[side]), (high[0], low[0]))
    half = rows // 2
    parts = quad_transpose(
        [result[:half, :LANES], result[:half, LANES:], result[half:, :LANES], result[half:, LANES:]]
    )
    for index in range(4):
        out[index] = parts[index]


def model_rows(counts, listing, returned, tables, rows, n, devices):
    owners, cap, _ = returned.shape
    block_count = listing.shape[0]
    smem = pl.BlockSpec(memory_space=pltpu.SMEM)
    table = pl.BlockSpec((1, n // 2, 2 * LANES), lambda s: (s, 0, 0))
    return pl.pallas_call(
        model_rows_kernel,
        grid=(devices // 4,),
        out_shape=jax.ShapeDtypeStruct((devices, rows // 2, LANES), f32),
        in_specs=[
            smem,
            smem,
            pl.BlockSpec((owners, cap, LANES), lambda s: (0, 0, 0)),
            table,
            table,
        ],
        out_specs=pl.BlockSpec((4, rows // 2, LANES), lambda s: (s, 0, 0)),
        scratch_shapes=[
            pltpu.VMEM((block_count + cap, LANES), f32),
            pltpu.VMEM((block_count, LANES), f32),
            pltpu.VMEM((2, rows, n // 2), bf16),
            pltpu.VMEM((2, rows, n // 2), bf16),
        ],
        compiler_params=pltpu.CompilerParams(vmem_limit_bytes=16 << 20),
        name="model_rows",
    )(counts, listing, returned, *tables)


def in_hbm(value):
    return pltpu.with_memory_space_constraint(value, pltpu.HBM)


def swap_all(value, axes):
    return lax.all_to_all(value, axes, split_axis=0, concat_axis=0, tiled=True)


def local_paired(misfit, kernel_spec, model_vec, weight_vec, active_list, send_counts):
    both = ("pen", "dep")
    pen_count = lax.axis_size("pen")
    devices = pen_count * lax.axis_size("dep")
    channels, rows, n = misfit.shape
    band = n // pen_count
    forward_np, inverse_np = row_tables(n, devices)
    row_forward = tuple(map(jnp.asarray, forward_np))
    row_inverse = jnp.asarray(np.stack(inverse_np, axis=1))
    forward_np, inverse_np = column_tables()
    col_forward = jnp.asarray(np.stack(forward_np, axis=1))
    col_inverse = jnp.asarray(np.stack(inverse_np, axis=1))
    me = lax.axis_index(both)
    half = devices // 2
    flags = jnp.stack([(me >= half).astype(jnp.int32), (me == 0).astype(jnp.int32)])
    counts = send_counts.reshape(pen_count)
    listing = active_list.reshape(-1)
    places = (listing & (RADIX - 1)) * band + (listing >> 4)
    owner_length = model_vec.shape[2]
    cap = owner_length // pen_count

    spec = kernel_spec.reshape((-1,) + kernel_spec.shape[2:])
    partner = [(d, devices - 1 - d) for d in range(devices)]
    got_b = lax.ppermute(part_spec(flags, spec, 8, 12), both, partner)
    sent_a = part_spec(flags, spec, 0, 8)
    got_a = lax.ppermute(sent_a, both, partner)
    edge = lax.ppermute(
        spec[:, 0:1, :].astype(f32), both, [(d, (devices - d) % half) for d in range(half, devices)]
    )
    source_counts = swap_all(counts, "pen")

    misfit, _ = lax.optimization_barrier((misfit, sent_a))
    chunk_a, chunk_b = misfit_rows(misfit, row_forward, devices)
    chunk_a, got_b, edge, source_counts = lax.optimization_barrier((chunk_a, got_b, edge, source_counts))
    chunk_b, got_a, got_b, edge = lax.optimization_barrier((chunk_b, got_a, got_b, edge))
    columns_a = swap_all(chunk_a, both).reshape(n, 2 * LANES)
    columns_b = swap_all(chunk_b, both).reshape(n, LANES)
    pairs = pair_spec(flags, spec, got_a, got_b, edge)
    sums, edges = adjoint_columns_a(flags, columns_a, pairs, col_forward)
    fields = adjoint_columns_b(flags, columns_b, edges, sums, pairs, col_forward, col_inverse)
    gradient, outgoing = gradient_rows(
        counts, places, swap_all(fields, both), row_inverse, band, n, cap
    )
    incoming = swap_all(outgoing, "pen")
    owned = (
        source_counts,
        incoming,
        model_vec.reshape(owner_length, LANES),
        weight_vec.reshape(owner_length, LANES),
    )
    updated = owner_call(owner_send_kernel, "owner_send", incoming.shape, *owned)
    updated, incoming = lax.optimization_barrier((updated, incoming))
    returned = swap_all(updated, "pen")
    model_new = owner_call(
        owner_keep_kernel, "owner_keep", (owner_length, LANES), owned[0], incoming, *owned[2:]
    )
    model_chunks = model_rows(counts, places, returned, row_forward, band, n, devices)
    model_chunks, gradient = lax.optimization_barrier((model_chunks, gradient))
    gradient = copied(gradient)
    out_b, edges, model = forward_columns_b(
        flags, swap_all(model_chunks, both), pairs, col_forward, col_inverse, n
    )
    back_b = swap_all(out_b.reshape(devices, rows, LANES), both)
    out_a = forward_columns_a(flags, model, edges, pairs, col_inverse)
    back_a = swap_all(out_a.reshape(devices, rows, 2 * LANES), both)
    predicted = predicted_rows(back_b, row_inverse, None, n)
    predicted = predicted_rows(back_a, row_inverse, predicted, n)
    return (gradient[None], model_new.reshape(model_vec.shape), predicted)


def local(misfit, kernel_spec, model_vec, weight_vec, active_list, send_counts):
    sizes = tuple(lax.axis_size(name) for name in ("pen", "dep", "chan"))
    if sizes == (16, 2, 1) and misfit.shape == (6, 64, RADIX * LANES) and kernel_spec.shape[1] == 2:
        plan = local_paired
    else:
        plan = local_general
    return plan(misfit, kernel_spec, model_vec, weight_vec, active_list, send_counts)


def solution(mesh):
    return jax.shard_map(
        local,
        mesh=mesh,
        in_specs=(
            P(("grp", "chan"), ("pen", "dep"), None),
            P("chan", None, ("pen", "dep"), None),
            P(("grp", "dep", "chan"), "pen", None, None),
            P(("grp", "dep", "chan"), "pen", None, None),
            P(("grp", "dep", "chan"), "pen", None),
            P(("grp", "dep", "chan"), "pen", None),
        ),
        out_specs=(
            P(("grp", "dep", "chan"), "pen", None),
            P(("grp", "dep", "chan"), "pen", None, None),
            P(("grp", "chan"), ("pen", "dep"), None),
        ),
        check_vma=False,
    )
```

```python
import functools
import math

import jax
import jax.numpy as jnp
import ml_dtypes
import numpy as np
from jax import lax
from jax.experimental import pallas as pl
from jax.experimental.pallas import tpu as pltpu
from jax.sharding import PartitionSpec as P

inner_radix = 128
step_size = 0.5
highest = lax.Precision.HIGHEST
letters_free = "cdefghij"


def unit_table(length, direction):
    indices = jnp.arange(length, dtype=jnp.int32)
    phases = indices[:, None] * indices[None, :] % length
    angles = 2.0 * math.pi / length * phases.astype(jnp.float32)
    return (jnp.cos(angles), direction * jnp.sin(angles))


def twiddle_table(outer_size, inner_size, direction):
    length = outer_size * inner_size
    phases = (
        jnp.arange(outer_size, dtype=jnp.int32)[:, None]
        * jnp.arange(inner_size, dtype=jnp.int32)[None, :]
        % length
    )
    angles = 2.0 * math.pi / length * phases.astype(jnp.float32)
    return (jnp.cos(angles), direction * jnp.sin(angles))


def contract(formula, operand, tables, real_only):
    product_one = jnp.einsum(formula, operand[0], tables[0], precision=highest)
    if operand[1] is None:
        return (product_one, jnp.einsum(formula, operand[0], tables[1], precision=highest))
    real_value = product_one - jnp.einsum(formula, operand[1], tables[1], precision=highest)
    if real_only:
        return (real_value, None)
    imag_value = jnp.einsum(formula, operand[0], tables[1], precision=highest) + jnp.einsum(
        formula, operand[1], tables[0], precision=highest
    )
    return (real_value, imag_value)


def transform(operand, dimension, direction, real_only):
    full_shape = operand[0].shape
    length = full_shape[dimension]
    inner_size = min(inner_radix, length)
    outer_size = length // inner_size
    split_shape = full_shape[:dimension] + (outer_size, inner_size) + full_shape[dimension + 1 :]
    leading = letters_free[:dimension]
    trailing = letters_free[dimension : len(full_shape) - 1]
    pieces = tuple((None if member is None else member.reshape(split_shape) for member in operand))
    sectioned = contract(
        leading + "ab" + trailing + ",ak->" + leading + "kb" + trailing,
        pieces,
        unit_table(outer_size, direction),
        False,
    )
    twist_real, twist_imag = twiddle_table(outer_size, inner_size, direction)
    twist_shape = (outer_size, inner_size) + (1,) * len(trailing)
    twist_real = twist_real.reshape(twist_shape)
    twist_imag = twist_imag.reshape(twist_shape)
    rotated = (
        sectioned[0] * twist_real - sectioned[1] * twist_imag,
        sectioned[0] * twist_imag + sectioned[1] * twist_real,
    )
    factor = 1.0 / length if direction > 0 else 1.0
    if len(trailing) == 0:
        result = contract(
            leading + "kb,bm->" + leading + "km",
            rotated,
            unit_table(inner_size, direction),
            real_only,
        )
        return tuple(
            (
                (
                    None
                    if member is None
                    else jnp.swapaxes(member, -1, -2).reshape(full_shape) * factor
                )
                for member in result
            )
        )
    result = contract(
        leading + "kb" + trailing + ",bm->" + leading + "mk" + trailing,
        rotated,
        unit_table(inner_size, direction),
        real_only,
    )
    return tuple(
        (None if member is None else member.reshape(full_shape) * factor for member in result)
    )


def exclusive_sum(counts):
    places = jnp.arange(counts.shape[0], dtype=jnp.int32)
    return jnp.sum(jnp.where(places[None, :] < places[:, None], counts[None, :], 0), axis=1)


def imag_channels(chan_place, chan_width):
    channel_ids = chan_place * chan_width + jnp.arange(chan_width, dtype=jnp.int32)
    return ((channel_ids == 2) | (channel_ids == 4))[:, None, None]


def channel_weighted(kernel_view, along):
    total = None
    for channel in range(kernel_view.shape[0]):
        kernel_now = kernel_view[channel].astype(jnp.float32)
        term = kernel_now * along[channel][None, None]
        total = term if total is None else total + term
    return total.reshape(-1, along.shape[1], along.shape[2])


def layer_weighted(kernel_view, grouped):
    ordered = jnp.swapaxes(grouped, 0, 1)
    outputs = []
    for channel in range(kernel_view.shape[0]):
        products = kernel_view[channel].astype(jnp.float32) * ordered
        outputs.append(jnp.sum(products, axis=(0, 1)))
    return jnp.stack(outputs)


def local_general(misfit, kernel_spec, model_vec, weight_vec, active_list, send_counts):
    pen_count = lax.axis_size("pen")
    dep_count = lax.axis_size("dep")
    chan_count = lax.axis_size("chan")
    chan_width, band_width, grid_width = misfit.shape
    column_width = kernel_spec.shape[2]
    kernel_view = kernel_spec.reshape(chan_width, dep_count, chan_count, column_width, grid_width)
    turned = imag_channels(lax.axis_index("chan"), chan_width)
    spectra_real, spectra_imag = transform((misfit, None), 2, -1.0, False)
    columns = (
        lax.all_to_all(spectra_real, ("pen", "dep"), split_axis=2, concat_axis=1, tiled=True),
        lax.all_to_all(spectra_imag, ("pen", "dep"), split_axis=2, concat_axis=1, tiled=True),
    )
    columns = (jnp.swapaxes(columns[0], 1, 2), jnp.swapaxes(columns[1], 1, 2))
    misfit_hat = transform(columns, 2, -1.0, False)
    along_real = jnp.where(turned, misfit_hat[1], misfit_hat[0])
    along_imag = jnp.where(turned, -misfit_hat[0], misfit_hat[1])
    partial_real = channel_weighted(kernel_view, along_real)
    partial_imag = channel_weighted(kernel_view, along_imag)
    fields = transform((partial_real, partial_imag), 2, 1.0, False)
    outgoing = tuple(
        (
            member.reshape(dep_count, chan_count, column_width, pen_count, -1)
            .transpose(3, 0, 1, 4, 2)
            .reshape(pen_count * dep_count, chan_count, -1, column_width)
            for member in fields
        )
    )
    arrived = (
        lax.all_to_all(outgoing[0], ("pen", "dep"), split_axis=0, concat_axis=3, tiled=True),
        lax.all_to_all(outgoing[1], ("pen", "dep"), split_axis=0, concat_axis=3, tiled=True),
    )
    real_fields = transform(arrived, 3, 1.0, True)[0]
    gradient = lax.psum_scatter(real_fields, "chan", scatter_dimension=1, tiled=True).reshape(
        1, -1, grid_width
    )
    blocks = gradient.reshape(-1, 128)
    block_count = blocks.shape[0]
    owner_length = model_vec.shape[2]
    slot_cap = owner_length // pen_count
    counts = send_counts.reshape(pen_count)
    starts = exclusive_sum(counts)
    slot_index = jnp.arange(slot_cap, dtype=jnp.int32)
    slot_valid = slot_index[None, :] < counts[:, None]
    in_list = jnp.minimum(starts[:, None] + slot_index[None, :], block_count - 1)
    listing = active_list.reshape(block_count)
    block_ids = listing[in_list]
    outgoing_blocks = jnp.where(slot_valid[:, :, None], blocks[block_ids], 0.0)
    incoming, arrived_counts = (
        lax.all_to_all(outgoing_blocks, "pen", split_axis=0, concat_axis=0, tiled=True),
        lax.all_to_all(counts.astype(jnp.float32), "pen", split_axis=0, concat_axis=0, tiled=True),
    )
    source_counts = arrived_counts.astype(jnp.int32)
    begins = exclusive_sum(source_counts)
    filled = slot_index[None, :] < source_counts[:, None]
    places = begins[:, None] + slot_index[None, :]
    safe_places = jnp.minimum(places, owner_length - 1)
    current = model_vec.reshape(owner_length, 128)
    scales = weight_vec.reshape(owner_length, 128)
    updated = jnp.clip(
        current[safe_places] - step_size * scales[safe_places].astype(jnp.float32) * incoming,
        -1.0,
        1.0,
    )
    targets = jnp.where(filled, places, owner_length)
    model_new = current.at[targets].set(updated, mode="drop").reshape(model_vec.shape)
    returned = lax.all_to_all(updated, "pen", split_axis=0, concat_axis=0, tiled=True)
    drop_ids = jnp.where(slot_valid, block_ids, block_count)
    model_grid = jnp.zeros((block_count, 128), jnp.float32).at[drop_ids].set(returned, mode="drop")
    model_grid = model_grid.reshape(-1, grid_width)
    surface_field = transform((model_grid, None), 1, -1.0, False)
    moved_columns = (
        lax.all_to_all(surface_field[0], ("pen", "dep"), split_axis=1, concat_axis=0, tiled=True),
        lax.all_to_all(surface_field[1], ("pen", "dep"), split_axis=1, concat_axis=0, tiled=True),
    )
    ordered = tuple(
        (
            member.reshape(pen_count, dep_count, -1, column_width)
            .transpose(1, 3, 0, 2)
            .reshape(dep_count, column_width, grid_width)
            for member in moved_columns
        )
    )
    model_hat = transform(ordered, 2, -1.0, False)
    layers_all = (
        lax.all_gather(model_hat[0], "chan", axis=0, tiled=True),
        lax.all_gather(model_hat[1], "chan", axis=0, tiled=True),
    )
    grouped = tuple(
        (member.reshape(chan_count, dep_count, column_width, grid_width) for member in layers_all)
    )
    summed_real = layer_weighted(kernel_view, grouped[0])
    summed_imag = layer_weighted(kernel_view, grouped[1])
    data_real = jnp.where(turned, -summed_imag, summed_real)
    data_imag = jnp.where(turned, summed_real, summed_imag)
    surface_rows = transform((data_real, data_imag), 2, 1.0, False)
    rows_back = (
        lax.all_to_all(surface_rows[0], ("pen", "dep"), split_axis=2, concat_axis=1, tiled=True),
        lax.all_to_all(surface_rows[1], ("pen", "dep"), split_axis=2, concat_axis=1, tiled=True),
    )
    predicted = jnp.swapaxes(transform(rows_back, 1, 1.0, True)[0], 1, 2)
    return (gradient, model_new, predicted)


RADIX = 16
UNROLL = 4
LANES = 128
TILES = (((0, 0), (1, 32), (2, 64), (3, 96)), ((4, 0), (5, 64)))
EDGES = ((4, 32), (0, 33), (1, 34), (5, 96), (2, 97), (3, 98))
f32 = jnp.float32
bf16 = jnp.bfloat16


def two_terms(table):
    high = table.astype(ml_dtypes.bfloat16)
    low = (table - high.astype(np.float64)).astype(ml_dtypes.bfloat16)
    return (high, low)


def row_frequencies(n, devices, width):
    device = np.arange(devices)[:, None]
    column = np.arange(width // 2)[None, :]
    return width * device + 2 * column + (device >= devices // 2)


@functools.cache
def row_tables(n, devices):
    width = n // devices
    freq = row_frequencies(n, devices, width).reshape(devices // 4, 1, LANES)
    y = np.arange(n // 2)[None, :, None]
    angle = 2.0 * math.pi / n * (freq * y % n)
    real, imag = np.cos(angle), -np.sin(angle)
    imag[0, :, 0] = 1.0 - 2.0 * (np.arange(n // 2) % 2)
    forward = np.concatenate([real, imag], axis=2)
    inverse = 2.0 * forward
    inverse[0, :, 0] *= 0.5
    inverse[0, :, LANES] *= 0.5
    inverse = inverse.swapaxes(1, 2).reshape(2, n // 2, 4, n // 8).transpose(2, 0, 1, 3) / float(n) ** 2
    return (two_terms(forward), two_terms(inverse))


@functools.cache
def column_tables():
    k = np.arange(RADIX)[:, None, None]
    m = np.arange(LANES)[None, :, None]
    b = np.arange(LANES)[None, None, :]
    n = RADIX * LANES
    angle = 2.0 * math.pi / n * ((16 * b * m + b * k) % n)
    real, sine = np.cos(angle), np.sin(angle)
    forward = np.concatenate(
        [np.concatenate([real, sine], axis=2), np.concatenate([-sine, real], axis=2)], axis=1
    )
    return (two_terms(forward), two_terms(forward.swapaxes(1, 2)))


@functools.cache
def lane_tables():
    edges = [lane for _, lane in EDGES]
    fold = np.zeros((2, LANES, LANES))
    spread = np.zeros((LANES, 2, LANES))
    for layer in range(2):
        for _, lane in TILES[1]:
            for i in range(32):
                fold[layer, lane + i, 64 * layer + i] = 1.0
                spread[64 * layer + i, layer, lane + i] = 1.0
        fold[layer, edges, 64 * layer + 32] = 1.0
        spread[64 * layer + 32, layer, edges] = 1.0
    fold = np.concatenate([fold[0], fold[0], fold[1], fold[1]])
    spread = np.tile(spread.reshape(LANES, 2 * LANES), (2, 1))
    return (fold.astype(ml_dtypes.bfloat16), spread.astype(ml_dtypes.bfloat16))


def split(value):
    high = value.astype(bf16)
    return high, (value - high.astype(f32)).astype(bf16)


def dot(a, b):
    return jnp.dot(a, b, preferred_element_type=f32)


def dot3(left, right):
    return dot(left[0], right[0]) + (dot(left[0], right[1]) + dot(left[1], right[0]))


def turn(value, shift):
    shift %= LANES
    return value if shift == 0 else pltpu.roll(value, shift, value.ndim - 1)


def lane_of(shape):
    return lax.broadcasted_iota(jnp.int32, shape, len(shape) - 1)


def quad_transpose(parts):
    lane = lane_of(parts[0].shape)
    low, even = lane < 64, lane % 64 < 32
    a, b, c, d = parts
    a, c = jnp.where(low, a, turn(c, 64)), jnp.where(low, turn(a, 64), c)
    b, d = jnp.where(low, b, turn(d, 64)), jnp.where(low, turn(b, 64), d)
    a, b = jnp.where(even, a, turn(b, 32)), jnp.where(even, turn(a, 96), b)
    c, d = jnp.where(even, c, turn(d, 32)), jnp.where(even, turn(c, 96), d)
    return [a, b, c, d]


def radix4(x, sign):
    (r0, i0), (r1, i1), (r2, i2), (r3, i3) = x
    ar, ai, br, bi = r0 + r2, i0 + i2, r0 - r2, i0 - i2
    cr, ci, dr, di = r1 + r3, i1 + i3, r1 - r3, i1 - i3
    if sign < 0:
        turned = (di, -dr)
    else:
        turned = (-di, dr)
    return [
        (ar + cr, ai + ci),
        (br + turned[0], bi + turned[1]),
        (ar - cr, ai - ci),
        (br - turned[0], bi - turned[1]),
    ]


def radix16(x, sign):
    inner = [radix4([x[4 * a1 + a0] for a1 in range(4)], sign) for a0 in range(4)]
    outputs = [None] * RADIX
    for k0 in range(4):
        column = []
        for a0 in range(4):
            re, im = inner[a0][k0]
            power = a0 * k0 % RADIX
            if power == 4:
                re, im = (im, -re) if sign < 0 else (-im, re)
            elif power == 2 or power == 6:
                scale = math.sqrt(0.5)
                c = scale if power == 2 else -scale
                if sign < 0:
                    re, im = re * c + im * scale, im * c - re * scale
                else:
                    re, im = re * c - im * scale, im * c + re * scale
            elif power != 0:
                c = math.cos(2.0 * math.pi * power / RADIX)
                s = sign * math.sin(2.0 * math.pi * power / RADIX)
                re, im = re * c - im * s, re * s + im * c
            column.append((re, im))
        for k1, value in enumerate(radix4(column, sign)):
            outputs[4 * k1 + k0] = value
    return outputs


def forward_blocks(load, work):
    @pl.loop(0, LANES // 8, unroll=UNROLL)
    def _(step):
        first = pl.multiple_of(step * 8, 8)
        outputs = radix16([load(a, first) for a in range(RADIX)], -1)
        for k, (re, im) in enumerate(outputs):
            work[k, pl.ds(first, 8), :] = re
            work[k, pl.ds(first + LANES, 8), :] = im


def inverse_blocks(work, store):
    @pl.loop(0, LANES // 8, unroll=UNROLL)
    def _(step):
        first = pl.multiple_of(step * 8, 8)
        inputs = [
            (work[k, pl.ds(first, 8), :], work[k, pl.ds(first + LANES, 8), :]) for k in range(RADIX)
        ]
        for a, (re, im) in enumerate(radix16(inputs, 1)):
            store(a, first, re, im)


def column_product(tables, value):
    high, low = split(value)
    wide = dot(tables[0], jnp.concatenate([high, low], axis=1))
    return wide[:, :LANES] + wide[:, LANES:] + dot(tables[1], high)


def choose_rows(wanted, value):
    columns = lax.broadcasted_iota(jnp.int32, (wanted.shape[0], value.shape[0]), 1)
    return dot((columns == wanted).astype(f32).astype(bf16), value)


def part_kernel(flags, spec, sent):
    half = sent.shape[1]
    wanted = 2 * (half - 1 - lax.broadcasted_iota(jnp.int32, (half, 2 * half), 0)) + 1 - flags[0]
    for line in range(sent.shape[0]):
        sent[line] = choose_rows(wanted, spec[line])


def part_spec(flags, spec, begin, end):
    count, width, n = spec.shape
    half = width // 2
    step = 2
    return pl.pallas_call(
        part_kernel,
        grid=((end - begin) // step,),
        out_shape=pltpu.HBM((end - begin, half, n), f32),
        in_specs=[
            pl.BlockSpec(memory_space=pltpu.SMEM),
            pl.BlockSpec((step, width, n), lambda s: (s + begin // step, 0, 0)),
        ],
        out_specs=pl.BlockSpec((step, half, n), lambda s: (s, 0, 0)),
        name="part_spec",
    )(flags, in_hbm(spec))


def pair_kernel(flags, spec, got_a, got_b, edge, pairs, own, mirror, room, own_t, mirror_t):
    step = pl.program_id(0)
    layer = lax.rem(step, 2)
    upper, first = flags[0], flags[1]
    half = got_a.shape[1]
    n = spec.shape[2]
    wanted = 2 * lax.broadcasted_iota(jnp.int32, (half, 2 * half), 0) + upper

    def weight(channel):
        return -0.5 if channel in (2, 4) else 0.5

    for tile in range(2):

        @pl.when(lax.div(step, 2) == tile)
        def _():
            if tile == 1:
                own[...] = jnp.zeros_like(own)
                mirror[...] = jnp.zeros_like(mirror)
                for channel, lane in EDGES:
                    row = edge[2 * channel + layer]
                    own[lane : lane + 1, :] = row * 0.5
                    mirror[lane : lane + 1, :] = row * weight(channel)
            for channel, lane in TILES[tile]:
                line = 2 * channel + layer
                kept = choose_rows(wanted, spec[line])
                own[lane : lane + half, :] = kept * 0.5
                room[0:1, :] = jnp.where(first == 1, kept[0:1, :], edge[line])
                room[1 : 1 + half, :] = got_a[line] if tile == 0 else got_b[line - 8]
                mirror[lane : lane + half, :] = (
                    jnp.where(upper == 1, room[1 : 1 + half, :], room[0:half, :]) * weight(channel)
                )

    for block in range(n // LANES):
        here = slice(block * LANES, (block + 1) * LANES)
        own_t[here, :] = jnp.transpose(own[:, here])
        mirror_t[here, :] = jnp.transpose(mirror[:, here])
    row = lax.broadcasted_iota(jnp.int32, (LANES, LANES), 0)
    for k in range(RADIX):
        wanted_k = LANES - 1 - row if k > 0 else (LANES - row) & (LANES - 1)
        other = mirror_t[pl.ds((RADIX - k) % RADIX, LANES, stride=RADIX), :]
        pairs[0, k * LANES : (k + 1) * LANES, :] = own_t[
            pl.ds(k, LANES, stride=RADIX), :
        ] + choose_rows(wanted_k, other.astype(bf16))


def pair_spec(flags, spec, got_a, got_b, edge):
    count, width, n = spec.shape
    single = pl.Buffered(1)
    return pl.pallas_call(
        pair_kernel,
        grid=(4,),
        out_shape=pltpu.HBM((4, n, LANES), f32),
        in_specs=[
            pl.BlockSpec(memory_space=pltpu.SMEM),
            pl.BlockSpec((count, width, n), lambda s: (0, 0, 0), pipeline_mode=single),
            pl.BlockSpec(got_a.shape, lambda s: (0, 0, 0), pipeline_mode=single),
            pl.BlockSpec(got_b.shape, lambda s: (0, 0, 0), pipeline_mode=single),
            pl.BlockSpec((count, 1, n), lambda s: (0, 0, 0)),
        ],
        out_specs=pl.BlockSpec((1, n, LANES), lambda s: (s, 0, 0)),
        scratch_shapes=[
            pltpu.VMEM((LANES, n), f32),
            pltpu.VMEM((LANES, n), f32),
            pltpu.VMEM((40, n), f32),
            pltpu.VMEM((n, LANES), f32),
            pltpu.VMEM((n, LANES), f32),
        ],
        compiler_params=pltpu.CompilerParams(vmem_limit_bytes=24 << 20),
        cost_estimate=pl.CostEstimate(flops=0, bytes_accessed=60_000_000, transcendentals=0),
        name="pair_spec",
    )(flags, in_hbm(spec), in_hbm(got_a), in_hbm(got_b), edge)


def misfit_rows_kernel(misfit, high, low, out_a, out_b, halves_high, halves_low):
    s = pl.program_id(0)
    channels, rows, n = misfit.shape

    @pl.when(s == 0)
    def _():
        value = misfit[...].reshape(channels * rows, n)
        first, second = value[:, : n // 2], value[:, n // 2 :]
        for index, combined in enumerate((first + second, first - second)):
            halves_high[index], halves_low[index] = split(combined)

    side = s // (pl.num_programs(0) // 2)
    result = dot3((halves_high[side], halves_low[side]), (high[0], low[0]))
    real = [result[rows * c : rows * (c + 1), :LANES] for c in range(channels)]
    imag = [result[rows * c : rows * (c + 1), LANES:] for c in range(channels)]
    parts = (quad_transpose(real[:4]), quad_transpose(imag[:4]))
    for index in range(4):
        out_a[index, :, :LANES] = parts[0][index]
        out_a[index, :, LANES:] = parts[1][index]
    for index, value in enumerate(quad_transpose([real[4], imag[4], real[5], imag[5]])):
        out_b[index] = value


def misfit_rows(misfit, tables, devices):
    channels, rows, n = misfit.shape
    table = pl.BlockSpec((1, n // 2, 2 * LANES), lambda s: (s, 0, 0))
    return pl.pallas_call(
        misfit_rows_kernel,
        grid=(devices // 4,),
        out_shape=[
            jax.ShapeDtypeStruct((devices, rows, 2 * LANES), f32),
            jax.ShapeDtypeStruct((devices, rows, LANES), f32),
        ],
        in_specs=[pl.BlockSpec((channels, rows, n), lambda s: (0, 0, 0)), table, table],
        out_specs=[
            pl.BlockSpec((4, rows, 2 * LANES), lambda s: (s, 0, 0)),
            pl.BlockSpec((4, rows, LANES), lambda s: (s, 0, 0)),
        ],
        scratch_shapes=[pltpu.VMEM((2, channels * rows, n // 2), bf16)] * 2,
        compiler_params=pltpu.CompilerParams(vmem_limit_bytes=22 << 20),
        name="misfit_rows",
    )(misfit, *tables)


TILES_Y = 4


def gather_columns(pieces, lhs_high, lhs_low):
    quads = 2 * lhs_high.shape[2] // (2 * LANES)
    for quad in range(quads):
        side, place = divmod(quad, quads // 2)
        here = slice(place * 2 * LANES, (place + 1) * 2 * LANES)
        lhs_high[side, :, here], lhs_low[side, :, here] = split(pieces(quad))


def half_rows(lhs_high, lhs_low, table):
    even, odd = (dot3((lhs_high[side], lhs_low[side]), (table[0, side, 0], table[0, side, 1])) for side in range(2))
    return even + odd, even - odd


def lhs_scratch(rows, n):
    return [pltpu.VMEM((2, rows, n // 2), bf16)] * 2


def table_spec(n):
    return pl.BlockSpec((1, 2, 2, n // 2, n // 8), lambda s: (s, 0, 0, 0, 0))


def predicted_kernel(begin, count, spectra, table, *refs):
    out, lhs_high, lhs_low, held, left = refs[-5:]
    s = pl.program_id(0)
    rows, n = out.shape[1:]
    width = n // 2 // TILES_Y

    def pieces(quad):
        if count == 2:
            c4r, c4i, c5r, c5i = quad_transpose([spectra[4 * quad + index] for index in range(4)])
            real, imag = (c4r, c5r), (c4i, c5i)
        else:
            real = quad_transpose([spectra[4 * quad + index, :, :LANES] for index in range(4)])
            imag = quad_transpose([spectra[4 * quad + index, :, LANES:] for index in range(4)])
        return jnp.concatenate([jnp.concatenate(pair, axis=1) for pair in zip(real, imag)], axis=0)

    def leave(step, side):
        here = (pl.ds(begin, count), slice(None), pl.ds(side * (n // 2) + step * width, width))
        return pltpu.make_async_copy(held.at[2 * step + side], out.at[here], left.at[2 * step + side])

    @pl.when(s == 0)
    def _():
        gather_columns(pieces, lhs_high, lhs_low)

    halves = half_rows(lhs_high, lhs_low, table)
    for step in range(TILES_Y):

        @pl.when(s == step)
        def _():
            for side in range(2):
                held[2 * step + side] = halves[side].reshape(count, rows, width)
                leave(step, side).start()

    @pl.when(s == TILES_Y - 1)
    def _():
        for step in range(TILES_Y):
            for side in range(2):
                leave(step, side).wait()


def predicted_rows(spectra, table, before, n):
    devices, rows, lanes = spectra.shape
    hbm = pl.BlockSpec(memory_space=pltpu.HBM)
    begin, count = (4, 2) if before is None else (0, 4)
    return pl.pallas_call(
        functools.partial(predicted_kernel, begin, count),
        grid=(TILES_Y,),
        out_shape=pltpu.HBM((6, rows, n), f32),
        in_specs=[
            pl.BlockSpec(spectra.shape, lambda s: (0, 0, 0), pipeline_mode=pl.Buffered(1)),
            table_spec(n),
        ]
        + ([] if before is None else [hbm]),
        out_specs=hbm,
        scratch_shapes=lhs_scratch(count * rows, n)
        + [
            pltpu.VMEM((2 * TILES_Y, count, rows, n // 2 // TILES_Y), f32),
            pltpu.SemaphoreType.DMA((2 * TILES_Y,)),
        ],
        input_output_aliases={} if before is None else {2: 0},
        compiler_params=pltpu.CompilerParams(vmem_limit_bytes=24 << 20),
        name="predicted_rows_b" if before is None else "predicted_rows_a",
    )(spectra, in_hbm(table), *([] if before is None else [before]))


GROUPS = 4


def started(*copies):
    made = [pltpu.make_async_copy(*copy) for copy in copies]
    for copy in made:
        copy.start()
    return made


def group_rows(group):
    size = RADIX // GROUPS * LANES
    return pl.ds(group * size, size)


def group_steps(group):
    return pl.ds(group * (RADIX // GROUPS), RADIX // GROUPS)


def in_group(group):
    return range(group * (RADIX // GROUPS), (group + 1) * (RADIX // GROUPS))


def pair_copies(pairs, tile, held, arrived, group):
    here = group_rows(group)
    return (pairs.at[pl.ds(2 * tile, 2), here], held.at[:, here], arrived.at[group])


def table_copies(table, held, arrived, group):
    here = group_steps(group)
    return (table.at[here], held.at[here], arrived.at[group])


def table_product(table, k, value):
    return column_product((table[k, 0], table[k, 1]), value)


TABLE = pltpu.VMEM((RADIX, 2, 2 * LANES, 2 * LANES), bf16)
WORK = pltpu.VMEM((RADIX, 2 * LANES, LANES), f32)
SIGNALS = pltpu.SemaphoreType.DMA((GROUPS,))


def pairs_like(n):
    return pltpu.VMEM((2, n, LANES), f32)


def turn_phase(channel_lanes, real, imag, sign):
    if sign < 0:
        return jnp.where(channel_lanes, imag, real), jnp.where(channel_lanes, -real, imag)
    return jnp.where(channel_lanes, -imag, real), jnp.where(channel_lanes, real, imag)


def adjoint_kernel_a(
    flags, spectra, pairs, table, sums, edges, work, here, held_pairs, held_table, got, got_pairs, got_table
):
    first = flags[1] == 1
    read = started((spectra, here, got.at[0]))
    later = [
        started(pair_copies(pairs, 0, held_pairs, got_pairs, g), table_copies(table, held_table, got_table, g))
        for g in range(GROUPS)
    ]
    lane8 = lane_of((8, LANES))
    packed = jnp.logical_and(lane8 % 32 == 0, first)
    read[0].wait()

    def load(a, row):
        real = here[pl.ds(a * LANES + row, 8), :LANES]
        imag = here[pl.ds(a * LANES + row, 8), LANES:]
        edges[pl.ds(a * LANES + row, 8), :] = jnp.where(lane8 % 64 == 33, turn(imag, 33), turn(imag, 2))
        return (real, jnp.where(packed, 0.0, imag))

    forward_blocks(load, work)
    lane = lane_of((LANES, LANES))
    turned = lane // 32 == 2
    for group in range(GROUPS):
        for copy in later[group]:
            copy.wait()
        for k in in_group(group):
            spectrum = table_product(held_table, k, work[k])
            real, imag = turn_phase(turned, spectrum[:LANES], spectrum[LANES:], -1)
            row = slice(k * LANES, (k + 1) * LANES)
            for index, value in enumerate((real, imag)):
                v0, v1 = value * held_pairs[0, row, :], value * held_pairs[1, row, :]
                both = jnp.where(lane < 64, v0, turn(v1, 64)) + jnp.where(lane < 64, turn(v0, 64), v1)
                sums[index, row, :] = both + turn(both, 96)


def adjoint_columns_a(flags, spectra, pairs, table):
    n = spectra.shape[0]
    hbm = pl.BlockSpec(memory_space=pltpu.HBM)
    return pl.pallas_call(
        adjoint_kernel_a,
        out_shape=[
            jax.ShapeDtypeStruct((2, n, LANES), f32),
            jax.ShapeDtypeStruct((n, LANES), f32),
        ],
        in_specs=[pl.BlockSpec(memory_space=pltpu.SMEM), hbm, hbm, hbm],
        scratch_shapes=[
            WORK,
            pltpu.VMEM((n, 2 * LANES), f32),
            pairs_like(n),
            TABLE,
            pltpu.SemaphoreType.DMA((1,)),
            SIGNALS,
            SIGNALS,
        ],
        compiler_params=pltpu.CompilerParams(vmem_limit_bytes=24 << 20),
        cost_estimate=pl.CostEstimate(flops=0, bytes_accessed=20_000_000, transcendentals=0),
        name="adjoint_columns_a",
    )(flags, in_hbm(spectra), in_hbm(pairs), in_hbm(table))


def adjoint_kernel_b(
    flags, spectra, edges, sums, fold, pairs, table, table_i, out,
    work, here, held_pairs, held_table, held_table_i, fields, chunks, got, got_pairs, got_table, got_table_i, left,
):
    first = flags[1] == 1
    read = started((spectra, here, got.at[0]))
    lane8 = lane_of((8, LANES))
    main = lane8 % 64 < 32
    packed = jnp.logical_and(lane8 % 64 == 0, first)
    in_place = lane8 % 64 == 32
    packed_edge = jnp.logical_and(in_place, first)
    moved = (lane8 % 64 == 33) | (lane8 % 64 == 34)
    read[0].wait()
    later = [
        started(
            table_copies(table, held_table, got_table, g),
            pair_copies(pairs, 1, held_pairs, got_pairs, g),
        )
        for g in range(GROUPS)
    ]
    last = [started(table_copies(table_i, held_table_i, got_table_i, g))[0] for g in range(GROUPS)]

    def load(a, row):
        value = here[pl.ds(a * LANES + row, 8), :]
        edge = edges[pl.ds(a * LANES + row, 8), :]
        real = jnp.where(main | in_place, value, jnp.where(moved, edge, 0.0))
        imag = jnp.where(jnp.logical_and(main, jnp.logical_not(packed)), turn(value, 96), 0.0)
        return (real, imag)

    forward_blocks(load, work)
    lane = lane_of((LANES, LANES))
    turned = (lane <= 32) | (lane == 97)
    on_main = lane % 64 < 32
    for group in range(GROUPS):
        for copy in later[group][:2]:
            copy.wait()
        for k in in_group(group):
            spectrum = table_product(held_table, k, work[k])
            row = slice(k * LANES, (k + 1) * LANES)
            parts = []
            for value in turn_phase(turned, spectrum[:LANES], spectrum[LANES:], -1):
                terms = split(value * held_pairs[0, row, :]) + split(value * held_pairs[1, row, :])
                parts.append(jnp.concatenate(terms, axis=1))
            folded = dot(jnp.concatenate(parts, axis=0), fold[...])
            for index in range(2):
                half = slice(index * LANES, (index + 1) * LANES)
                work[k, half] = folded[half] + jnp.where(on_main, sums[index, row, :], 0.0)
    for group in range(GROUPS):
        last[group].wait()
        for k in in_group(group):
            work[k] = table_product(held_table_i, k, work[k])

    def store(a, row, real, imag):
        fields[pl.ds(a * LANES + row, 8), :] = jnp.where(main | packed_edge, real, turn(imag, 32))

    inverse_blocks(work, store)
    lane64 = lane_of((64, LANES))
    leaving = []
    for band in range(RADIX):
        upper, lower = (fields[band * LANES + side : band * LANES + side + 64, :] for side in (0, 64))
        chunks[2 * band] = jnp.where(lane64 < 64, upper, turn(lower, 64))
        chunks[2 * band + 1] = jnp.where(lane64 < 64, turn(upper, 64), lower)
        if band % 4 == 3:
            part = pl.ds(2 * (band - 3), 8)
            leaving += started((chunks.at[part], out.at[part], left.at[band // 4]))
    for copy in leaving:
        copy.wait()


def adjoint_columns_b(flags, spectra, edges, sums, pairs, table, table_i):
    n = spectra.shape[0]
    hbm = pl.BlockSpec(memory_space=pltpu.HBM)
    vmem = pl.BlockSpec(memory_space=pltpu.VMEM)
    chunks = (2 * RADIX, 64, LANES)
    return pl.pallas_call(
        adjoint_kernel_b,
        out_shape=pltpu.HBM(chunks, f32),
        in_specs=[pl.BlockSpec(memory_space=pltpu.SMEM), hbm, vmem, vmem, vmem, hbm, hbm, hbm],
        out_specs=hbm,
        scratch_shapes=[
            WORK,
            pltpu.VMEM((n, LANES), f32),
            pairs_like(n),
            TABLE,
            TABLE,
            pltpu.VMEM((n, LANES), f32),
            pltpu.VMEM(chunks, f32),
            pltpu.SemaphoreType.DMA((1,)),
            SIGNALS,
            SIGNALS,
            SIGNALS,
            SIGNALS,
        ],
        compiler_params=pltpu.CompilerParams(vmem_limit_bytes=30 << 20),
        cost_estimate=pl.CostEstimate(flops=0, bytes_accessed=20_000_000, transcendentals=0),
        name="adjoint_columns_b",
    )(flags, in_hbm(spectra), edges, sums, jnp.asarray(lane_tables()[0]), in_hbm(pairs), in_hbm(table), in_hbm(table_i))


def forward_kernel_b(
    flags, moved, spread, pairs, table, table_i, out, edges, model,
    work, here, held_pairs, held_table, held_table_i, fields, chunk, held_model, held_edges,
    got, got_pairs, got_table, got_table_i, left,
):
    first = flags[1] == 1
    read = started((moved, here, got.at[0]))
    lane64 = lane_of((64, LANES))
    main64 = lane64 % 64 < 32
    packed64 = jnp.logical_and(lane64 % 64 == 0, first)
    read[0].wait()
    later = [
        started(
            table_copies(table, held_table, got_table, g),
            pair_copies(pairs, 1, held_pairs, got_pairs, g),
        )
        for g in range(GROUPS)
    ]
    last = [started(table_copies(table_i, held_table_i, got_table_i, g))[0] for g in range(GROUPS)]
    for band in range(RADIX):
        value0, value1 = here[2 * band], here[2 * band + 1]
        sides = (
            jnp.where(lane64 < 64, value0, turn(value1, 64)),
            jnp.where(lane64 < 64, turn(value0, 64), value1),
        )
        for side, value in enumerate(sides):
            row = band * LANES + 64 * side
            fields[0, row : row + 64, :] = value
            fields[1, row : row + 64, :] = jnp.where(
                jnp.logical_and(main64, jnp.logical_not(packed64)), turn(value, 96), 0.0
            )

    def load(a, row):
        return tuple(fields[part, pl.ds(a * LANES + row, 8), :] for part in range(2))

    forward_blocks(load, work)
    lane = lane_of((LANES, LANES))
    turned = (lane <= 32) | (lane == 97)
    for group in range(GROUPS):
        for copy in later[group]:
            copy.wait()
        for k in in_group(group):
            spectrum = table_product(held_table, k, work[k])
            held_model[k] = spectrum
            row = slice(k * LANES, (k + 1) * LANES)
            both = dot(jnp.concatenate(split(spectrum), axis=1), spread[...])
            totals = [
                both[part * LANES : (part + 1) * LANES, :LANES] * held_pairs[0, row, :]
                + both[part * LANES : (part + 1) * LANES, LANES:] * held_pairs[1, row, :]
                for part in range(2)
            ]
            work[k, :LANES], work[k, LANES:] = turn_phase(turned, *totals, 1)
    leaving = started((held_model, model, left.at[1]))
    for group in range(GROUPS):
        last[group].wait()
        for k in in_group(group):
            work[k] = table_product(held_table_i, k, work[k])

    lane8 = lane_of((8, LANES))
    main = lane8 % 64 < 32
    packed = jnp.logical_and(lane8 % 64 == 32, first)

    def store(a, row, real, imag):
        chunk[pl.ds(a * LANES + row, 8), :] = jnp.where(
            jnp.logical_or(main, packed), real, turn(imag, 32)
        )
        held_edges[pl.ds(a * LANES + row, 8), :] = real

    inverse_blocks(work, store)
    leaving += started((chunk, out, left.at[0]), (held_edges, edges, left.at[2]))
    for copy in leaving:
        copy.wait()


def forward_columns_b(flags, moved, pairs, table, table_i, n):
    hbm = pl.BlockSpec(memory_space=pltpu.HBM)
    return pl.pallas_call(
        forward_kernel_b,
        out_shape=[
            pltpu.HBM((n, LANES), f32),
            pltpu.HBM((n, LANES), f32),
            pltpu.HBM((RADIX, 2 * LANES, LANES), f32),
        ],
        in_specs=[
            pl.BlockSpec(memory_space=pltpu.SMEM),
            hbm,
            pl.BlockSpec(memory_space=pltpu.VMEM),
            hbm,
            hbm,
            hbm,
        ],
        out_specs=[hbm, hbm, hbm],
        scratch_shapes=[
            WORK,
            pltpu.VMEM(moved.shape, f32),
            pairs_like(n),
            TABLE,
            TABLE,
            pairs_like(n),
            pltpu.VMEM((n, LANES), f32),
            WORK,
            pltpu.VMEM((n, LANES), f32),
            pltpu.SemaphoreType.DMA((1,)),
            SIGNALS,
            SIGNALS,
            SIGNALS,
            pltpu.SemaphoreType.DMA((3,)),
        ],
        compiler_params=pltpu.CompilerParams(vmem_limit_bytes=34 << 20),
        cost_estimate=pl.CostEstimate(flops=0, bytes_accessed=20_000_000, transcendentals=0),
        name="forward_columns_b",
    )(flags, in_hbm(moved), jnp.asarray(lane_tables()[1]), in_hbm(pairs), in_hbm(table), in_hbm(table_i))


def forward_kernel_a(
    flags, model, edges, pairs, table_i, out,
    work, held_model, held_edges, held_pairs, held_table_i, chunk, got, got_pairs, got_table_i, left,
):
    first = flags[1] == 1
    later = [
        started(
            (model.at[group_steps(g)], held_model.at[group_steps(g)], got.at[g]),
            pair_copies(pairs, 0, held_pairs, got_pairs, g),
            table_copies(table_i, held_table_i, got_table_i, g),
        )
        for g in range(GROUPS)
    ]
    edges_read = started((edges, held_edges, left.at[1]))
    lane = lane_of((LANES, LANES))
    turned = lane // 32 == 2

    def spread(value):
        swapped = turn(value, 64)
        both = (jnp.where(lane < 64, value, swapped), jnp.where(lane < 64, swapped, value))
        return [jnp.where(lane % 64 < 32, layer, turn(layer, 32)) for layer in both]

    for group in range(GROUPS):
        for copy in later[group]:
            copy.wait()
        for k in in_group(group):
            row = slice(k * LANES, (k + 1) * LANES)
            totals = []
            for part in range(2):
                layers = spread(held_model[k, part * LANES : (part + 1) * LANES, :])
                totals.append(layers[0] * held_pairs[0, row, :] + layers[1] * held_pairs[1, row, :])
            real, imag = turn_phase(turned, *totals, 1)
            work[k] = table_product(held_table_i, k, jnp.concatenate([real, imag], axis=0))

    lane8 = lane_of((8, LANES))
    packed = jnp.logical_and(lane8 % 32 == 0, first)

    def store(a, row, real, imag):
        edge = held_edges[pl.ds(a * LANES + row, 8), :]
        edge = jnp.where(lane8 % 64 < 32, turn(edge, 95), turn(edge, 126))
        chunk[pl.ds(a * LANES + row, 8), :LANES] = real
        chunk[pl.ds(a * LANES + row, 8), LANES:] = jnp.where(packed, edge, imag)

    edges_read[0].wait()
    inverse_blocks(work, store)
    for copy in started((chunk, out, left.at[0])):
        copy.wait()


def forward_columns_a(flags, model, edges, pairs, table_i):
    n = edges.shape[0]
    hbm = pl.BlockSpec(memory_space=pltpu.HBM)
    return pl.pallas_call(
        forward_kernel_a,
        out_shape=pltpu.HBM((n, 2 * LANES), f32),
        in_specs=[pl.BlockSpec(memory_space=pltpu.SMEM), hbm, hbm, hbm, hbm],
        out_specs=hbm,
        scratch_shapes=[
            WORK,
            WORK,
            pltpu.VMEM((n, LANES), f32),
            pairs_like(n),
            TABLE,
            pltpu.VMEM((n, 2 * LANES), f32),
            SIGNALS,
            SIGNALS,
            SIGNALS,
            pltpu.SemaphoreType.DMA((2,)),
        ],
        compiler_params=pltpu.CompilerParams(vmem_limit_bytes=26 << 20),
        cost_estimate=pl.CostEstimate(flops=0, bytes_accessed=16_000_000, transcendentals=0),
        name="forward_columns_a",
    )(flags, in_hbm(model), in_hbm(edges), in_hbm(pairs), in_hbm(table_i))


def gradient_kernel(
    counts, listing, spectra, table, gradient, outgoing,
    lhs_high, lhs_low, held, blocks, compact, segments, left, sent,
):
    s = pl.program_id(0)
    rows, n = gradient.shape
    owners, cap, _ = outgoing.shape
    width = n // 2 // TILES_Y

    def pieces(quad):
        parts = quad_transpose([spectra[4 * quad + index] for index in range(4)])
        return jnp.concatenate(
            [jnp.concatenate([parts[0], parts[2]], axis=0), jnp.concatenate([parts[1], parts[3]], axis=0)],
            axis=1,
        )

    def leave(step, side):
        here = (slice(None), pl.ds(side * (n // 2) + step * width, width))
        return pltpu.make_async_copy(held.at[2 * step + side], gradient.at[here], left.at[2 * step + side])

    @pl.when(s == 0)
    def _():
        gather_columns(pieces, lhs_high, lhs_low)

    halves = half_rows(lhs_high, lhs_low, table)
    for step in range(TILES_Y):

        @pl.when(s == step)
        def _():
            for side in range(2):
                held[2 * step + side] = halves[side]
                leave(step, side).start()
                for q in range(width // LANES):
                    place = side * (RADIX // 2) + step * (width // LANES) + q
                    blocks[place * rows : (place + 1) * rows, :] = halves[side][:, q * LANES : (q + 1) * LANES]

    @pl.when(s == TILES_Y - 1)
    def _():
        total = lax.fori_loop(0, owners, lambda o, t: t + counts[o], jnp.int32(0))

        @pl.loop(0, lax.div(total + 15, 16))
        def _(step):
            for index in range(16):
                at = step * 16 + index
                compact[pl.ds(at, 1), :] = blocks[pl.ds(listing[at], 1), :]

        copies = []
        offset = 0
        for o in range(owners):
            segments[o] = compact[pl.ds(offset, cap), :]
            copies.append(pltpu.make_async_copy(segments.at[o], outgoing.at[o], sent.at[o]))
            copies[-1].start()
            offset = offset + counts[o]
        for copy in copies:
            copy.wait()
        for step in range(TILES_Y):
            for side in range(2):
                leave(step, side).wait()


def gradient_rows(counts, listing, spectra, table, rows, n, cap):
    owners = counts.shape[0]
    smem = pl.BlockSpec(memory_space=pltpu.SMEM)
    hbm = pl.BlockSpec(memory_space=pltpu.HBM)
    block_count = listing.shape[0]
    return pl.pallas_call(
        gradient_kernel,
        grid=(TILES_Y,),
        out_shape=[pltpu.HBM((rows, n), f32), pltpu.HBM((owners, cap, LANES), f32)],
        in_specs=[
            smem,
            smem,
            pl.BlockSpec(spectra.shape, lambda s: (0, 0, 0), pipeline_mode=pl.Buffered(1)),
            table_spec(n),
        ],
        out_specs=[hbm, hbm],
        scratch_shapes=lhs_scratch(rows, n)
        + [
            pltpu.VMEM((2 * TILES_Y, rows, n // 2 // TILES_Y), f32),
            pltpu.VMEM((block_count, LANES), f32),
            pltpu.VMEM((block_count + cap, LANES), f32),
            pltpu.VMEM((owners, cap, LANES), f32),
            pltpu.SemaphoreType.DMA((2 * TILES_Y,)),
            pltpu.SemaphoreType.DMA((owners,)),
        ],
        compiler_params=pltpu.CompilerParams(vmem_limit_bytes=20 << 20),
        name="gradient_rows",
    )(counts, listing, spectra, in_hbm(table))


def owner_segments(counts, incoming, current, weights, room, scales, keep):
    sources, cap, _ = incoming.shape
    length = current.shape[0]
    room[:length, :] = current[...]
    room[length:, :] = jnp.zeros_like(room[length:, :])
    scales[:length, :] = weights[...].astype(f32) * step_size
    scales[length:, :] = jnp.zeros_like(scales[length:, :])
    begin = 0
    for p in range(sources):
        before = room[pl.ds(begin, cap), :]
        after = jnp.clip(before - scales[pl.ds(begin, cap), :] * incoming[p], -1.0, 1.0)
        keep(p, begin, before, after)
        begin = begin + counts[p]


def owner_send_kernel(counts, incoming, current, weights, updated, room, scales):
    def keep(p, begin, before, after):
        updated[p] = after

    owner_segments(counts, incoming, current, weights, room, scales, keep)


def owner_keep_kernel(counts, incoming, current, weights, model_new, room, scales):
    row = lax.broadcasted_iota(jnp.int32, incoming.shape[1:], 0)

    def keep(p, begin, before, after):
        room[pl.ds(begin, before.shape[0]), :] = jnp.where(row < counts[p], after, before)

    owner_segments(counts, incoming, current, weights, room, scales, keep)
    model_new[...] = room[: current.shape[0], :]


def owner_call(kernel, name, shape, counts, incoming, current, weights):
    sources, cap, _ = incoming.shape
    length = current.shape[0]
    return pl.pallas_call(
        kernel,
        out_shape=jax.ShapeDtypeStruct(shape, f32),
        in_specs=[pl.BlockSpec(memory_space=pltpu.SMEM)] + [pl.BlockSpec(memory_space=pltpu.VMEM)] * 3,
        scratch_shapes=[pltpu.VMEM((length + cap, LANES), f32)] * 2,
        compiler_params=pltpu.CompilerParams(vmem_limit_bytes=16 << 20),
        name=name,
    )(counts, incoming, current, weights)


def copy_kernel(source, target):
    target[...] = source[...]


def copied(value):
    rows, n = value.shape
    block = pl.BlockSpec((rows // 4, n), lambda s: (s, 0))
    return pl.pallas_call(
        copy_kernel,
        grid=(4,),
        out_shape=pltpu.HBM(value.shape, value.dtype),
        in_specs=[block],
        out_specs=block,
        cost_estimate=pl.CostEstimate(flops=0, bytes_accessed=4_000_000, transcendentals=0),
        name="copied",
    )(in_hbm(value))


def model_rows_kernel(counts, listing, returned, high, low, out, compact, grid, halves_high, halves_low):
    s = pl.program_id(0)
    owners, cap, _ = returned.shape
    rows = halves_high.shape[1]

    @pl.when(s == 0)
    def _():
        grid[...] = jnp.zeros_like(grid)
        offset = 0
        for o in range(owners):
            compact[pl.ds(offset, cap), :] = returned[o]
            offset = offset + counts[o]
        total = offset

        @pl.loop(0, lax.div(total, 8))
        def _(step):
            for index in range(8):
                at = step * 8 + index
                grid[pl.ds(listing[at], 1), :] = compact[pl.ds(at, 1), :]

        @pl.loop(lax.div(total, 8) * 8, total)
        def _(at):
            grid[pl.ds(listing[at], 1), :] = compact[pl.ds(at, 1), :]

        half = RADIX // 2
        for q in range(half):
            first = grid[q * rows : (q + 1) * rows, :]
            second = grid[(q + half) * rows : (q + half + 1) * rows, :]
            for index, combined in enumerate((first + second, first - second)):
                top, rest = split(combined)
                halves_high[index, :, q * LANES : (q + 1) * LANES] = top
                halves_low[index, :, q * LANES : (q + 1) * LANES] = rest

    side = s // (pl.num_programs(0) // 2)
    result = dot3((halves_high[side], halves_low[side]), (high[0], low[0]))
    half = rows // 2
    parts = quad_transpose(
        [result[:half, :LANES], result[:half, LANES:], result[half:, :LANES], result[half:, LANES:]]
    )
    for index in range(4):
        out[index] = parts[index]


def model_rows(counts, listing, returned, tables, rows, n, devices):
    owners, cap, _ = returned.shape
    block_count = listing.shape[0]
    smem = pl.BlockSpec(memory_space=pltpu.SMEM)
    table = pl.BlockSpec((1, n // 2, 2 * LANES), lambda s: (s, 0, 0))
    return pl.pallas_call(
        model_rows_kernel,
        grid=(devices // 4,),
        out_shape=jax.ShapeDtypeStruct((devices, rows // 2, LANES), f32),
        in_specs=[
            smem,
            smem,
            pl.BlockSpec((owners, cap, LANES), lambda s: (0, 0, 0)),
            table,
            table,
        ],
        out_specs=pl.BlockSpec((4, rows // 2, LANES), lambda s: (s, 0, 0)),
        scratch_shapes=[
            pltpu.VMEM((block_count + cap, LANES), f32),
            pltpu.VMEM((block_count, LANES), f32),
            pltpu.VMEM((2, rows, n // 2), bf16),
            pltpu.VMEM((2, rows, n // 2), bf16),
        ],
        compiler_params=pltpu.CompilerParams(vmem_limit_bytes=16 << 20),
        name="model_rows",
    )(counts, listing, returned, *tables)


def in_hbm(value):
    return pltpu.with_memory_space_constraint(value, pltpu.HBM)


def swap_all(value, axes):
    return lax.all_to_all(value, axes, split_axis=0, concat_axis=0, tiled=True)


def local_paired(misfit, kernel_spec, model_vec, weight_vec, active_list, send_counts):
    both = ("pen", "dep")
    pen_count = lax.axis_size("pen")
    devices = pen_count * lax.axis_size("dep")
    channels, rows, n = misfit.shape
    band = n // pen_count
    forward_np, inverse_np = row_tables(n, devices)
    row_forward = tuple(map(jnp.asarray, forward_np))
    row_inverse = jnp.asarray(np.stack(inverse_np, axis=2))
    forward_np, inverse_np = column_tables()
    col_forward = jnp.asarray(np.stack(forward_np, axis=1))
    col_inverse = jnp.asarray(np.stack(inverse_np, axis=1))
    me = lax.axis_index(both)
    half = devices // 2
    flags = jnp.stack([(me >= half).astype(jnp.int32), (me == 0).astype(jnp.int32)])
    counts = send_counts.reshape(pen_count)
    listing = active_list.reshape(-1)
    places = (listing & (RADIX - 1)) * band + (listing >> 4)
    owner_length = model_vec.shape[2]
    cap = owner_length // pen_count

    spec = kernel_spec.reshape((-1,) + kernel_spec.shape[2:])
    partner = [(d, devices - 1 - d) for d in range(devices)]
    got_b = lax.ppermute(part_spec(flags, spec, 8, 12), both, partner)
    sent_a = part_spec(flags, spec, 0, 8)
    got_a = lax.ppermute(sent_a, both, partner)
    edge = lax.ppermute(
        spec[:, 0:1, :].astype(f32), both, [(d, (devices - d) % half) for d in range(half, devices)]
    )
    source_counts = swap_all(counts, "pen")

    misfit, _ = lax.optimization_barrier((misfit, sent_a))
    chunk_a, chunk_b = misfit_rows(misfit, row_forward, devices)
    chunk_a, got_b, edge, source_counts = lax.optimization_barrier((chunk_a, got_b, edge, source_counts))
    chunk_b, got_a, got_b, edge = lax.optimization_barrier((chunk_b, got_a, got_b, edge))
    columns_a = swap_all(chunk_a, both).reshape(n, 2 * LANES)
    columns_b = swap_all(chunk_b, both).reshape(n, LANES)
    pairs = pair_spec(flags, spec, got_a, got_b, edge)
    sums, edges = adjoint_columns_a(flags, columns_a, pairs, col_forward)
    fields = adjoint_columns_b(flags, columns_b, edges, sums, pairs, col_forward, col_inverse)
    gradient, outgoing = gradient_rows(
        counts, places, swap_all(fields, both), row_inverse, band, n, cap
    )
    outgoing, gradient = lax.optimization_barrier((outgoing, gradient))
    incoming = swap_all(outgoing, "pen")
    gradient, source_counts = lax.optimization_barrier((copied(gradient), source_counts))
    owned = (
        source_counts,
        incoming,
        model_vec.reshape(owner_length, LANES),
        weight_vec.reshape(owner_length, LANES),
    )
    updated = owner_call(owner_send_kernel, "owner_send", incoming.shape, *owned)
    updated, incoming = lax.optimization_barrier((updated, incoming))
    returned = swap_all(updated, "pen")
    model_chunks = model_rows(counts, places, returned, row_forward, band, n, devices)
    model_chunks, incoming = lax.optimization_barrier((model_chunks, incoming))
    moved = swap_all(model_chunks, both)
    model_new = owner_call(
        owner_keep_kernel, "owner_keep", (owner_length, LANES), owned[0], incoming, *owned[2:]
    )
    model_new, flags = lax.optimization_barrier((model_new, flags))
    out_b, edges, model = forward_columns_b(
        flags, moved, pairs, col_forward, col_inverse, n
    )
    back_b = swap_all(out_b.reshape(devices, rows, LANES), both)
    out_a = forward_columns_a(flags, model, edges, pairs, col_inverse)
    back_a = swap_all(out_a.reshape(devices, rows, 2 * LANES), both)
    predicted = predicted_rows(back_b, row_inverse, None, n)
    predicted = predicted_rows(back_a, row_inverse, predicted, n)
    return (gradient[None], model_new.reshape(model_vec.shape), predicted)


def local(misfit, kernel_spec, model_vec, weight_vec, active_list, send_counts):
    sizes = tuple(lax.axis_size(name) for name in ("pen", "dep", "chan"))
    if sizes == (16, 2, 1) and misfit.shape == (6, 64, RADIX * LANES) and kernel_spec.shape[1] == 2:
        plan = local_paired
    else:
        plan = local_general
    return plan(misfit, kernel_spec, model_vec, weight_vec, active_list, send_counts)


def solution(mesh):
    return jax.shard_map(
        local,
        mesh=mesh,
        in_specs=(
            P(("grp", "chan"), ("pen", "dep"), None),
            P("chan", None, ("pen", "dep"), None),
            P(("grp", "dep", "chan"), "pen", None, None),
            P(("grp", "dep", "chan"), "pen", None, None),
            P(("grp", "dep", "chan"), "pen", None),
            P(("grp", "dep", "chan"), "pen", None),
        ),
        out_specs=(
            P(("grp", "dep", "chan"), "pen", None),
            P(("grp", "dep", "chan"), "pen", None, None),
            P(("grp", "chan"), ("pen", "dep"), None),
        ),
        check_vma=False,
    )
```

```python
import functools
import math

import jax
import jax.numpy as jnp
import ml_dtypes
import numpy as np
from jax import lax
from jax.experimental import pallas as pl
from jax.experimental.pallas import tpu as pltpu
from jax.sharding import PartitionSpec as P

inner_radix = 128
step_size = 0.5
highest = lax.Precision.HIGHEST
letters_free = "cdefghij"


def unit_table(length, direction):
    indices = jnp.arange(length, dtype=jnp.int32)
    phases = indices[:, None] * indices[None, :] % length
    angles = 2.0 * math.pi / length * phases.astype(jnp.float32)
    return (jnp.cos(angles), direction * jnp.sin(angles))


def twiddle_table(outer_size, inner_size, direction):
    length = outer_size * inner_size
    phases = (
        jnp.arange(outer_size, dtype=jnp.int32)[:, None]
        * jnp.arange(inner_size, dtype=jnp.int32)[None, :]
        % length
    )
    angles = 2.0 * math.pi / length * phases.astype(jnp.float32)
    return (jnp.cos(angles), direction * jnp.sin(angles))


def contract(formula, operand, tables, real_only):
    product_one = jnp.einsum(formula, operand[0], tables[0], precision=highest)
    if operand[1] is None:
        return (product_one, jnp.einsum(formula, operand[0], tables[1], precision=highest))
    real_value = product_one - jnp.einsum(formula, operand[1], tables[1], precision=highest)
    if real_only:
        return (real_value, None)
    imag_value = jnp.einsum(formula, operand[0], tables[1], precision=highest) + jnp.einsum(
        formula, operand[1], tables[0], precision=highest
    )
    return (real_value, imag_value)


def transform(operand, dimension, direction, real_only):
    full_shape = operand[0].shape
    length = full_shape[dimension]
    inner_size = min(inner_radix, length)
    outer_size = length // inner_size
    split_shape = full_shape[:dimension] + (outer_size, inner_size) + full_shape[dimension + 1 :]
    leading = letters_free[:dimension]
    trailing = letters_free[dimension : len(full_shape) - 1]
    pieces = tuple((None if member is None else member.reshape(split_shape) for member in operand))
    sectioned = contract(
        leading + "ab" + trailing + ",ak->" + leading + "kb" + trailing,
        pieces,
        unit_table(outer_size, direction),
        False,
    )
    twist_real, twist_imag = twiddle_table(outer_size, inner_size, direction)
    twist_shape = (outer_size, inner_size) + (1,) * len(trailing)
    twist_real = twist_real.reshape(twist_shape)
    twist_imag = twist_imag.reshape(twist_shape)
    rotated = (
        sectioned[0] * twist_real - sectioned[1] * twist_imag,
        sectioned[0] * twist_imag + sectioned[1] * twist_real,
    )
    factor = 1.0 / length if direction > 0 else 1.0
    if len(trailing) == 0:
        result = contract(
            leading + "kb,bm->" + leading + "km",
            rotated,
            unit_table(inner_size, direction),
            real_only,
        )
        return tuple(
            (
                (
                    None
                    if member is None
                    else jnp.swapaxes(member, -1, -2).reshape(full_shape) * factor
                )
                for member in result
            )
        )
    result = contract(
        leading + "kb" + trailing + ",bm->" + leading + "mk" + trailing,
        rotated,
        unit_table(inner_size, direction),
        real_only,
    )
    return tuple(
        (None if member is None else member.reshape(full_shape) * factor for member in result)
    )


def exclusive_sum(counts):
    places = jnp.arange(counts.shape[0], dtype=jnp.int32)
    return jnp.sum(jnp.where(places[None, :] < places[:, None], counts[None, :], 0), axis=1)


def imag_channels(chan_place, chan_width):
    channel_ids = chan_place * chan_width + jnp.arange(chan_width, dtype=jnp.int32)
    return ((channel_ids == 2) | (channel_ids == 4))[:, None, None]


def channel_weighted(kernel_view, along):
    total = None
    for channel in range(kernel_view.shape[0]):
        kernel_now = kernel_view[channel].astype(jnp.float32)
        term = kernel_now * along[channel][None, None]
        total = term if total is None else total + term
    return total.reshape(-1, along.shape[1], along.shape[2])


def layer_weighted(kernel_view, grouped):
    ordered = jnp.swapaxes(grouped, 0, 1)
    outputs = []
    for channel in range(kernel_view.shape[0]):
        products = kernel_view[channel].astype(jnp.float32) * ordered
        outputs.append(jnp.sum(products, axis=(0, 1)))
    return jnp.stack(outputs)


def local_general(misfit, kernel_spec, model_vec, weight_vec, active_list, send_counts):
    pen_count = lax.axis_size("pen")
    dep_count = lax.axis_size("dep")
    chan_count = lax.axis_size("chan")
    chan_width, band_width, grid_width = misfit.shape
    column_width = kernel_spec.shape[2]
    kernel_view = kernel_spec.reshape(chan_width, dep_count, chan_count, column_width, grid_width)
    turned = imag_channels(lax.axis_index("chan"), chan_width)
    spectra_real, spectra_imag = transform((misfit, None), 2, -1.0, False)
    columns = (
        lax.all_to_all(spectra_real, ("pen", "dep"), split_axis=2, concat_axis=1, tiled=True),
        lax.all_to_all(spectra_imag, ("pen", "dep"), split_axis=2, concat_axis=1, tiled=True),
    )
    columns = (jnp.swapaxes(columns[0], 1, 2), jnp.swapaxes(columns[1], 1, 2))
    misfit_hat = transform(columns, 2, -1.0, False)
    along_real = jnp.where(turned, misfit_hat[1], misfit_hat[0])
    along_imag = jnp.where(turned, -misfit_hat[0], misfit_hat[1])
    partial_real = channel_weighted(kernel_view, along_real)
    partial_imag = channel_weighted(kernel_view, along_imag)
    fields = transform((partial_real, partial_imag), 2, 1.0, False)
    outgoing = tuple(
        (
            member.reshape(dep_count, chan_count, column_width, pen_count, -1)
            .transpose(3, 0, 1, 4, 2)
            .reshape(pen_count * dep_count, chan_count, -1, column_width)
            for member in fields
        )
    )
    arrived = (
        lax.all_to_all(outgoing[0], ("pen", "dep"), split_axis=0, concat_axis=3, tiled=True),
        lax.all_to_all(outgoing[1], ("pen", "dep"), split_axis=0, concat_axis=3, tiled=True),
    )
    real_fields = transform(arrived, 3, 1.0, True)[0]
    gradient = lax.psum_scatter(real_fields, "chan", scatter_dimension=1, tiled=True).reshape(
        1, -1, grid_width
    )
    blocks = gradient.reshape(-1, 128)
    block_count = blocks.shape[0]
    owner_length = model_vec.shape[2]
    slot_cap = owner_length // pen_count
    counts = send_counts.reshape(pen_count)
    starts = exclusive_sum(counts)
    slot_index = jnp.arange(slot_cap, dtype=jnp.int32)
    slot_valid = slot_index[None, :] < counts[:, None]
    in_list = jnp.minimum(starts[:, None] + slot_index[None, :], block_count - 1)
    listing = active_list.reshape(block_count)
    block_ids = listing[in_list]
    outgoing_blocks = jnp.where(slot_valid[:, :, None], blocks[block_ids], 0.0)
    incoming, arrived_counts = (
        lax.all_to_all(outgoing_blocks, "pen", split_axis=0, concat_axis=0, tiled=True),
        lax.all_to_all(counts.astype(jnp.float32), "pen", split_axis=0, concat_axis=0, tiled=True),
    )
    source_counts = arrived_counts.astype(jnp.int32)
    begins = exclusive_sum(source_counts)
    filled = slot_index[None, :] < source_counts[:, None]
    places = begins[:, None] + slot_index[None, :]
    safe_places = jnp.minimum(places, owner_length - 1)
    current = model_vec.reshape(owner_length, 128)
    scales = weight_vec.reshape(owner_length, 128)
    updated = jnp.clip(
        current[safe_places] - step_size * scales[safe_places].astype(jnp.float32) * incoming,
        -1.0,
        1.0,
    )
    targets = jnp.where(filled, places, owner_length)
    model_new = current.at[targets].set(updated, mode="drop").reshape(model_vec.shape)
    returned = lax.all_to_all(updated, "pen", split_axis=0, concat_axis=0, tiled=True)
    drop_ids = jnp.where(slot_valid, block_ids, block_count)
    model_grid = jnp.zeros((block_count, 128), jnp.float32).at[drop_ids].set(returned, mode="drop")
    model_grid = model_grid.reshape(-1, grid_width)
    surface_field = transform((model_grid, None), 1, -1.0, False)
    moved_columns = (
        lax.all_to_all(surface_field[0], ("pen", "dep"), split_axis=1, concat_axis=0, tiled=True),
        lax.all_to_all(surface_field[1], ("pen", "dep"), split_axis=1, concat_axis=0, tiled=True),
    )
    ordered = tuple(
        (
            member.reshape(pen_count, dep_count, -1, column_width)
            .transpose(1, 3, 0, 2)
            .reshape(dep_count, column_width, grid_width)
            for member in moved_columns
        )
    )
    model_hat = transform(ordered, 2, -1.0, False)
    layers_all = (
        lax.all_gather(model_hat[0], "chan", axis=0, tiled=True),
        lax.all_gather(model_hat[1], "chan", axis=0, tiled=True),
    )
    grouped = tuple(
        (member.reshape(chan_count, dep_count, column_width, grid_width) for member in layers_all)
    )
    summed_real = layer_weighted(kernel_view, grouped[0])
    summed_imag = layer_weighted(kernel_view, grouped[1])
    data_real = jnp.where(turned, -summed_imag, summed_real)
    data_imag = jnp.where(turned, summed_real, summed_imag)
    surface_rows = transform((data_real, data_imag), 2, 1.0, False)
    rows_back = (
        lax.all_to_all(surface_rows[0], ("pen", "dep"), split_axis=2, concat_axis=1, tiled=True),
        lax.all_to_all(surface_rows[1], ("pen", "dep"), split_axis=2, concat_axis=1, tiled=True),
    )
    predicted = jnp.swapaxes(transform(rows_back, 1, 1.0, True)[0], 1, 2)
    return (gradient, model_new, predicted)


RADIX = 16
UNROLL = 4
LANES = 128
TILES = (((0, 0), (1, 32), (2, 64), (3, 96)), ((4, 0), (5, 64)))
EDGES = ((4, 32), (0, 33), (1, 34), (5, 96), (2, 97), (3, 98))
f32 = jnp.float32
bf16 = jnp.bfloat16


def two_terms(table):
    high = table.astype(ml_dtypes.bfloat16)
    low = (table - high.astype(np.float64)).astype(ml_dtypes.bfloat16)
    return (high, low)


def row_frequencies(n, devices, width):
    device = np.arange(devices)[:, None]
    column = np.arange(width // 2)[None, :]
    return width * device + 2 * column + (device >= devices // 2)


@functools.cache
def row_tables(n, devices):
    width = n // devices
    freq = row_frequencies(n, devices, width).reshape(devices // 4, 1, LANES)
    y = np.arange(n // 2)[None, :, None]
    angle = 2.0 * math.pi / n * (freq * y % n)
    real, imag = np.cos(angle), -np.sin(angle)
    imag[0, :, 0] = 1.0 - 2.0 * (np.arange(n // 2) % 2)
    forward = np.concatenate([real, imag], axis=2)
    inverse = 2.0 * forward
    inverse[0, :, 0] *= 0.5
    inverse[0, :, LANES] *= 0.5
    inverse = inverse.swapaxes(1, 2).reshape(2, n // 2, 4, n // 8).transpose(2, 0, 1, 3) / float(n) ** 2
    return (two_terms(forward), two_terms(inverse))


@functools.cache
def column_tables():
    k = np.arange(RADIX)[:, None, None]
    m = np.arange(LANES)[None, :, None]
    b = np.arange(LANES)[None, None, :]
    n = RADIX * LANES
    angle = 2.0 * math.pi / n * ((16 * b * m + b * k) % n)
    real, sine = np.cos(angle), np.sin(angle)
    forward = np.concatenate(
        [np.concatenate([real, sine], axis=2), np.concatenate([-sine, real], axis=2)], axis=1
    )
    return (two_terms(forward), two_terms(forward.swapaxes(1, 2)))


@functools.cache
def lane_tables():
    edges = [lane for _, lane in EDGES]
    fold = np.zeros((2, LANES, LANES))
    spread = np.zeros((LANES, 2, LANES))
    for layer in range(2):
        for _, lane in TILES[1]:
            for i in range(32):
                fold[layer, lane + i, 64 * layer + i] = 1.0
                spread[64 * layer + i, layer, lane + i] = 1.0
        fold[layer, edges, 64 * layer + 32] = 1.0
        spread[64 * layer + 32, layer, edges] = 1.0
    fold = np.concatenate([fold[0], fold[0], fold[1], fold[1]])
    spread = np.tile(spread.reshape(LANES, 2 * LANES), (2, 1))
    return (fold.astype(ml_dtypes.bfloat16), spread.astype(ml_dtypes.bfloat16))


def split(value):
    high = value.astype(bf16)
    return high, (value - high.astype(f32)).astype(bf16)


def dot(a, b):
    return jnp.dot(a, b, preferred_element_type=f32)


def dot3(left, right):
    return dot(left[0], right[0]) + (dot(left[0], right[1]) + dot(left[1], right[0]))


def turn(value, shift):
    shift %= LANES
    return value if shift == 0 else pltpu.roll(value, shift, value.ndim - 1)


def lane_of(shape):
    return lax.broadcasted_iota(jnp.int32, shape, len(shape) - 1)


def quad_transpose(parts):
    lane = lane_of(parts[0].shape)
    low, even = lane < 64, lane % 64 < 32
    a, b, c, d = parts
    a, c = jnp.where(low, a, turn(c, 64)), jnp.where(low, turn(a, 64), c)
    b, d = jnp.where(low, b, turn(d, 64)), jnp.where(low, turn(b, 64), d)
    a, b = jnp.where(even, a, turn(b, 32)), jnp.where(even, turn(a, 96), b)
    c, d = jnp.where(even, c, turn(d, 32)), jnp.where(even, turn(c, 96), d)
    return [a, b, c, d]


def radix4(x, sign):
    (r0, i0), (r1, i1), (r2, i2), (r3, i3) = x
    ar, ai, br, bi = r0 + r2, i0 + i2, r0 - r2, i0 - i2
    cr, ci, dr, di = r1 + r3, i1 + i3, r1 - r3, i1 - i3
    if sign < 0:
        turned = (di, -dr)
    else:
        turned = (-di, dr)
    return [
        (ar + cr, ai + ci),
        (br + turned[0], bi + turned[1]),
        (ar - cr, ai - ci),
        (br - turned[0], bi - turned[1]),
    ]


def radix16(x, sign):
    inner = [radix4([x[4 * a1 + a0] for a1 in range(4)], sign) for a0 in range(4)]
    outputs = [None] * RADIX
    for k0 in range(4):
        column = []
        for a0 in range(4):
            re, im = inner[a0][k0]
            power = a0 * k0 % RADIX
            if power == 4:
                re, im = (im, -re) if sign < 0 else (-im, re)
            elif power == 2 or power == 6:
                scale = math.sqrt(0.5)
                c = scale if power == 2 else -scale
                if sign < 0:
                    re, im = re * c + im * scale, im * c - re * scale
                else:
                    re, im = re * c - im * scale, im * c + re * scale
            elif power != 0:
                c = math.cos(2.0 * math.pi * power / RADIX)
                s = sign * math.sin(2.0 * math.pi * power / RADIX)
                re, im = re * c - im * s, re * s + im * c
            column.append((re, im))
        for k1, value in enumerate(radix4(column, sign)):
            outputs[4 * k1 + k0] = value
    return outputs


def forward_blocks(load, work, begin=0, rows=LANES):
    @pl.loop(0, rows // 8, unroll=UNROLL)
    def _(step):
        row = pl.multiple_of(step * 8, 8)
        outputs = radix16([load(a, row) for a in range(RADIX)], -1)
        for k, (re, im) in enumerate(outputs):
            work[k, pl.ds(begin + row, 8), :] = re
            work[k, pl.ds(begin + row + LANES, 8), :] = im


def inverse_blocks(work, store):
    @pl.loop(0, LANES // 8, unroll=UNROLL)
    def _(step):
        first = pl.multiple_of(step * 8, 8)
        inputs = [
            (work[k, pl.ds(first, 8), :], work[k, pl.ds(first + LANES, 8), :]) for k in range(RADIX)
        ]
        for a, (re, im) in enumerate(radix16(inputs, 1)):
            store(a, first, re, im)


def column_product(tables, value):
    high, low = split(value)
    wide = dot(tables[0], jnp.concatenate([high, low], axis=1))
    return wide[:, :LANES] + wide[:, LANES:] + dot(tables[1], high)


def choose_rows(wanted, value):
    columns = lax.broadcasted_iota(jnp.int32, (wanted.shape[0], value.shape[0]), 1)
    return dot((columns == wanted).astype(f32).astype(bf16), value)


def part_kernel(flags, spec, sent):
    half = sent.shape[1]
    wanted = 2 * (half - 1 - lax.broadcasted_iota(jnp.int32, (half, 2 * half), 0)) + 1 - flags[0]
    for line in range(sent.shape[0]):
        sent[line] = choose_rows(wanted, spec[line])


def part_spec(flags, spec, begin, end):
    count, width, n = spec.shape
    half = width // 2
    step = 2
    return pl.pallas_call(
        part_kernel,
        grid=((end - begin) // step,),
        out_shape=pltpu.HBM((end - begin, half, n), f32),
        in_specs=[
            pl.BlockSpec(memory_space=pltpu.SMEM),
            pl.BlockSpec((step, width, n), lambda s: (s + begin // step, 0, 0)),
        ],
        out_specs=pl.BlockSpec((step, half, n), lambda s: (s, 0, 0)),
        name="part_spec",
    )(flags, in_hbm(spec))


def pair_kernel(flags, spec, got_a, got_b, edge, pairs, own, mirror, room, own_t, mirror_t):
    step = pl.program_id(0)
    layer = lax.rem(step, 2)
    upper, first = flags[0], flags[1]
    half = got_a.shape[1]
    n = spec.shape[2]
    wanted = 2 * lax.broadcasted_iota(jnp.int32, (half, 2 * half), 0) + upper

    def weight(channel):
        return -0.5 if channel in (2, 4) else 0.5

    for tile in range(2):

        @pl.when(lax.div(step, 2) == tile)
        def _():
            if tile == 1:
                own[...] = jnp.zeros_like(own)
                mirror[...] = jnp.zeros_like(mirror)
                for channel, lane in EDGES:
                    row = edge[2 * channel + layer]
                    own[lane : lane + 1, :] = row * 0.5
                    mirror[lane : lane + 1, :] = row * weight(channel)
            for channel, lane in TILES[tile]:
                line = 2 * channel + layer
                kept = choose_rows(wanted, spec[line])
                own[lane : lane + half, :] = kept * 0.5
                room[0:1, :] = jnp.where(first == 1, kept[0:1, :], edge[line])
                room[1 : 1 + half, :] = got_a[line] if tile == 0 else got_b[line - 8]
                mirror[lane : lane + half, :] = (
                    jnp.where(upper == 1, room[1 : 1 + half, :], room[0:half, :]) * weight(channel)
                )

    for block in range(n // LANES):
        here = slice(block * LANES, (block + 1) * LANES)
        own_t[here, :] = jnp.transpose(own[:, here])
        mirror_t[here, :] = jnp.transpose(mirror[:, here])
    row = lax.broadcasted_iota(jnp.int32, (LANES, LANES), 0)
    for k in range(RADIX):
        wanted_k = LANES - 1 - row if k > 0 else (LANES - row) & (LANES - 1)
        other = mirror_t[pl.ds((RADIX - k) % RADIX, LANES, stride=RADIX), :]
        pairs[0, k * LANES : (k + 1) * LANES, :] = own_t[
            pl.ds(k, LANES, stride=RADIX), :
        ] + choose_rows(wanted_k, other.astype(bf16))


def pair_spec(flags, spec, got_a, got_b, edge):
    count, width, n = spec.shape
    single = pl.Buffered(1)
    return pl.pallas_call(
        pair_kernel,
        grid=(4,),
        out_shape=pltpu.HBM((4, n, LANES), f32),
        in_specs=[
            pl.BlockSpec(memory_space=pltpu.SMEM),
            pl.BlockSpec((count, width, n), lambda s: (0, 0, 0), pipeline_mode=single),
            pl.BlockSpec(got_a.shape, lambda s: (0, 0, 0), pipeline_mode=single),
            pl.BlockSpec(got_b.shape, lambda s: (0, 0, 0), pipeline_mode=single),
            pl.BlockSpec((count, 1, n), lambda s: (0, 0, 0)),
        ],
        out_specs=pl.BlockSpec((1, n, LANES), lambda s: (s, 0, 0)),
        scratch_shapes=[
            pltpu.VMEM((LANES, n), f32),
            pltpu.VMEM((LANES, n), f32),
            pltpu.VMEM((40, n), f32),
            pltpu.VMEM((n, LANES), f32),
            pltpu.VMEM((n, LANES), f32),
        ],
        compiler_params=pltpu.CompilerParams(vmem_limit_bytes=24 << 20),
        cost_estimate=pl.CostEstimate(flops=0, bytes_accessed=60_000_000, transcendentals=0),
        name="pair_spec",
    )(flags, in_hbm(spec), in_hbm(got_a), in_hbm(got_b), edge)


def misfit_rows_kernel(misfit, high, low, out_a, out_b, halves_high, halves_low):
    s = pl.program_id(0)
    channels, rows, n = misfit.shape

    @pl.when(s == 0)
    def _():
        value = misfit[...].reshape(channels * rows, n)
        first, second = value[:, : n // 2], value[:, n // 2 :]
        for index, combined in enumerate((first + second, first - second)):
            halves_high[index], halves_low[index] = split(combined)

    side = s // (pl.num_programs(0) // 2)
    result = dot3((halves_high[side], halves_low[side]), (high[0], low[0]))
    real = [result[rows * c : rows * (c + 1), :LANES] for c in range(channels)]
    imag = [result[rows * c : rows * (c + 1), LANES:] for c in range(channels)]
    parts = (quad_transpose(real[:4]), quad_transpose(imag[:4]))
    for index in range(4):
        out_a[index, :, :LANES] = parts[0][index]
        out_a[index, :, LANES:] = parts[1][index]
    for index, value in enumerate(quad_transpose([real[4], imag[4], real[5], imag[5]])):
        out_b[index] = value


def misfit_rows(misfit, tables, devices):
    channels, rows, n = misfit.shape
    table = pl.BlockSpec((1, n // 2, 2 * LANES), lambda s: (s, 0, 0))
    return pl.pallas_call(
        misfit_rows_kernel,
        grid=(devices // 4,),
        out_shape=[
            jax.ShapeDtypeStruct((devices, rows, 2 * LANES), f32),
            jax.ShapeDtypeStruct((devices, rows, LANES), f32),
        ],
        in_specs=[pl.BlockSpec((channels, rows, n), lambda s: (0, 0, 0)), table, table],
        out_specs=[
            pl.BlockSpec((4, rows, 2 * LANES), lambda s: (s, 0, 0)),
            pl.BlockSpec((4, rows, LANES), lambda s: (s, 0, 0)),
        ],
        scratch_shapes=[pltpu.VMEM((2, channels * rows, n // 2), bf16)] * 2,
        compiler_params=pltpu.CompilerParams(vmem_limit_bytes=22 << 20),
        name="misfit_rows",
    )(misfit, *tables)


TILES_Y = 4


def gather_columns(pieces, fetched, lhs_high, lhs_low):
    spectra, here, arrived, table, held, ready = fetched
    quads = spectra.shape[0] // 4
    copies = [
        pltpu.make_async_copy(
            spectra.at[pl.ds(4 * quad, 4)], here.at[pl.ds(4 * quad, 4)], arrived.at[quad]
        )
        for quad in range(quads)
    ]
    for copy in copies:
        copy.start()
    for step in range(TILES_Y):
        pltpu.make_async_copy(table.at[step], held.at[step], ready.at[step]).start()
    for quad in range(quads):
        copies[quad].wait()
        side, place = divmod(quad, quads // 2)
        at = slice(place * 2 * LANES, (place + 1) * 2 * LANES)
        lhs_high[side, :, at], lhs_low[side, :, at] = split(pieces(quad))


def half_rows(lhs_high, lhs_low, fetched):
    s = pl.program_id(0)
    _, _, _, table, held, ready = fetched
    pltpu.make_async_copy(table.at[s], held.at[s], ready.at[s]).wait()
    even, odd = (dot3((lhs_high[side], lhs_low[side]), (held[s, side, 0], held[s, side, 1])) for side in range(2))
    return even + odd, even - odd


def row_scratch(spectra, rows, n):
    return [
        pltpu.VMEM(spectra.shape, f32),
        pltpu.SemaphoreType.DMA((spectra.shape[0] // 4,)),
        pltpu.VMEM((TILES_Y, 2, 2, n // 2, n // 2 // TILES_Y), bf16),
        pltpu.SemaphoreType.DMA((TILES_Y,)),
        pltpu.VMEM((2, rows, n // 2), bf16),
        pltpu.VMEM((2, rows, n // 2), bf16),
    ]


def predicted_kernel(begin, count, spectra, table, *refs):
    out, here, arrived, held_table, ready, lhs_high, lhs_low, held, left = refs[-9:]
    fetched = (spectra, here, arrived, table, held_table, ready)
    s = pl.program_id(0)
    rows, n = out.shape[1:]
    width = n // 2 // TILES_Y

    def pieces(quad):
        if count == 2:
            c4r, c4i, c5r, c5i = quad_transpose([here[4 * quad + index] for index in range(4)])
            real, imag = (c4r, c5r), (c4i, c5i)
        else:
            real = quad_transpose([here[4 * quad + index, :, :LANES] for index in range(4)])
            imag = quad_transpose([here[4 * quad + index, :, LANES:] for index in range(4)])
        return jnp.concatenate([jnp.concatenate(pair, axis=1) for pair in zip(real, imag)], axis=0)

    def leave(step, side):
        place = (pl.ds(begin, count), slice(None), pl.ds(side * (n // 2) + step * width, width))
        return pltpu.make_async_copy(held.at[2 * step + side], out.at[place], left.at[2 * step + side])

    @pl.when(s == 0)
    def _():
        gather_columns(pieces, fetched, lhs_high, lhs_low)

    halves = half_rows(lhs_high, lhs_low, fetched)
    for step in range(TILES_Y):

        @pl.when(s == step)
        def _():
            for side in range(2):
                held[2 * step + side] = halves[side].reshape(count, rows, width)
                leave(step, side).start()

    @pl.when(s == TILES_Y - 1)
    def _():
        for step in range(TILES_Y):
            for side in range(2):
                leave(step, side).wait()


def predicted_rows(spectra, table, before, n):
    devices, rows, lanes = spectra.shape
    hbm = pl.BlockSpec(memory_space=pltpu.HBM)
    begin, count = (4, 2) if before is None else (0, 4)
    return pl.pallas_call(
        functools.partial(predicted_kernel, begin, count),
        grid=(TILES_Y,),
        out_shape=pltpu.HBM((6, rows, n), f32),
        in_specs=[pl.BlockSpec(memory_space=pl.ANY)] + [hbm] * (1 if before is None else 2),
        out_specs=hbm,
        scratch_shapes=row_scratch(spectra, count * rows, n)
        + [
            pltpu.VMEM((2 * TILES_Y, count, rows, n // 2 // TILES_Y), f32),
            pltpu.SemaphoreType.DMA((2 * TILES_Y,)),
        ],
        input_output_aliases={} if before is None else {2: 0},
        compiler_params=pltpu.CompilerParams(vmem_limit_bytes=28 << 20),
        name="predicted_rows_b" if before is None else "predicted_rows_a",
    )(spectra, in_hbm(table), *([] if before is None else [before]))


GROUPS = 4


def started(*copies):
    made = [pltpu.make_async_copy(*copy) for copy in copies]
    for copy in made:
        copy.start()
    return made


def group_rows(group):
    size = RADIX // GROUPS * LANES
    return pl.ds(group * size, size)


def group_steps(group):
    return pl.ds(group * (RADIX // GROUPS), RADIX // GROUPS)


def in_group(group):
    return range(group * (RADIX // GROUPS), (group + 1) * (RADIX // GROUPS))


def pair_copies(pairs, tile, held, arrived, group):
    here = group_rows(group)
    return (pairs.at[pl.ds(2 * tile, 2), here], held.at[:, here], arrived.at[group])


def table_copies(table, held, arrived, group):
    here = group_steps(group)
    return (table.at[here], held.at[here], arrived.at[group])


def stacked_product(table, k, value):
    high, low = split(value)
    terms = jnp.concatenate([table[k, 0], table[k, 1]], axis=0)
    wide = dot(terms, jnp.concatenate([high, low], axis=1))
    size = high.shape[0]
    return wide[:size, :LANES] + wide[:size, LANES:] + wide[size:, :LANES]


def table_product(table, k, value):
    return column_product((table[k, 0], table[k, 1]), value)


TABLE = pltpu.VMEM((RADIX, 2, 2 * LANES, 2 * LANES), bf16)
WORK = pltpu.VMEM((RADIX, 2 * LANES, LANES), f32)
SIGNALS = pltpu.SemaphoreType.DMA((GROUPS,))


def pairs_like(n):
    return pltpu.VMEM((2, n, LANES), f32)


def turn_phase(channel_lanes, real, imag, sign):
    if sign < 0:
        return jnp.where(channel_lanes, imag, real), jnp.where(channel_lanes, -real, imag)
    return jnp.where(channel_lanes, -imag, real), jnp.where(channel_lanes, real, imag)


def adjoint_kernel_a(
    flags, spectra, pairs, table, sums, edges, work, here, held_pairs, held_table, got, got_pairs, got_table
):
    first = flags[1] == 1
    read = started((spectra, here, got.at[0]))
    later = [
        started(pair_copies(pairs, 0, held_pairs, got_pairs, g), table_copies(table, held_table, got_table, g))
        for g in range(GROUPS)
    ]
    lane8 = lane_of((8, LANES))
    packed = jnp.logical_and(lane8 % 32 == 0, first)
    read[0].wait()

    def load(a, row):
        real = here[pl.ds(a * LANES + row, 8), :LANES]
        imag = here[pl.ds(a * LANES + row, 8), LANES:]
        edges[pl.ds(a * LANES + row, 8), :] = jnp.where(lane8 % 64 == 33, turn(imag, 33), turn(imag, 2))
        return (real, jnp.where(packed, 0.0, imag))

    forward_blocks(load, work)
    lane = lane_of((LANES, LANES))
    turned = lane // 32 == 2
    for group in range(GROUPS):
        for copy in later[group]:
            copy.wait()
        for k in in_group(group):
            spectrum = table_product(held_table, k, work[k])
            real, imag = turn_phase(turned, spectrum[:LANES], spectrum[LANES:], -1)
            row = slice(k * LANES, (k + 1) * LANES)
            for index, value in enumerate((real, imag)):
                v0, v1 = value * held_pairs[0, row, :], value * held_pairs[1, row, :]
                both = jnp.where(lane < 64, v0, turn(v1, 64)) + jnp.where(lane < 64, turn(v0, 64), v1)
                sums[index, row, :] = both + turn(both, 96)


def adjoint_columns_a(flags, spectra, pairs, table):
    n = spectra.shape[0]
    hbm = pl.BlockSpec(memory_space=pltpu.HBM)
    return pl.pallas_call(
        adjoint_kernel_a,
        out_shape=[
            jax.ShapeDtypeStruct((2, n, LANES), f32),
            jax.ShapeDtypeStruct((n, LANES), f32),
        ],
        in_specs=[pl.BlockSpec(memory_space=pltpu.SMEM), hbm, hbm, hbm],
        scratch_shapes=[
            WORK,
            pltpu.VMEM((n, 2 * LANES), f32),
            pairs_like(n),
            TABLE,
            pltpu.SemaphoreType.DMA((1,)),
            SIGNALS,
            SIGNALS,
        ],
        compiler_params=pltpu.CompilerParams(vmem_limit_bytes=24 << 20),
        cost_estimate=pl.CostEstimate(flops=0, bytes_accessed=20_000_000, transcendentals=0),
        name="adjoint_columns_a",
    )(flags, in_hbm(spectra), in_hbm(pairs), in_hbm(table))


def adjoint_kernel_b(
    flags, spectra, edges, sums, fold, pairs, table, table_i, out,
    work, here, held_pairs, held_table, held_table_i, fields, chunks, got, got_pairs, got_table, got_table_i, left,
):
    first = flags[1] == 1
    read = started((spectra, here, got.at[0]))
    lane8 = lane_of((8, LANES))
    main = lane8 % 64 < 32
    packed = jnp.logical_and(lane8 % 64 == 0, first)
    in_place = lane8 % 64 == 32
    packed_edge = jnp.logical_and(in_place, first)
    moved = (lane8 % 64 == 33) | (lane8 % 64 == 34)
    read[0].wait()
    later = [
        started(
            table_copies(table, held_table, got_table, g),
            pair_copies(pairs, 1, held_pairs, got_pairs, g),
        )
        for g in range(GROUPS)
    ]
    last = [started(table_copies(table_i, held_table_i, got_table_i, g))[0] for g in range(GROUPS)]

    def load(a, row):
        value = here[pl.ds(a * LANES + row, 8), :]
        edge = edges[pl.ds(a * LANES + row, 8), :]
        real = jnp.where(main | in_place, value, jnp.where(moved, edge, 0.0))
        imag = jnp.where(jnp.logical_and(main, jnp.logical_not(packed)), turn(value, 96), 0.0)
        return (real, imag)

    forward_blocks(load, work)
    lane = lane_of((LANES, LANES))
    turned = (lane <= 32) | (lane == 97)
    on_main = lane % 64 < 32
    for group in range(GROUPS):
        for copy in later[group][:2]:
            copy.wait()
        for k in in_group(group):
            spectrum = stacked_product(held_table, k, work[k])
            row = slice(k * LANES, (k + 1) * LANES)
            parts = []
            for value in turn_phase(turned, spectrum[:LANES], spectrum[LANES:], -1):
                terms = split(value * held_pairs[0, row, :]) + split(value * held_pairs[1, row, :])
                parts.append(jnp.concatenate(terms, axis=1))
            folded = dot(jnp.concatenate(parts, axis=0), fold[...])
            for index in range(2):
                half = slice(index * LANES, (index + 1) * LANES)
                work[k, half] = folded[half] + jnp.where(on_main, sums[index, row, :], 0.0)
    for group in range(GROUPS):
        last[group].wait()
        for k in in_group(group):
            work[k] = stacked_product(held_table_i, k, work[k])

    def store(a, row, real, imag):
        fields[pl.ds(a * LANES + row, 8), :] = jnp.where(main | packed_edge, real, turn(imag, 32))

    inverse_blocks(work, store)
    lane64 = lane_of((64, LANES))
    leaving = []
    for band in range(RADIX):
        upper, lower = (fields[band * LANES + side : band * LANES + side + 64, :] for side in (0, 64))
        chunks[2 * band] = jnp.where(lane64 < 64, upper, turn(lower, 64))
        chunks[2 * band + 1] = jnp.where(lane64 < 64, turn(upper, 64), lower)
        if band % 4 == 3:
            part = pl.ds(2 * (band - 3), 8)
            leaving += started((chunks.at[part], out.at[part], left.at[band // 4]))
    for copy in leaving:
        copy.wait()


def adjoint_columns_b(flags, spectra, edges, sums, pairs, table, table_i):
    n = spectra.shape[0]
    hbm = pl.BlockSpec(memory_space=pltpu.HBM)
    vmem = pl.BlockSpec(memory_space=pltpu.VMEM)
    chunks = (2 * RADIX, 64, LANES)
    return pl.pallas_call(
        adjoint_kernel_b,
        out_shape=pltpu.HBM(chunks, f32),
        in_specs=[pl.BlockSpec(memory_space=pltpu.SMEM), hbm, vmem, vmem, vmem, hbm, hbm, hbm],
        out_specs=hbm,
        scratch_shapes=[
            WORK,
            pltpu.VMEM((n, LANES), f32),
            pairs_like(n),
            TABLE,
            TABLE,
            pltpu.VMEM((n, LANES), f32),
            pltpu.VMEM(chunks, f32),
            pltpu.SemaphoreType.DMA((1,)),
            SIGNALS,
            SIGNALS,
            SIGNALS,
            SIGNALS,
        ],
        compiler_params=pltpu.CompilerParams(vmem_limit_bytes=30 << 20),
        cost_estimate=pl.CostEstimate(flops=0, bytes_accessed=20_000_000, transcendentals=0),
        name="adjoint_columns_b",
    )(flags, in_hbm(spectra), edges, sums, jnp.asarray(lane_tables()[0]), in_hbm(pairs), in_hbm(table), in_hbm(table_i))


def forward_kernel_b(
    flags, moved, spread, pairs, table, table_i, out, edges, model,
    work, here, held_pairs, held_table, held_table_i, chunk, held_model, held_edges,
    got, got_pairs, got_table, got_table_i, left,
):
    first = flags[1] == 1
    read = started((moved, here, got.at[0]))
    read[0].wait()
    later = [
        started(
            table_copies(table, held_table, got_table, g),
            pair_copies(pairs, 1, held_pairs, got_pairs, g),
        )
        for g in range(GROUPS)
    ]
    last = [started(table_copies(table_i, held_table_i, got_table_i, g))[0] for g in range(GROUPS)]
    lane8 = lane_of((8, LANES))
    main = lane8 % 64 < 32
    real_only = jnp.logical_or(jnp.logical_not(main), jnp.logical_and(lane8 % 64 == 0, first))

    for side in range(2):

        def load(band, row):
            value0, value1 = here[2 * band, pl.ds(row, 8), :], here[2 * band + 1, pl.ds(row, 8), :]
            if side == 0:
                value = jnp.where(lane8 < 64, value0, turn(value1, 64))
            else:
                value = jnp.where(lane8 < 64, turn(value0, 64), value1)
            return (value, jnp.where(real_only, 0.0, turn(value, 96)))

        forward_blocks(load, work, 64 * side, 64)
    lane = lane_of((LANES, LANES))
    turned = (lane <= 32) | (lane == 97)
    for group in range(GROUPS):
        for copy in later[group]:
            copy.wait()
        for k in in_group(group):
            spectrum = table_product(held_table, k, work[k])
            held_model[k] = spectrum
            row = slice(k * LANES, (k + 1) * LANES)
            both = dot(jnp.concatenate(split(spectrum), axis=1), spread[...])
            totals = [
                both[part * LANES : (part + 1) * LANES, :LANES] * held_pairs[0, row, :]
                + both[part * LANES : (part + 1) * LANES, LANES:] * held_pairs[1, row, :]
                for part in range(2)
            ]
            work[k, :LANES], work[k, LANES:] = turn_phase(turned, *totals, 1)
    leaving = started((held_model, model, left.at[1]))
    for group in range(GROUPS):
        last[group].wait()
        for k in in_group(group):
            work[k] = table_product(held_table_i, k, work[k])

    packed = jnp.logical_and(lane8 % 64 == 32, first)

    def store(a, row, real, imag):
        chunk[pl.ds(a * LANES + row, 8), :] = jnp.where(
            jnp.logical_or(main, packed), real, turn(imag, 32)
        )
        held_edges[pl.ds(a * LANES + row, 8), :] = real

    inverse_blocks(work, store)
    leaving += started((chunk, out, left.at[0]), (held_edges, edges, left.at[2]))
    for copy in leaving:
        copy.wait()


def forward_columns_b(flags, moved, pairs, table, table_i, n):
    hbm = pl.BlockSpec(memory_space=pltpu.HBM)
    return pl.pallas_call(
        forward_kernel_b,
        out_shape=[
            pltpu.HBM((n, LANES), f32),
            pltpu.HBM((n, LANES), f32),
            pltpu.HBM((RADIX, 2 * LANES, LANES), f32),
        ],
        in_specs=[
            pl.BlockSpec(memory_space=pltpu.SMEM),
            hbm,
            pl.BlockSpec(memory_space=pltpu.VMEM),
            hbm,
            hbm,
            hbm,
        ],
        out_specs=[hbm, hbm, hbm],
        scratch_shapes=[
            WORK,
            pltpu.VMEM(moved.shape, f32),
            pairs_like(n),
            TABLE,
            TABLE,
            pltpu.VMEM((n, LANES), f32),
            WORK,
            pltpu.VMEM((n, LANES), f32),
            pltpu.SemaphoreType.DMA((1,)),
            SIGNALS,
            SIGNALS,
            SIGNALS,
            pltpu.SemaphoreType.DMA((3,)),
        ],
        compiler_params=pltpu.CompilerParams(vmem_limit_bytes=34 << 20),
        cost_estimate=pl.CostEstimate(flops=0, bytes_accessed=20_000_000, transcendentals=0),
        name="forward_columns_b",
    )(flags, in_hbm(moved), jnp.asarray(lane_tables()[1]), in_hbm(pairs), in_hbm(table), in_hbm(table_i))


def forward_kernel_a(
    flags, model, edges, pairs, table_i, out,
    work, held_model, held_edges, held_pairs, held_table_i, chunk, got, got_pairs, got_table_i, left,
):
    first = flags[1] == 1
    later = [
        started(
            (model.at[group_steps(g)], held_model.at[group_steps(g)], got.at[g]),
            pair_copies(pairs, 0, held_pairs, got_pairs, g),
            table_copies(table_i, held_table_i, got_table_i, g),
        )
        for g in range(GROUPS)
    ]
    edges_read = started((edges, held_edges, left.at[1]))
    lane = lane_of((LANES, LANES))
    turned = lane // 32 == 2

    def spread(value):
        swapped = turn(value, 64)
        both = (jnp.where(lane < 64, value, swapped), jnp.where(lane < 64, swapped, value))
        return [jnp.where(lane % 64 < 32, layer, turn(layer, 32)) for layer in both]

    for group in range(GROUPS):
        for copy in later[group]:
            copy.wait()
        for k in in_group(group):
            row = slice(k * LANES, (k + 1) * LANES)
            totals = []
            for part in range(2):
                layers = spread(held_model[k, part * LANES : (part + 1) * LANES, :])
                totals.append(layers[0] * held_pairs[0, row, :] + layers[1] * held_pairs[1, row, :])
            real, imag = turn_phase(turned, *totals, 1)
            work[k] = table_product(held_table_i, k, jnp.concatenate([real, imag], axis=0))

    lane8 = lane_of((8, LANES))
    packed = jnp.logical_and(lane8 % 32 == 0, first)

    def store(a, row, real, imag):
        edge = held_edges[pl.ds(a * LANES + row, 8), :]
        edge = jnp.where(lane8 % 64 < 32, turn(edge, 95), turn(edge, 126))
        chunk[pl.ds(a * LANES + row, 8), :LANES] = real
        chunk[pl.ds(a * LANES + row, 8), LANES:] = jnp.where(packed, edge, imag)

    edges_read[0].wait()
    inverse_blocks(work, store)
    for copy in started((chunk, out, left.at[0])):
        copy.wait()


def forward_columns_a(flags, model, edges, pairs, table_i):
    n = edges.shape[0]
    hbm = pl.BlockSpec(memory_space=pltpu.HBM)
    return pl.pallas_call(
        forward_kernel_a,
        out_shape=pltpu.HBM((n, 2 * LANES), f32),
        in_specs=[pl.BlockSpec(memory_space=pltpu.SMEM), hbm, hbm, hbm, hbm],
        out_specs=hbm,
        scratch_shapes=[
            WORK,
            WORK,
            pltpu.VMEM((n, LANES), f32),
            pairs_like(n),
            TABLE,
            pltpu.VMEM((n, 2 * LANES), f32),
            SIGNALS,
            SIGNALS,
            SIGNALS,
            pltpu.SemaphoreType.DMA((2,)),
        ],
        compiler_params=pltpu.CompilerParams(vmem_limit_bytes=26 << 20),
        cost_estimate=pl.CostEstimate(flops=0, bytes_accessed=16_000_000, transcendentals=0),
        name="forward_columns_a",
    )(flags, in_hbm(model), in_hbm(edges), in_hbm(pairs), in_hbm(table_i))


def gradient_kernel(
    counts, listing, spectra, table, gradient, outgoing,
    here, arrived, held_table, ready, lhs_high, lhs_low, held, blocks, compact, segments, left, sent,
):
    s = pl.program_id(0)
    rows, n = gradient.shape
    fetched = (spectra, here, arrived, table, held_table, ready)
    owners, cap, _ = outgoing.shape
    width = n // 2 // TILES_Y

    def pieces(quad):
        parts = quad_transpose([here[4 * quad + index] for index in range(4)])
        return jnp.concatenate(
            [jnp.concatenate([parts[0], parts[2]], axis=0), jnp.concatenate([parts[1], parts[3]], axis=0)],
            axis=1,
        )

    def leave(step, side):
        place = (slice(None), pl.ds(side * (n // 2) + step * width, width))
        return pltpu.make_async_copy(held.at[2 * step + side], gradient.at[place], left.at[2 * step + side])

    @pl.when(s == 0)
    def _():
        gather_columns(pieces, fetched, lhs_high, lhs_low)

    halves = half_rows(lhs_high, lhs_low, fetched)
    for step in range(TILES_Y):

        @pl.when(s == step)
        def _():
            for side in range(2):
                held[2 * step + side] = halves[side]
                leave(step, side).start()
                for q in range(width // LANES):
                    place = side * (RADIX // 2) + step * (width // LANES) + q
                    blocks[place * rows : (place + 1) * rows, :] = halves[side][:, q * LANES : (q + 1) * LANES]

    @pl.when(s == TILES_Y - 1)
    def _():
        total = lax.fori_loop(0, owners, lambda o, t: t + counts[o], jnp.int32(0))

        full = total == blocks.shape[0]

        @pl.when(full)
        def _():
            for q in range(RADIX):
                compact[pl.ds(q, rows, stride=RADIX), :] = blocks[q * rows : (q + 1) * rows, :]

        @pl.loop(0, jnp.where(full, 0, lax.div(total + 15, 16)))
        def _(step):
            for index in range(16):
                at = step * 16 + index
                compact[pl.ds(at, 1), :] = blocks[pl.ds(listing[at], 1), :]

        copies = []
        offset = 0
        for o in range(owners):
            segments[o] = compact[pl.ds(offset, cap), :]
            copies.append(pltpu.make_async_copy(segments.at[o], outgoing.at[o], sent.at[o]))
            copies[-1].start()
            offset = offset + counts[o]
        for copy in copies:
            copy.wait()
        for step in range(TILES_Y):
            for side in range(2):
                leave(step, side).wait()


def gradient_rows(counts, listing, spectra, table, rows, n, cap):
    owners = counts.shape[0]
    smem = pl.BlockSpec(memory_space=pltpu.SMEM)
    hbm = pl.BlockSpec(memory_space=pltpu.HBM)
    block_count = listing.shape[0]
    return pl.pallas_call(
        gradient_kernel,
        grid=(TILES_Y,),
        out_shape=[pltpu.HBM((rows, n), f32), pltpu.HBM((owners, cap, LANES), f32)],
        in_specs=[
            smem,
            smem,
            pl.BlockSpec(memory_space=pl.ANY),
            hbm,
        ],
        out_specs=[hbm, hbm],
        scratch_shapes=row_scratch(spectra, rows, n)
        + [
            pltpu.VMEM((2 * TILES_Y, rows, n // 2 // TILES_Y), f32),
            pltpu.VMEM((block_count, LANES), f32),
            pltpu.VMEM((block_count + cap, LANES), f32),
            pltpu.VMEM((owners, cap, LANES), f32),
            pltpu.SemaphoreType.DMA((2 * TILES_Y,)),
            pltpu.SemaphoreType.DMA((owners,)),
        ],
        compiler_params=pltpu.CompilerParams(vmem_limit_bytes=26 << 20),
        name="gradient_rows",
    )(counts, listing, spectra, in_hbm(table))


def owner_segments(counts, incoming, current, weights, room, scales, keep):
    sources, cap, _ = incoming.shape
    length = current.shape[0]
    room[:length, :] = current[...]
    room[length:, :] = jnp.zeros_like(room[length:, :])
    scales[:length, :] = weights[...].astype(f32) * step_size
    scales[length:, :] = jnp.zeros_like(scales[length:, :])
    begin = 0
    for p in range(sources):
        before = room[pl.ds(begin, cap), :]
        after = jnp.clip(before - scales[pl.ds(begin, cap), :] * incoming[p], -1.0, 1.0)
        keep(p, begin, before, after)
        begin = begin + counts[p]


def owner_send_kernel(counts, incoming, current, weights, updated, room, scales):
    def keep(p, begin, before, after):
        updated[p] = after

    owner_segments(counts, incoming, current, weights, room, scales, keep)


def owner_keep_kernel(counts, incoming, current, weights, model_new, room, scales):
    row = lax.broadcasted_iota(jnp.int32, incoming.shape[1:], 0)

    def keep(p, begin, before, after):
        room[pl.ds(begin, before.shape[0]), :] = jnp.where(row < counts[p], after, before)

    owner_segments(counts, incoming, current, weights, room, scales, keep)
    model_new[...] = room[: current.shape[0], :]


def owner_call(kernel, name, shape, counts, incoming, current, weights):
    sources, cap, _ = incoming.shape
    length = current.shape[0]
    return pl.pallas_call(
        kernel,
        out_shape=jax.ShapeDtypeStruct(shape, f32),
        in_specs=[pl.BlockSpec(memory_space=pltpu.SMEM)] + [pl.BlockSpec(memory_space=pltpu.VMEM)] * 3,
        scratch_shapes=[pltpu.VMEM((length + cap, LANES), f32)] * 2,
        compiler_params=pltpu.CompilerParams(vmem_limit_bytes=16 << 20),
        name=name,
    )(counts, incoming, current, weights)


def copy_kernel(source, target):
    target[...] = source[...]


def copied(value):
    rows, n = value.shape
    block = pl.BlockSpec((rows // 4, n), lambda s: (s, 0))
    return pl.pallas_call(
        copy_kernel,
        grid=(4,),
        out_shape=pltpu.HBM(value.shape, value.dtype),
        in_specs=[block],
        out_specs=block,
        cost_estimate=pl.CostEstimate(flops=0, bytes_accessed=4_000_000, transcendentals=0),
        name="copied",
    )(in_hbm(value))


def model_rows_kernel(counts, listing, returned, high, low, out, compact, grid, halves_high, halves_low):
    s = pl.program_id(0)
    owners, cap, _ = returned.shape
    rows = halves_high.shape[1]

    @pl.when(s == 0)
    def _():
        offset = 0
        for o in range(owners):
            compact[pl.ds(offset, cap), :] = returned[o]
            offset = offset + counts[o]
        full = offset == grid.shape[0]
        total = jnp.where(full, 0, offset)

        @pl.when(full)
        def _():
            for q in range(RADIX):
                grid[q * rows : (q + 1) * rows, :] = compact[pl.ds(q, rows, stride=RADIX), :]

        @pl.when(jnp.logical_not(full))
        def _():
            grid[...] = jnp.zeros_like(grid)

        @pl.loop(0, lax.div(total, 8))
        def _(step):
            for index in range(8):
                at = step * 8 + index
                grid[pl.ds(listing[at], 1), :] = compact[pl.ds(at, 1), :]

        @pl.loop(lax.div(total, 8) * 8, total)
        def _(at):
            grid[pl.ds(listing[at], 1), :] = compact[pl.ds(at, 1), :]

        half = RADIX // 2
        for q in range(half):
            first = grid[q * rows : (q + 1) * rows, :]
            second = grid[(q + half) * rows : (q + half + 1) * rows, :]
            for index, combined in enumerate((first + second, first - second)):
                top, rest = split(combined)
                halves_high[index, :, q * LANES : (q + 1) * LANES] = top
                halves_low[index, :, q * LANES : (q + 1) * LANES] = rest

    side = s // (pl.num_programs(0) // 2)
    result = dot3((halves_high[side], halves_low[side]), (high[0], low[0]))
    half = rows // 2
    parts = quad_transpose(
        [result[:half, :LANES], result[:half, LANES:], result[half:, :LANES], result[half:, LANES:]]
    )
    for index in range(4):
        out[index] = parts[index]


def model_rows(counts, listing, returned, tables, rows, n, devices):
    owners, cap, _ = returned.shape
    block_count = listing.shape[0]
    smem = pl.BlockSpec(memory_space=pltpu.SMEM)
    table = pl.BlockSpec((1, n // 2, 2 * LANES), lambda s: (s, 0, 0))
    return pl.pallas_call(
        model_rows_kernel,
        grid=(devices // 4,),
        out_shape=pltpu.HBM((devices, rows // 2, LANES), f32),
        in_specs=[
            smem,
            smem,
            pl.BlockSpec((owners, cap, LANES), lambda s: (0, 0, 0)),
            table,
            table,
        ],
        out_specs=pl.BlockSpec((4, rows // 2, LANES), lambda s: (s, 0, 0)),
        scratch_shapes=[
            pltpu.VMEM((block_count + cap, LANES), f32),
            pltpu.VMEM((block_count, LANES), f32),
            pltpu.VMEM((2, rows, n // 2), bf16),
            pltpu.VMEM((2, rows, n // 2), bf16),
        ],
        compiler_params=pltpu.CompilerParams(vmem_limit_bytes=16 << 20),
        name="model_rows",
    )(counts, listing, returned, *tables)


def in_hbm(value):
    return pltpu.with_memory_space_constraint(value, pltpu.HBM)


def swap_all(value, axes):
    return lax.all_to_all(value, axes, split_axis=0, concat_axis=0, tiled=True)


def local_paired(misfit, kernel_spec, model_vec, weight_vec, active_list, send_counts):
    both = ("pen", "dep")
    pen_count = lax.axis_size("pen")
    devices = pen_count * lax.axis_size("dep")
    channels, rows, n = misfit.shape
    band = n // pen_count
    forward_np, inverse_np = row_tables(n, devices)
    row_forward = tuple(map(jnp.asarray, forward_np))
    row_inverse = jnp.asarray(np.stack(inverse_np, axis=2))
    forward_np, inverse_np = column_tables()
    col_forward = jnp.asarray(np.stack(forward_np, axis=1))
    col_inverse = jnp.asarray(np.stack(inverse_np, axis=1))
    me = lax.axis_index(both)
    half = devices // 2
    flags = jnp.stack([(me >= half).astype(jnp.int32), (me == 0).astype(jnp.int32)])
    counts = send_counts.reshape(pen_count)
    listing = active_list.reshape(-1)
    places = (listing & (RADIX - 1)) * band + (listing >> 4)
    owner_length = model_vec.shape[2]
    cap = owner_length // pen_count

    spec = kernel_spec.reshape((-1,) + kernel_spec.shape[2:])
    partner = [(d, devices - 1 - d) for d in range(devices)]
    got_b = lax.ppermute(part_spec(flags, spec, 8, 12), both, partner)
    sent_a = part_spec(flags, spec, 0, 8)
    got_a = lax.ppermute(sent_a, both, partner)
    edge = lax.ppermute(
        spec[:, 0:1, :].astype(f32), both, [(d, (devices - d) % half) for d in range(half, devices)]
    )
    source_counts = swap_all(counts, "pen")

    misfit, _ = lax.optimization_barrier((misfit, sent_a))
    chunk_a, chunk_b = misfit_rows(misfit, row_forward, devices)
    chunk_a, got_b, edge, source_counts = lax.optimization_barrier((chunk_a, got_b, edge, source_counts))
    chunk_b, got_a, got_b, edge = lax.optimization_barrier((chunk_b, got_a, got_b, edge))
    columns_a = swap_all(chunk_a, both).reshape(n, 2 * LANES)
    columns_b = swap_all(chunk_b, both).reshape(n, LANES)
    pairs = pair_spec(flags, spec, got_a, got_b, edge)
    sums, edges = adjoint_columns_a(flags, columns_a, pairs, col_forward)
    fields = adjoint_columns_b(flags, columns_b, edges, sums, pairs, col_forward, col_inverse)
    gradient, outgoing = gradient_rows(
        counts, places, swap_all(fields, both), row_inverse, band, n, cap
    )
    outgoing, gradient = lax.optimization_barrier((outgoing, gradient))
    incoming = swap_all(outgoing, "pen")
    gradient, source_counts = lax.optimization_barrier((copied(gradient), source_counts))
    owned = (
        source_counts,
        incoming,
        model_vec.reshape(owner_length, LANES),
        weight_vec.reshape(owner_length, LANES),
    )
    updated = owner_call(owner_send_kernel, "owner_send", incoming.shape, *owned)
    updated, incoming = lax.optimization_barrier((updated, incoming))
    returned = swap_all(updated, "pen")
    model_chunks = model_rows(counts, places, returned, row_forward, band, n, devices)
    model_chunks, incoming = lax.optimization_barrier((model_chunks, incoming))
    moved = swap_all(model_chunks, both)
    model_new = owner_call(
        owner_keep_kernel, "owner_keep", (owner_length, LANES), owned[0], incoming, *owned[2:]
    )
    model_new, flags = lax.optimization_barrier((model_new, flags))
    out_b, edges, model = forward_columns_b(
        flags, moved, pairs, col_forward, col_inverse, n
    )
    back_b = swap_all(out_b.reshape(devices, rows, LANES), both)
    out_a = forward_columns_a(flags, model, edges, pairs, col_inverse)
    back_a = swap_all(out_a.reshape(devices, rows, 2 * LANES), both)
    predicted = predicted_rows(back_b, row_inverse, None, n)
    predicted = predicted_rows(back_a, row_inverse, predicted, n)
    return (gradient[None], model_new.reshape(model_vec.shape), predicted)


def local(misfit, kernel_spec, model_vec, weight_vec, active_list, send_counts):
    sizes = tuple(lax.axis_size(name) for name in ("pen", "dep", "chan"))
    if sizes == (16, 2, 1) and misfit.shape == (6, 64, RADIX * LANES) and kernel_spec.shape[1] == 2:
        plan = local_paired
    else:
        plan = local_general
    return plan(misfit, kernel_spec, model_vec, weight_vec, active_list, send_counts)


def solution(mesh):
    return jax.shard_map(
        local,
        mesh=mesh,
        in_specs=(
            P(("grp", "chan"), ("pen", "dep"), None),
            P("chan", None, ("pen", "dep"), None),
            P(("grp", "dep", "chan"), "pen", None, None),
            P(("grp", "dep", "chan"), "pen", None, None),
            P(("grp", "dep", "chan"), "pen", None),
            P(("grp", "dep", "chan"), "pen", None),
        ),
        out_specs=(
            P(("grp", "dep", "chan"), "pen", None),
            P(("grp", "dep", "chan"), "pen", None, None),
            P(("grp", "chan"), ("pen", "dep"), None),
        ),
        check_vma=False,
    )
```

```python
import functools
import math

import jax
import jax.numpy as jnp
import ml_dtypes
import numpy as np
from jax import lax
from jax.experimental import pallas as pl
from jax.experimental.pallas import tpu as pltpu
from jax.sharding import PartitionSpec as P

inner_radix = 128
step_size = 0.5
highest = lax.Precision.HIGHEST
letters_free = "cdefghij"


def unit_table(length, direction):
    indices = jnp.arange(length, dtype=jnp.int32)
    phases = indices[:, None] * indices[None, :] % length
    angles = 2.0 * math.pi / length * phases.astype(jnp.float32)
    return (jnp.cos(angles), direction * jnp.sin(angles))


def twiddle_table(outer_size, inner_size, direction):
    length = outer_size * inner_size
    phases = (
        jnp.arange(outer_size, dtype=jnp.int32)[:, None]
        * jnp.arange(inner_size, dtype=jnp.int32)[None, :]
        % length
    )
    angles = 2.0 * math.pi / length * phases.astype(jnp.float32)
    return (jnp.cos(angles), direction * jnp.sin(angles))


def contract(formula, operand, tables, real_only):
    product_one = jnp.einsum(formula, operand[0], tables[0], precision=highest)
    if operand[1] is None:
        return (product_one, jnp.einsum(formula, operand[0], tables[1], precision=highest))
    real_value = product_one - jnp.einsum(formula, operand[1], tables[1], precision=highest)
    if real_only:
        return (real_value, None)
    imag_value = jnp.einsum(formula, operand[0], tables[1], precision=highest) + jnp.einsum(
        formula, operand[1], tables[0], precision=highest
    )
    return (real_value, imag_value)


def transform(operand, dimension, direction, real_only):
    full_shape = operand[0].shape
    length = full_shape[dimension]
    inner_size = min(inner_radix, length)
    outer_size = length // inner_size
    split_shape = full_shape[:dimension] + (outer_size, inner_size) + full_shape[dimension + 1 :]
    leading = letters_free[:dimension]
    trailing = letters_free[dimension : len(full_shape) - 1]
    pieces = tuple((None if member is None else member.reshape(split_shape) for member in operand))
    sectioned = contract(
        leading + "ab" + trailing + ",ak->" + leading + "kb" + trailing,
        pieces,
        unit_table(outer_size, direction),
        False,
    )
    twist_real, twist_imag = twiddle_table(outer_size, inner_size, direction)
    twist_shape = (outer_size, inner_size) + (1,) * len(trailing)
    twist_real = twist_real.reshape(twist_shape)
    twist_imag = twist_imag.reshape(twist_shape)
    rotated = (
        sectioned[0] * twist_real - sectioned[1] * twist_imag,
        sectioned[0] * twist_imag + sectioned[1] * twist_real,
    )
    factor = 1.0 / length if direction > 0 else 1.0
    if len(trailing) == 0:
        result = contract(
            leading + "kb,bm->" + leading + "km",
            rotated,
            unit_table(inner_size, direction),
            real_only,
        )
        return tuple(
            (
                (
                    None
                    if member is None
                    else jnp.swapaxes(member, -1, -2).reshape(full_shape) * factor
                )
                for member in result
            )
        )
    result = contract(
        leading + "kb" + trailing + ",bm->" + leading + "mk" + trailing,
        rotated,
        unit_table(inner_size, direction),
        real_only,
    )
    return tuple(
        (None if member is None else member.reshape(full_shape) * factor for member in result)
    )


def exclusive_sum(counts):
    places = jnp.arange(counts.shape[0], dtype=jnp.int32)
    return jnp.sum(jnp.where(places[None, :] < places[:, None], counts[None, :], 0), axis=1)


def imag_channels(chan_place, chan_width):
    channel_ids = chan_place * chan_width + jnp.arange(chan_width, dtype=jnp.int32)
    return ((channel_ids == 2) | (channel_ids == 4))[:, None, None]


def channel_weighted(kernel_view, along):
    total = None
    for channel in range(kernel_view.shape[0]):
        kernel_now = kernel_view[channel].astype(jnp.float32)
        term = kernel_now * along[channel][None, None]
        total = term if total is None else total + term
    return total.reshape(-1, along.shape[1], along.shape[2])


def layer_weighted(kernel_view, grouped):
    ordered = jnp.swapaxes(grouped, 0, 1)
    outputs = []
    for channel in range(kernel_view.shape[0]):
        products = kernel_view[channel].astype(jnp.float32) * ordered
        outputs.append(jnp.sum(products, axis=(0, 1)))
    return jnp.stack(outputs)


def local_general(misfit, kernel_spec, model_vec, weight_vec, active_list, send_counts):
    pen_count = lax.axis_size("pen")
    dep_count = lax.axis_size("dep")
    chan_count = lax.axis_size("chan")
    chan_width, band_width, grid_width = misfit.shape
    column_width = kernel_spec.shape[2]
    kernel_view = kernel_spec.reshape(chan_width, dep_count, chan_count, column_width, grid_width)
    turned = imag_channels(lax.axis_index("chan"), chan_width)
    spectra_real, spectra_imag = transform((misfit, None), 2, -1.0, False)
    columns = (
        lax.all_to_all(spectra_real, ("pen", "dep"), split_axis=2, concat_axis=1, tiled=True),
        lax.all_to_all(spectra_imag, ("pen", "dep"), split_axis=2, concat_axis=1, tiled=True),
    )
    columns = (jnp.swapaxes(columns[0], 1, 2), jnp.swapaxes(columns[1], 1, 2))
    misfit_hat = transform(columns, 2, -1.0, False)
    along_real = jnp.where(turned, misfit_hat[1], misfit_hat[0])
    along_imag = jnp.where(turned, -misfit_hat[0], misfit_hat[1])
    partial_real = channel_weighted(kernel_view, along_real)
    partial_imag = channel_weighted(kernel_view, along_imag)
    fields = transform((partial_real, partial_imag), 2, 1.0, False)
    outgoing = tuple(
        (
            member.reshape(dep_count, chan_count, column_width, pen_count, -1)
            .transpose(3, 0, 1, 4, 2)
            .reshape(pen_count * dep_count, chan_count, -1, column_width)
            for member in fields
        )
    )
    arrived = (
        lax.all_to_all(outgoing[0], ("pen", "dep"), split_axis=0, concat_axis=3, tiled=True),
        lax.all_to_all(outgoing[1], ("pen", "dep"), split_axis=0, concat_axis=3, tiled=True),
    )
    real_fields = transform(arrived, 3, 1.0, True)[0]
    gradient = lax.psum_scatter(real_fields, "chan", scatter_dimension=1, tiled=True).reshape(
        1, -1, grid_width
    )
    blocks = gradient.reshape(-1, 128)
    block_count = blocks.shape[0]
    owner_length = model_vec.shape[2]
    slot_cap = owner_length // pen_count
    counts = send_counts.reshape(pen_count)
    starts = exclusive_sum(counts)
    slot_index = jnp.arange(slot_cap, dtype=jnp.int32)
    slot_valid = slot_index[None, :] < counts[:, None]
    in_list = jnp.minimum(starts[:, None] + slot_index[None, :], block_count - 1)
    listing = active_list.reshape(block_count)
    block_ids = listing[in_list]
    outgoing_blocks = jnp.where(slot_valid[:, :, None], blocks[block_ids], 0.0)
    incoming, arrived_counts = (
        lax.all_to_all(outgoing_blocks, "pen", split_axis=0, concat_axis=0, tiled=True),
        lax.all_to_all(counts.astype(jnp.float32), "pen", split_axis=0, concat_axis=0, tiled=True),
    )
    source_counts = arrived_counts.astype(jnp.int32)
    begins = exclusive_sum(source_counts)
    filled = slot_index[None, :] < source_counts[:, None]
    places = begins[:, None] + slot_index[None, :]
    safe_places = jnp.minimum(places, owner_length - 1)
    current = model_vec.reshape(owner_length, 128)
    scales = weight_vec.reshape(owner_length, 128)
    updated = jnp.clip(
        current[safe_places] - step_size * scales[safe_places].astype(jnp.float32) * incoming,
        -1.0,
        1.0,
    )
    targets = jnp.where(filled, places, owner_length)
    model_new = current.at[targets].set(updated, mode="drop").reshape(model_vec.shape)
    returned = lax.all_to_all(updated, "pen", split_axis=0, concat_axis=0, tiled=True)
    drop_ids = jnp.where(slot_valid, block_ids, block_count)
    model_grid = jnp.zeros((block_count, 128), jnp.float32).at[drop_ids].set(returned, mode="drop")
    model_grid = model_grid.reshape(-1, grid_width)
    surface_field = transform((model_grid, None), 1, -1.0, False)
    moved_columns = (
        lax.all_to_all(surface_field[0], ("pen", "dep"), split_axis=1, concat_axis=0, tiled=True),
        lax.all_to_all(surface_field[1], ("pen", "dep"), split_axis=1, concat_axis=0, tiled=True),
    )
    ordered = tuple(
        (
            member.reshape(pen_count, dep_count, -1, column_width)
            .transpose(1, 3, 0, 2)
            .reshape(dep_count, column_width, grid_width)
            for member in moved_columns
        )
    )
    model_hat = transform(ordered, 2, -1.0, False)
    layers_all = (
        lax.all_gather(model_hat[0], "chan", axis=0, tiled=True),
        lax.all_gather(model_hat[1], "chan", axis=0, tiled=True),
    )
    grouped = tuple(
        (member.reshape(chan_count, dep_count, column_width, grid_width) for member in layers_all)
    )
    summed_real = layer_weighted(kernel_view, grouped[0])
    summed_imag = layer_weighted(kernel_view, grouped[1])
    data_real = jnp.where(turned, -summed_imag, summed_real)
    data_imag = jnp.where(turned, summed_real, summed_imag)
    surface_rows = transform((data_real, data_imag), 2, 1.0, False)
    rows_back = (
        lax.all_to_all(surface_rows[0], ("pen", "dep"), split_axis=2, concat_axis=1, tiled=True),
        lax.all_to_all(surface_rows[1], ("pen", "dep"), split_axis=2, concat_axis=1, tiled=True),
    )
    predicted = jnp.swapaxes(transform(rows_back, 1, 1.0, True)[0], 1, 2)
    return (gradient, model_new, predicted)


RADIX = 16
UNROLL = 4
LANES = 128
TILES = (((0, 0), (1, 32), (2, 64), (3, 96)), ((4, 0), (5, 64)))
EDGES = ((4, 32), (0, 33), (1, 34), (5, 96), (2, 97), (3, 98))
f32 = jnp.float32
bf16 = jnp.bfloat16


def two_terms(table):
    high = table.astype(ml_dtypes.bfloat16)
    low = (table - high.astype(np.float64)).astype(ml_dtypes.bfloat16)
    return (high, low)


def row_frequencies(n, devices, width):
    device = np.arange(devices)[:, None]
    column = np.arange(width // 2)[None, :]
    return width * device + 2 * column + (device >= devices // 2)


@functools.cache
def row_tables(n, devices):
    width = n // devices
    freq = row_frequencies(n, devices, width).reshape(devices // 4, 1, LANES)
    y = np.arange(n // 2)[None, :, None]
    angle = 2.0 * math.pi / n * (freq * y % n)
    real, imag = np.cos(angle), -np.sin(angle)
    imag[0, :, 0] = 1.0 - 2.0 * (np.arange(n // 2) % 2)
    forward = np.concatenate([real, imag], axis=2)
    inverse = 2.0 * forward
    inverse[0, :, 0] *= 0.5
    inverse[0, :, LANES] *= 0.5
    inverse = inverse.swapaxes(1, 2).reshape(2, n // 2, 4, n // 8).transpose(2, 0, 1, 3) / float(n) ** 2
    return (two_terms(forward), two_terms(inverse))


@functools.cache
def column_tables():
    k = np.arange(RADIX)[:, None, None]
    m = np.arange(LANES)[None, :, None]
    b = np.arange(LANES)[None, None, :]
    n = RADIX * LANES
    angle = 2.0 * math.pi / n * ((16 * b * m + b * k) % n)
    real, sine = np.cos(angle), np.sin(angle)
    forward = np.concatenate(
        [np.concatenate([real, sine], axis=2), np.concatenate([-sine, real], axis=2)], axis=1
    )
    return (two_terms(forward), two_terms(forward.swapaxes(1, 2)))


@functools.cache
def lane_tables():
    edges = [lane for _, lane in EDGES]
    fold = np.zeros((2, LANES, LANES))
    spread = np.zeros((LANES, 2, LANES))
    for layer in range(2):
        for _, lane in TILES[1]:
            for i in range(32):
                fold[layer, lane + i, 64 * layer + i] = 1.0
                spread[64 * layer + i, layer, lane + i] = 1.0
        fold[layer, edges, 64 * layer + 32] = 1.0
        spread[64 * layer + 32, layer, edges] = 1.0
    fold = np.concatenate([fold[0], fold[0], fold[1], fold[1]])
    spread = np.tile(spread.reshape(LANES, 2 * LANES), (2, 1))
    return (fold.astype(ml_dtypes.bfloat16), spread.astype(ml_dtypes.bfloat16))


def split(value):
    high = value.astype(bf16)
    return high, (value - high.astype(f32)).astype(bf16)


def dot(a, b):
    return jnp.dot(a, b, preferred_element_type=f32)


def dot3(left, right):
    return dot(left[0], right[0]) + (dot(left[0], right[1]) + dot(left[1], right[0]))


def turn(value, shift):
    shift %= LANES
    return value if shift == 0 else pltpu.roll(value, shift, value.ndim - 1)


def lane_of(shape):
    return lax.broadcasted_iota(jnp.int32, shape, len(shape) - 1)


def quad_transpose(parts):
    lane = lane_of(parts[0].shape)
    low, even = lane < 64, lane % 64 < 32
    a, b, c, d = parts
    a, c = jnp.where(low, a, turn(c, 64)), jnp.where(low, turn(a, 64), c)
    b, d = jnp.where(low, b, turn(d, 64)), jnp.where(low, turn(b, 64), d)
    a, b = jnp.where(even, a, turn(b, 32)), jnp.where(even, turn(a, 96), b)
    c, d = jnp.where(even, c, turn(d, 32)), jnp.where(even, turn(c, 96), d)
    return [a, b, c, d]


def radix4(x, sign):
    (r0, i0), (r1, i1), (r2, i2), (r3, i3) = x
    ar, ai, br, bi = r0 + r2, i0 + i2, r0 - r2, i0 - i2
    cr, ci, dr, di = r1 + r3, i1 + i3, r1 - r3, i1 - i3
    if sign < 0:
        turned = (di, -dr)
    else:
        turned = (-di, dr)
    return [
        (ar + cr, ai + ci),
        (br + turned[0], bi + turned[1]),
        (ar - cr, ai - ci),
        (br - turned[0], bi - turned[1]),
    ]


def radix16(x, sign):
    inner = [radix4([x[4 * a1 + a0] for a1 in range(4)], sign) for a0 in range(4)]
    outputs = [None] * RADIX
    for k0 in range(4):
        column = []
        for a0 in range(4):
            re, im = inner[a0][k0]
            power = a0 * k0 % RADIX
            if power == 4:
                re, im = (im, -re) if sign < 0 else (-im, re)
            elif power == 2 or power == 6:
                scale = math.sqrt(0.5)
                c = scale if power == 2 else -scale
                if sign < 0:
                    re, im = re * c + im * scale, im * c - re * scale
                else:
                    re, im = re * c - im * scale, im * c + re * scale
            elif power != 0:
                c = math.cos(2.0 * math.pi * power / RADIX)
                s = sign * math.sin(2.0 * math.pi * power / RADIX)
                re, im = re * c - im * s, re * s + im * c
            column.append((re, im))
        for k1, value in enumerate(radix4(column, sign)):
            outputs[4 * k1 + k0] = value
    return outputs


def forward_blocks(load, work, begin=0, rows=LANES):
    @pl.loop(0, rows // 8, unroll=UNROLL)
    def _(step):
        row = pl.multiple_of(step * 8, 8)
        outputs = radix16([load(a, row) for a in range(RADIX)], -1)
        for k, (re, im) in enumerate(outputs):
            work[k, pl.ds(begin + row, 8), :] = re
            work[k, pl.ds(begin + row + LANES, 8), :] = im


def inverse_blocks(work, store):
    @pl.loop(0, LANES // 8, unroll=UNROLL)
    def _(step):
        first = pl.multiple_of(step * 8, 8)
        inputs = [
            (work[k, pl.ds(first, 8), :], work[k, pl.ds(first + LANES, 8), :]) for k in range(RADIX)
        ]
        for a, (re, im) in enumerate(radix16(inputs, 1)):
            store(a, first, re, im)


def column_product(tables, value):
    high, low = split(value)
    wide = dot(tables[0], jnp.concatenate([high, low], axis=1))
    return wide[:, :LANES] + wide[:, LANES:] + dot(tables[1], high)


def choose_rows(wanted, value):
    columns = lax.broadcasted_iota(jnp.int32, (wanted.shape[0], value.shape[0]), 1)
    return dot((columns == wanted).astype(f32).astype(bf16), value)


def part_kernel(flags, spec, sent):
    half = sent.shape[1]
    wanted = 2 * (half - 1 - lax.broadcasted_iota(jnp.int32, (half, 2 * half), 0)) + 1 - flags[0]
    for line in range(sent.shape[0]):
        sent[line] = choose_rows(wanted, spec[line])


def part_spec(flags, spec, begin, end):
    count, width, n = spec.shape
    half = width // 2
    step = 2
    return pl.pallas_call(
        part_kernel,
        grid=((end - begin) // step,),
        out_shape=pltpu.HBM((end - begin, half, n), f32),
        in_specs=[
            pl.BlockSpec(memory_space=pltpu.SMEM),
            pl.BlockSpec((step, width, n), lambda s: (s + begin // step, 0, 0)),
        ],
        out_specs=pl.BlockSpec((step, half, n), lambda s: (s, 0, 0)),
        name="part_spec",
    )(flags, in_hbm(spec))


def pair_kernel(flags, spec, got_a, got_b, edge, pairs, own, mirror, room, own_t, mirror_t):
    step = pl.program_id(0)
    layer = lax.rem(step, 2)
    upper, first = flags[0], flags[1]
    half = got_a.shape[1]
    n = spec.shape[2]
    wanted = 2 * lax.broadcasted_iota(jnp.int32, (half, 2 * half), 0) + upper

    def weight(channel):
        return -0.5 if channel in (2, 4) else 0.5

    for tile in range(2):

        @pl.when(lax.div(step, 2) == tile)
        def _():
            if tile == 1:
                own[...] = jnp.zeros_like(own)
                mirror[...] = jnp.zeros_like(mirror)
                for channel, lane in EDGES:
                    row = edge[2 * channel + layer]
                    own[lane : lane + 1, :] = row * 0.5
                    mirror[lane : lane + 1, :] = row * weight(channel)
            for channel, lane in TILES[tile]:
                line = 2 * channel + layer
                kept = choose_rows(wanted, spec[line])
                own[lane : lane + half, :] = kept * 0.5
                room[0:1, :] = jnp.where(first == 1, kept[0:1, :], edge[line])
                room[1 : 1 + half, :] = got_a[line] if tile == 0 else got_b[line - 8]
                mirror[lane : lane + half, :] = (
                    jnp.where(upper == 1, room[1 : 1 + half, :], room[0:half, :]) * weight(channel)
                )

    for block in range(n // LANES):
        here = slice(block * LANES, (block + 1) * LANES)
        own_t[here, :] = jnp.transpose(own[:, here])
        mirror_t[here, :] = jnp.transpose(mirror[:, here])
    row = lax.broadcasted_iota(jnp.int32, (LANES, LANES), 0)
    for k in range(RADIX):
        wanted_k = LANES - 1 - row if k > 0 else (LANES - row) & (LANES - 1)
        other = mirror_t[pl.ds((RADIX - k) % RADIX, LANES, stride=RADIX), :]
        pairs[0, k * LANES : (k + 1) * LANES, :] = own_t[
            pl.ds(k, LANES, stride=RADIX), :
        ] + choose_rows(wanted_k, other.astype(bf16))


def pair_spec(flags, spec, got_a, got_b, edge):
    count, width, n = spec.shape
    single = pl.Buffered(1)
    return pl.pallas_call(
        pair_kernel,
        grid=(4,),
        out_shape=pltpu.HBM((4, n, LANES), f32),
        in_specs=[
            pl.BlockSpec(memory_space=pltpu.SMEM),
            pl.BlockSpec((count, width, n), lambda s: (0, 0, 0), pipeline_mode=single),
            pl.BlockSpec(got_a.shape, lambda s: (0, 0, 0), pipeline_mode=single),
            pl.BlockSpec(got_b.shape, lambda s: (0, 0, 0), pipeline_mode=single),
            pl.BlockSpec((count, 1, n), lambda s: (0, 0, 0)),
        ],
        out_specs=pl.BlockSpec((1, n, LANES), lambda s: (s, 0, 0)),
        scratch_shapes=[
            pltpu.VMEM((LANES, n), f32),
            pltpu.VMEM((LANES, n), f32),
            pltpu.VMEM((40, n), f32),
            pltpu.VMEM((n, LANES), f32),
            pltpu.VMEM((n, LANES), f32),
        ],
        compiler_params=pltpu.CompilerParams(vmem_limit_bytes=24 << 20),
        cost_estimate=pl.CostEstimate(flops=0, bytes_accessed=60_000_000, transcendentals=0),
        name="pair_spec",
    )(flags, in_hbm(spec), in_hbm(got_a), in_hbm(got_b), edge)


def misfit_rows_kernel(misfit, high, low, out_a, out_b, halves_high, halves_low):
    s = pl.program_id(0)
    channels, rows, n = misfit.shape

    @pl.when(s == 0)
    def _():
        value = misfit[...].reshape(channels * rows, n)
        first, second = value[:, : n // 2], value[:, n // 2 :]
        for index, combined in enumerate((first + second, first - second)):
            halves_high[index], halves_low[index] = split(combined)

    side = s // (pl.num_programs(0) // 2)
    result = dot3((halves_high[side], halves_low[side]), (high[0], low[0]))
    real = [result[rows * c : rows * (c + 1), :LANES] for c in range(channels)]
    imag = [result[rows * c : rows * (c + 1), LANES:] for c in range(channels)]
    parts = (quad_transpose(real[:4]), quad_transpose(imag[:4]))
    for index in range(4):
        out_a[index, :, :LANES] = parts[0][index]
        out_a[index, :, LANES:] = parts[1][index]
    for index, value in enumerate(quad_transpose([real[4], imag[4], real[5], imag[5]])):
        out_b[index] = value


def misfit_rows(misfit, tables, devices):
    channels, rows, n = misfit.shape
    table = pl.BlockSpec((1, n // 2, 2 * LANES), lambda s: (s, 0, 0))
    return pl.pallas_call(
        misfit_rows_kernel,
        grid=(devices // 4,),
        out_shape=[
            jax.ShapeDtypeStruct((devices, rows, 2 * LANES), f32),
            jax.ShapeDtypeStruct((devices, rows, LANES), f32),
        ],
        in_specs=[pl.BlockSpec((channels, rows, n), lambda s: (0, 0, 0)), table, table],
        out_specs=[
            pl.BlockSpec((4, rows, 2 * LANES), lambda s: (s, 0, 0)),
            pl.BlockSpec((4, rows, LANES), lambda s: (s, 0, 0)),
        ],
        scratch_shapes=[pltpu.VMEM((2, channels * rows, n // 2), bf16)] * 2,
        compiler_params=pltpu.CompilerParams(vmem_limit_bytes=22 << 20),
        name="misfit_rows",
    )(misfit, *tables)


TILES_Y = 4


def gather_columns(pieces, fetched, lhs_high, lhs_low):
    spectra, here, arrived, table, held, ready = fetched
    quads = spectra.shape[0] // 4
    copies = [
        pltpu.make_async_copy(
            spectra.at[pl.ds(4 * quad, 4)], here.at[pl.ds(4 * quad, 4)], arrived.at[quad]
        )
        for quad in range(quads)
    ]
    for copy in copies:
        copy.start()
    for step in range(TILES_Y):
        pltpu.make_async_copy(table.at[step], held.at[step], ready.at[step]).start()
    for quad in range(quads):
        copies[quad].wait()
        side, place = divmod(quad, quads // 2)
        at = slice(place * 2 * LANES, (place + 1) * 2 * LANES)
        lhs_high[side, :, at], lhs_low[side, :, at] = split(pieces(quad))


def half_rows(lhs_high, lhs_low, fetched):
    s = pl.program_id(0)
    _, _, _, table, held, ready = fetched
    pltpu.make_async_copy(table.at[s], held.at[s], ready.at[s]).wait()
    even, odd = (dot3((lhs_high[side], lhs_low[side]), (held[s, side, 0], held[s, side, 1])) for side in range(2))
    return even + odd, even - odd


def row_scratch(spectra, rows, n):
    return [
        pltpu.VMEM(spectra.shape, f32),
        pltpu.SemaphoreType.DMA((spectra.shape[0] // 4,)),
        pltpu.VMEM((TILES_Y, 2, 2, n // 2, n // 2 // TILES_Y), bf16),
        pltpu.SemaphoreType.DMA((TILES_Y,)),
        pltpu.VMEM((2, rows, n // 2), bf16),
        pltpu.VMEM((2, rows, n // 2), bf16),
    ]


def predicted_kernel(begin, count, spectra, table, *refs):
    out, here, arrived, held_table, ready, lhs_high, lhs_low, held, left = refs[-9:]
    fetched = (spectra, here, arrived, table, held_table, ready)
    s = pl.program_id(0)
    rows, n = out.shape[1:]
    width = n // 2 // TILES_Y

    def pieces(quad):
        if count == 2:
            c4r, c4i, c5r, c5i = quad_transpose([here[4 * quad + index] for index in range(4)])
            real, imag = (c4r, c5r), (c4i, c5i)
        else:
            real = quad_transpose([here[4 * quad + index, :, :LANES] for index in range(4)])
            imag = quad_transpose([here[4 * quad + index, :, LANES:] for index in range(4)])
        return jnp.concatenate([jnp.concatenate(pair, axis=1) for pair in zip(real, imag)], axis=0)

    def leave(step, side):
        place = (pl.ds(begin, count), slice(None), pl.ds(side * (n // 2) + step * width, width))
        return pltpu.make_async_copy(held.at[2 * step + side], out.at[place], left.at[2 * step + side])

    @pl.when(s == 0)
    def _():
        gather_columns(pieces, fetched, lhs_high, lhs_low)

    halves = half_rows(lhs_high, lhs_low, fetched)
    for step in range(TILES_Y):

        @pl.when(s == step)
        def _():
            for side in range(2):
                held[2 * step + side] = halves[side].reshape(count, rows, width)
                leave(step, side).start()

    @pl.when(s == TILES_Y - 1)
    def _():
        for step in range(TILES_Y):
            for side in range(2):
                leave(step, side).wait()


def predicted_rows(spectra, table, before, n):
    devices, rows, lanes = spectra.shape
    hbm = pl.BlockSpec(memory_space=pltpu.HBM)
    begin, count = (4, 2) if before is None else (0, 4)
    return pl.pallas_call(
        functools.partial(predicted_kernel, begin, count),
        grid=(TILES_Y,),
        out_shape=pltpu.HBM((6, rows, n), f32),
        in_specs=[pl.BlockSpec(memory_space=pl.ANY)] + [hbm] * (1 if before is None else 2),
        out_specs=hbm,
        scratch_shapes=row_scratch(spectra, count * rows, n)
        + [
            pltpu.VMEM((2 * TILES_Y, count, rows, n // 2 // TILES_Y), f32),
            pltpu.SemaphoreType.DMA((2 * TILES_Y,)),
        ],
        input_output_aliases={} if before is None else {2: 0},
        compiler_params=pltpu.CompilerParams(vmem_limit_bytes=28 << 20),
        name="predicted_rows_b" if before is None else "predicted_rows_a",
    )(spectra, in_hbm(table), *([] if before is None else [before]))


GROUPS = 4


def started(*copies):
    made = [pltpu.make_async_copy(*copy) for copy in copies]
    for copy in made:
        copy.start()
    return made


def group_rows(group):
    size = RADIX // GROUPS * LANES
    return pl.ds(group * size, size)


def group_steps(group):
    return pl.ds(group * (RADIX // GROUPS), RADIX // GROUPS)


def in_group(group):
    return range(group * (RADIX // GROUPS), (group + 1) * (RADIX // GROUPS))


def pair_copies(pairs, tile, held, arrived, group):
    here = group_rows(group)
    return (pairs.at[pl.ds(2 * tile, 2), here], held.at[:, here], arrived.at[group])


def table_copies(table, held, arrived, group):
    here = group_steps(group)
    return (table.at[here], held.at[here], arrived.at[group])


def stacked_product(table, k, value):
    high, low = split(value)
    terms = jnp.concatenate([table[k, 0], table[k, 1]], axis=0)
    wide = dot(terms, jnp.concatenate([high, low], axis=1))
    size = high.shape[0]
    return wide[:size, :LANES] + wide[:size, LANES:] + wide[size:, :LANES]


def table_product(table, k, value):
    return column_product((table[k, 0], table[k, 1]), value)


TABLE = pltpu.VMEM((RADIX, 2, 2 * LANES, 2 * LANES), bf16)
WORK = pltpu.VMEM((RADIX, 2 * LANES, LANES), f32)
SIGNALS = pltpu.SemaphoreType.DMA((GROUPS,))


def pairs_like(n):
    return pltpu.VMEM((2, n, LANES), f32)


def turn_phase(channel_lanes, real, imag, sign):
    if sign < 0:
        return jnp.where(channel_lanes, imag, real), jnp.where(channel_lanes, -real, imag)
    return jnp.where(channel_lanes, -imag, real), jnp.where(channel_lanes, real, imag)


def adjoint_kernel_a(
    flags, spectra, pairs, table, sums, edges, work, here, held_pairs, held_table, got, got_pairs, got_table
):
    first = flags[1] == 1
    read = started((spectra, here, got.at[0]))
    later = [
        started(pair_copies(pairs, 0, held_pairs, got_pairs, g), table_copies(table, held_table, got_table, g))
        for g in range(GROUPS)
    ]
    lane8 = lane_of((8, LANES))
    packed = jnp.logical_and(lane8 % 32 == 0, first)
    read[0].wait()

    def load(a, row):
        real = here[pl.ds(a * LANES + row, 8), :LANES]
        imag = here[pl.ds(a * LANES + row, 8), LANES:]
        edges[pl.ds(a * LANES + row, 8), :] = jnp.where(lane8 % 64 == 33, turn(imag, 33), turn(imag, 2))
        return (real, jnp.where(packed, 0.0, imag))

    forward_blocks(load, work)
    lane = lane_of((LANES, LANES))
    turned = lane // 32 == 2
    for group in range(GROUPS):
        for copy in later[group]:
            copy.wait()
        for k in in_group(group):
            spectrum = table_product(held_table, k, work[k])
            real, imag = turn_phase(turned, spectrum[:LANES], spectrum[LANES:], -1)
            row = slice(k * LANES, (k + 1) * LANES)
            for index, value in enumerate((real, imag)):
                v0, v1 = value * held_pairs[0, row, :], value * held_pairs[1, row, :]
                both = jnp.where(lane < 64, v0, turn(v1, 64)) + jnp.where(lane < 64, turn(v0, 64), v1)
                sums[index, row, :] = both + turn(both, 96)


def adjoint_columns_a(flags, spectra, pairs, table):
    n = spectra.shape[0]
    hbm = pl.BlockSpec(memory_space=pltpu.HBM)
    return pl.pallas_call(
        adjoint_kernel_a,
        out_shape=[
            jax.ShapeDtypeStruct((2, n, LANES), f32),
            jax.ShapeDtypeStruct((n, LANES), f32),
        ],
        in_specs=[pl.BlockSpec(memory_space=pltpu.SMEM), hbm, hbm, hbm],
        scratch_shapes=[
            WORK,
            pltpu.VMEM((n, 2 * LANES), f32),
            pairs_like(n),
            TABLE,
            pltpu.SemaphoreType.DMA((1,)),
            SIGNALS,
            SIGNALS,
        ],
        compiler_params=pltpu.CompilerParams(vmem_limit_bytes=24 << 20),
        cost_estimate=pl.CostEstimate(flops=0, bytes_accessed=20_000_000, transcendentals=0),
        name="adjoint_columns_a",
    )(flags, in_hbm(spectra), in_hbm(pairs), in_hbm(table))


def adjoint_kernel_b(
    flags, spectra, edges, sums, fold, pairs, table, table_i, out,
    work, here, held_pairs, held_table, held_table_i, fields, chunks, got, got_pairs, got_table, got_table_i, left,
):
    first = flags[1] == 1
    read = started((spectra, here, got.at[0]))
    lane8 = lane_of((8, LANES))
    main = lane8 % 64 < 32
    packed = jnp.logical_and(lane8 % 64 == 0, first)
    in_place = lane8 % 64 == 32
    packed_edge = jnp.logical_and(in_place, first)
    moved = (lane8 % 64 == 33) | (lane8 % 64 == 34)
    read[0].wait()
    later = [
        started(
            table_copies(table, held_table, got_table, g),
            pair_copies(pairs, 1, held_pairs, got_pairs, g),
        )
        for g in range(GROUPS)
    ]
    last = [started(table_copies(table_i, held_table_i, got_table_i, g))[0] for g in range(GROUPS)]

    def load(a, row):
        value = here[pl.ds(a * LANES + row, 8), :]
        edge = edges[pl.ds(a * LANES + row, 8), :]
        real = jnp.where(main | in_place, value, jnp.where(moved, edge, 0.0))
        imag = jnp.where(jnp.logical_and(main, jnp.logical_not(packed)), turn(value, 96), 0.0)
        return (real, imag)

    forward_blocks(load, work)
    lane = lane_of((LANES, LANES))
    turned = (lane <= 32) | (lane == 97)
    on_main = lane % 64 < 32
    for group in range(GROUPS):
        for copy in later[group][:2]:
            copy.wait()
        for k in in_group(group):
            work[k] = stacked_product(held_table, k, work[k])
        for k in in_group(group):
            spectrum = work[k]
            row = slice(k * LANES, (k + 1) * LANES)
            parts = []
            for value in turn_phase(turned, spectrum[:LANES], spectrum[LANES:], -1):
                terms = split(value * held_pairs[0, row, :]) + split(value * held_pairs[1, row, :])
                parts.append(jnp.concatenate(terms, axis=1))
            folded = dot(jnp.concatenate(parts, axis=0), fold[...])
            for index in range(2):
                half = slice(index * LANES, (index + 1) * LANES)
                work[k, half] = folded[half] + jnp.where(on_main, sums[index, row, :], 0.0)
    for group in range(GROUPS):
        last[group].wait()
        for k in in_group(group):
            work[k] = stacked_product(held_table_i, k, work[k])

    def store(a, row, real, imag):
        fields[pl.ds(a * LANES + row, 8), :] = jnp.where(main | packed_edge, real, turn(imag, 32))

    inverse_blocks(work, store)
    lane64 = lane_of((64, LANES))
    leaving = []
    for band in range(RADIX):
        upper, lower = (fields[band * LANES + side : band * LANES + side + 64, :] for side in (0, 64))
        chunks[2 * band] = jnp.where(lane64 < 64, upper, turn(lower, 64))
        chunks[2 * band + 1] = jnp.where(lane64 < 64, turn(upper, 64), lower)
        if band % 4 == 3:
            part = pl.ds(2 * (band - 3), 8)
            leaving += started((chunks.at[part], out.at[part], left.at[band // 4]))
    for copy in leaving:
        copy.wait()


def adjoint_columns_b(flags, spectra, edges, sums, pairs, table, table_i):
    n = spectra.shape[0]
    hbm = pl.BlockSpec(memory_space=pltpu.HBM)
    vmem = pl.BlockSpec(memory_space=pltpu.VMEM)
    chunks = (2 * RADIX, 64, LANES)
    return pl.pallas_call(
        adjoint_kernel_b,
        out_shape=pltpu.HBM(chunks, f32),
        in_specs=[pl.BlockSpec(memory_space=pltpu.SMEM), hbm, vmem, vmem, vmem, hbm, hbm, hbm],
        out_specs=hbm,
        scratch_shapes=[
            WORK,
            pltpu.VMEM((n, LANES), f32),
            pairs_like(n),
            TABLE,
            TABLE,
            pltpu.VMEM((n, LANES), f32),
            pltpu.VMEM(chunks, f32),
            pltpu.SemaphoreType.DMA((1,)),
            SIGNALS,
            SIGNALS,
            SIGNALS,
            SIGNALS,
        ],
        compiler_params=pltpu.CompilerParams(vmem_limit_bytes=30 << 20),
        cost_estimate=pl.CostEstimate(flops=0, bytes_accessed=20_000_000, transcendentals=0),
        name="adjoint_columns_b",
    )(flags, in_hbm(spectra), edges, sums, jnp.asarray(lane_tables()[0]), in_hbm(pairs), in_hbm(table), in_hbm(table_i))


def forward_kernel_b(
    flags, moved, spread, pairs, table, table_i, out, edges, model,
    work, here, held_pairs, held_table, held_table_i, chunk, held_model, held_edges,
    got, got_pairs, got_table, got_table_i, left,
):
    first = flags[1] == 1
    read = started((moved, here, got.at[0]))
    read[0].wait()
    later = [
        started(
            table_copies(table, held_table, got_table, g),
            pair_copies(pairs, 1, held_pairs, got_pairs, g),
        )
        for g in range(GROUPS)
    ]
    last = [started(table_copies(table_i, held_table_i, got_table_i, g))[0] for g in range(GROUPS)]
    lane8 = lane_of((8, LANES))
    main = lane8 % 64 < 32
    real_only = jnp.logical_or(jnp.logical_not(main), jnp.logical_and(lane8 % 64 == 0, first))

    for side in range(2):

        def load(band, row):
            value0, value1 = here[2 * band, pl.ds(row, 8), :], here[2 * band + 1, pl.ds(row, 8), :]
            if side == 0:
                value = jnp.where(lane8 < 64, value0, turn(value1, 64))
            else:
                value = jnp.where(lane8 < 64, turn(value0, 64), value1)
            return (value, jnp.where(real_only, 0.0, turn(value, 96)))

        forward_blocks(load, work, 64 * side, 64)
    lane = lane_of((LANES, LANES))
    turned = (lane <= 32) | (lane == 97)
    for group in range(GROUPS):
        for copy in later[group]:
            copy.wait()
        for k in in_group(group):
            held_model[k] = table_product(held_table, k, work[k])
        for k in in_group(group):
            spectrum = held_model[k]
            row = slice(k * LANES, (k + 1) * LANES)
            both = dot(jnp.concatenate(split(spectrum), axis=1), spread[...])
            totals = [
                both[part * LANES : (part + 1) * LANES, :LANES] * held_pairs[0, row, :]
                + both[part * LANES : (part + 1) * LANES, LANES:] * held_pairs[1, row, :]
                for part in range(2)
            ]
            work[k, :LANES], work[k, LANES:] = turn_phase(turned, *totals, 1)
    leaving = started((held_model, model, left.at[1]))
    for group in range(GROUPS):
        last[group].wait()
        for k in in_group(group):
            work[k] = table_product(held_table_i, k, work[k])

    packed = jnp.logical_and(lane8 % 64 == 32, first)

    def store(a, row, real, imag):
        chunk[pl.ds(a * LANES + row, 8), :] = jnp.where(
            jnp.logical_or(main, packed), real, turn(imag, 32)
        )
        held_edges[pl.ds(a * LANES + row, 8), :] = real

    inverse_blocks(work, store)
    leaving += started((chunk, out, left.at[0]), (held_edges, edges, left.at[2]))
    for copy in leaving:
        copy.wait()


def forward_columns_b(flags, moved, pairs, table, table_i, n):
    hbm = pl.BlockSpec(memory_space=pltpu.HBM)
    return pl.pallas_call(
        forward_kernel_b,
        out_shape=[
            pltpu.HBM((n, LANES), f32),
            pltpu.HBM((n, LANES), f32),
            pltpu.HBM((RADIX, 2 * LANES, LANES), f32),
        ],
        in_specs=[
            pl.BlockSpec(memory_space=pltpu.SMEM),
            hbm,
            pl.BlockSpec(memory_space=pltpu.VMEM),
            hbm,
            hbm,
            hbm,
        ],
        out_specs=[hbm, hbm, hbm],
        scratch_shapes=[
            WORK,
            pltpu.VMEM(moved.shape, f32),
            pairs_like(n),
            TABLE,
            TABLE,
            pltpu.VMEM((n, LANES), f32),
            WORK,
            pltpu.VMEM((n, LANES), f32),
            pltpu.SemaphoreType.DMA((1,)),
            SIGNALS,
            SIGNALS,
            SIGNALS,
            pltpu.SemaphoreType.DMA((3,)),
        ],
        compiler_params=pltpu.CompilerParams(vmem_limit_bytes=34 << 20),
        cost_estimate=pl.CostEstimate(flops=0, bytes_accessed=20_000_000, transcendentals=0),
        name="forward_columns_b",
    )(flags, in_hbm(moved), jnp.asarray(lane_tables()[1]), in_hbm(pairs), in_hbm(table), in_hbm(table_i))


def forward_kernel_a(
    flags, model, edges, pairs, table_i, out,
    work, held_model, held_edges, held_pairs, held_table_i, chunk, got, got_pairs, got_table_i, left,
):
    first = flags[1] == 1
    later = [
        started(
            (model.at[group_steps(g)], held_model.at[group_steps(g)], got.at[g]),
            pair_copies(pairs, 0, held_pairs, got_pairs, g),
            table_copies(table_i, held_table_i, got_table_i, g),
        )
        for g in range(GROUPS)
    ]
    edges_read = started((edges, held_edges, left.at[1]))
    lane = lane_of((LANES, LANES))
    turned = lane // 32 == 2

    def spread(value):
        swapped = turn(value, 64)
        both = (jnp.where(lane < 64, value, swapped), jnp.where(lane < 64, swapped, value))
        return [jnp.where(lane % 64 < 32, layer, turn(layer, 32)) for layer in both]

    for group in range(GROUPS):
        for copy in later[group]:
            copy.wait()
        for k in in_group(group):
            row = slice(k * LANES, (k + 1) * LANES)
            totals = []
            for part in range(2):
                layers = spread(held_model[k, part * LANES : (part + 1) * LANES, :])
                totals.append(layers[0] * held_pairs[0, row, :] + layers[1] * held_pairs[1, row, :])
            real, imag = turn_phase(turned, *totals, 1)
            work[k] = table_product(held_table_i, k, jnp.concatenate([real, imag], axis=0))

    lane8 = lane_of((8, LANES))
    packed = jnp.logical_and(lane8 % 32 == 0, first)

    def store(a, row, real, imag):
        edge = held_edges[pl.ds(a * LANES + row, 8), :]
        edge = jnp.where(lane8 % 64 < 32, turn(edge, 95), turn(edge, 126))
        chunk[pl.ds(a * LANES + row, 8), :LANES] = real
        chunk[pl.ds(a * LANES + row, 8), LANES:] = jnp.where(packed, edge, imag)

    edges_read[0].wait()
    inverse_blocks(work, store)
    for copy in started((chunk, out, left.at[0])):
        copy.wait()


def forward_columns_a(flags, model, edges, pairs, table_i):
    n = edges.shape[0]
    hbm = pl.BlockSpec(memory_space=pltpu.HBM)
    return pl.pallas_call(
        forward_kernel_a,
        out_shape=pltpu.HBM((n, 2 * LANES), f32),
        in_specs=[pl.BlockSpec(memory_space=pltpu.SMEM), hbm, hbm, hbm, hbm],
        out_specs=hbm,
        scratch_shapes=[
            WORK,
            WORK,
            pltpu.VMEM((n, LANES), f32),
            pairs_like(n),
            TABLE,
            pltpu.VMEM((n, 2 * LANES), f32),
            SIGNALS,
            SIGNALS,
            SIGNALS,
            pltpu.SemaphoreType.DMA((2,)),
        ],
        compiler_params=pltpu.CompilerParams(vmem_limit_bytes=26 << 20),
        cost_estimate=pl.CostEstimate(flops=0, bytes_accessed=16_000_000, transcendentals=0),
        name="forward_columns_a",
    )(flags, in_hbm(model), in_hbm(edges), in_hbm(pairs), in_hbm(table_i))


def gradient_kernel(
    counts, listing, spectra, table, gradient, outgoing,
    here, arrived, held_table, ready, lhs_high, lhs_low, held, blocks, compact, segments, left, sent,
):
    s = pl.program_id(0)
    rows, n = gradient.shape
    fetched = (spectra, here, arrived, table, held_table, ready)
    owners, cap, _ = outgoing.shape
    width = n // 2 // TILES_Y

    def pieces(quad):
        parts = quad_transpose([here[4 * quad + index] for index in range(4)])
        return jnp.concatenate(
            [jnp.concatenate([parts[0], parts[2]], axis=0), jnp.concatenate([parts[1], parts[3]], axis=0)],
            axis=1,
        )

    def leave(step, side):
        place = (slice(None), pl.ds(side * (n // 2) + step * width, width))
        return pltpu.make_async_copy(held.at[2 * step + side], gradient.at[place], left.at[2 * step + side])

    @pl.when(s == 0)
    def _():
        gather_columns(pieces, fetched, lhs_high, lhs_low)

    halves = half_rows(lhs_high, lhs_low, fetched)
    for step in range(TILES_Y):

        @pl.when(s == step)
        def _():
            for side in range(2):
                held[2 * step + side] = halves[side]
                leave(step, side).start()
                for q in range(width // LANES):
                    place = side * (RADIX // 2) + step * (width // LANES) + q
                    blocks[place * rows : (place + 1) * rows, :] = halves[side][:, q * LANES : (q + 1) * LANES]

    @pl.when(s == TILES_Y - 1)
    def _():
        total = lax.fori_loop(0, owners, lambda o, t: t + counts[o], jnp.int32(0))

        full = total == blocks.shape[0]

        @pl.when(full)
        def _():
            for q in range(RADIX):
                compact[pl.ds(q, rows, stride=RADIX), :] = blocks[q * rows : (q + 1) * rows, :]

        @pl.loop(0, jnp.where(full, 0, lax.div(total + 15, 16)))
        def _(step):
            for index in range(16):
                at = step * 16 + index
                compact[pl.ds(at, 1), :] = blocks[pl.ds(listing[at], 1), :]

        copies = []
        offset = 0
        for o in range(owners):
            segments[o] = compact[pl.ds(offset, cap), :]
            copies.append(pltpu.make_async_copy(segments.at[o], outgoing.at[o], sent.at[o]))
            copies[-1].start()
            offset = offset + counts[o]
        for copy in copies:
            copy.wait()
        for step in range(TILES_Y):
            for side in range(2):
                leave(step, side).wait()


def gradient_rows(counts, listing, spectra, table, rows, n, cap):
    owners = counts.shape[0]
    smem = pl.BlockSpec(memory_space=pltpu.SMEM)
    hbm = pl.BlockSpec(memory_space=pltpu.HBM)
    block_count = listing.shape[0]
    return pl.pallas_call(
        gradient_kernel,
        grid=(TILES_Y,),
        out_shape=[pltpu.HBM((rows, n), f32), pltpu.HBM((owners, cap, LANES), f32)],
        in_specs=[
            smem,
            smem,
            pl.BlockSpec(memory_space=pl.ANY),
            hbm,
        ],
        out_specs=[hbm, hbm],
        scratch_shapes=row_scratch(spectra, rows, n)
        + [
            pltpu.VMEM((2 * TILES_Y, rows, n // 2 // TILES_Y), f32),
            pltpu.VMEM((block_count, LANES), f32),
            pltpu.VMEM((block_count + cap, LANES), f32),
            pltpu.VMEM((owners, cap, LANES), f32),
            pltpu.SemaphoreType.DMA((2 * TILES_Y,)),
            pltpu.SemaphoreType.DMA((owners,)),
        ],
        compiler_params=pltpu.CompilerParams(vmem_limit_bytes=26 << 20),
        name="gradient_rows",
    )(counts, listing, spectra, in_hbm(table))


def owner_segments(counts, incoming, current, weights, room, scales, keep):
    sources, cap, _ = incoming.shape
    length = current.shape[0]
    room[:length, :] = current[...]
    room[length:, :] = jnp.zeros_like(room[length:, :])
    scales[:length, :] = weights[...].astype(f32) * step_size
    scales[length:, :] = jnp.zeros_like(scales[length:, :])
    begin = 0
    for p in range(sources):
        before = room[pl.ds(begin, cap), :]
        after = jnp.clip(before - scales[pl.ds(begin, cap), :] * incoming[p], -1.0, 1.0)
        keep(p, begin, before, after)
        begin = begin + counts[p]


def owner_send_kernel(counts, incoming, current, weights, updated, room, scales):
    def keep(p, begin, before, after):
        updated[p] = after

    owner_segments(counts, incoming, current, weights, room, scales, keep)


def owner_keep_kernel(counts, incoming, current, weights, model_new, room, scales):
    row = lax.broadcasted_iota(jnp.int32, incoming.shape[1:], 0)

    def keep(p, begin, before, after):
        room[pl.ds(begin, before.shape[0]), :] = jnp.where(row < counts[p], after, before)

    owner_segments(counts, incoming, current, weights, room, scales, keep)
    model_new[...] = room[: current.shape[0], :]


def owner_call(kernel, name, shape, counts, incoming, current, weights):
    sources, cap, _ = incoming.shape
    length = current.shape[0]
    return pl.pallas_call(
        kernel,
        out_shape=jax.ShapeDtypeStruct(shape, f32),
        in_specs=[pl.BlockSpec(memory_space=pltpu.SMEM)] + [pl.BlockSpec(memory_space=pltpu.VMEM)] * 3,
        scratch_shapes=[pltpu.VMEM((length + cap, LANES), f32)] * 2,
        compiler_params=pltpu.CompilerParams(vmem_limit_bytes=16 << 20),
        name=name,
    )(counts, incoming, current, weights)


def copy_kernel(source, target):
    target[...] = source[...]


def copied(value):
    rows, n = value.shape
    block = pl.BlockSpec((rows // 4, n), lambda s: (s, 0))
    return pl.pallas_call(
        copy_kernel,
        grid=(4,),
        out_shape=pltpu.HBM(value.shape, value.dtype),
        in_specs=[block],
        out_specs=block,
        cost_estimate=pl.CostEstimate(flops=0, bytes_accessed=4_000_000, transcendentals=0),
        name="copied",
    )(in_hbm(value))


def model_rows_kernel(counts, listing, returned, high, low, out, compact, grid, halves_high, halves_low):
    s = pl.program_id(0)
    owners, cap, _ = returned.shape
    rows = halves_high.shape[1]

    @pl.when(s == 0)
    def _():
        offset = 0
        for o in range(owners):
            compact[pl.ds(offset, cap), :] = returned[o]
            offset = offset + counts[o]
        full = offset == grid.shape[0]
        total = jnp.where(full, 0, offset)

        @pl.when(full)
        def _():
            for q in range(RADIX):
                grid[q * rows : (q + 1) * rows, :] = compact[pl.ds(q, rows, stride=RADIX), :]

        @pl.when(jnp.logical_not(full))
        def _():
            grid[...] = jnp.zeros_like(grid)

        @pl.loop(0, lax.div(total, 8))
        def _(step):
            for index in range(8):
                at = step * 8 + index
                grid[pl.ds(listing[at], 1), :] = compact[pl.ds(at, 1), :]

        @pl.loop(lax.div(total, 8) * 8, total)
        def _(at):
            grid[pl.ds(listing[at], 1), :] = compact[pl.ds(at, 1), :]

        half = RADIX // 2
        for q in range(half):
            first = grid[q * rows : (q + 1) * rows, :]
            second = grid[(q + half) * rows : (q + half + 1) * rows, :]
            for index, combined in enumerate((first + second, first - second)):
                top, rest = split(combined)
                halves_high[index, :, q * LANES : (q + 1) * LANES] = top
                halves_low[index, :, q * LANES : (q + 1) * LANES] = rest

    side = s // (pl.num_programs(0) // 2)
    result = dot3((halves_high[side], halves_low[side]), (high[0], low[0]))
    half = rows // 2
    parts = quad_transpose(
        [result[:half, :LANES], result[:half, LANES:], result[half:, :LANES], result[half:, LANES:]]
    )
    for index in range(4):
        out[index] = parts[index]


def model_rows(counts, listing, returned, tables, rows, n, devices):
    owners, cap, _ = returned.shape
    block_count = listing.shape[0]
    smem = pl.BlockSpec(memory_space=pltpu.SMEM)
    table = pl.BlockSpec((1, n // 2, 2 * LANES), lambda s: (s, 0, 0))
    return pl.pallas_call(
        model_rows_kernel,
        grid=(devices // 4,),
        out_shape=pltpu.HBM((devices, rows // 2, LANES), f32),
        in_specs=[
            smem,
            smem,
            pl.BlockSpec((owners, cap, LANES), lambda s: (0, 0, 0)),
            table,
            table,
        ],
        out_specs=pl.BlockSpec((4, rows // 2, LANES), lambda s: (s, 0, 0)),
        scratch_shapes=[
            pltpu.VMEM((block_count + cap, LANES), f32),
            pltpu.VMEM((block_count, LANES), f32),
            pltpu.VMEM((2, rows, n // 2), bf16),
            pltpu.VMEM((2, rows, n // 2), bf16),
        ],
        compiler_params=pltpu.CompilerParams(vmem_limit_bytes=16 << 20),
        name="model_rows",
    )(counts, listing, returned, *tables)


def in_hbm(value):
    return pltpu.with_memory_space_constraint(value, pltpu.HBM)


def swap_all(value, axes):
    return lax.all_to_all(value, axes, split_axis=0, concat_axis=0, tiled=True)


def local_paired(misfit, kernel_spec, model_vec, weight_vec, active_list, send_counts):
    both = ("pen", "dep")
    pen_count = lax.axis_size("pen")
    devices = pen_count * lax.axis_size("dep")
    channels, rows, n = misfit.shape
    band = n // pen_count
    forward_np, inverse_np = row_tables(n, devices)
    row_forward = tuple(map(jnp.asarray, forward_np))
    row_inverse = jnp.asarray(np.stack(inverse_np, axis=2))
    forward_np, inverse_np = column_tables()
    col_forward = jnp.asarray(np.stack(forward_np, axis=1))
    col_inverse = jnp.asarray(np.stack(inverse_np, axis=1))
    me = lax.axis_index(both)
    half = devices // 2
    flags = jnp.stack([(me >= half).astype(jnp.int32), (me == 0).astype(jnp.int32)])
    counts = send_counts.reshape(pen_count)
    listing = active_list.reshape(-1)
    places = (listing & (RADIX - 1)) * band + (listing >> 4)
    owner_length = model_vec.shape[2]
    cap = owner_length // pen_count

    spec = kernel_spec.reshape((-1,) + kernel_spec.shape[2:])
    partner = [(d, devices - 1 - d) for d in range(devices)]
    got_b = lax.ppermute(part_spec(flags, spec, 8, 12), both, partner)
    sent_a = part_spec(flags, spec, 0, 8)
    got_a = lax.ppermute(sent_a, both, partner)
    edge = lax.ppermute(
        spec[:, 0:1, :].astype(f32), both, [(d, (devices - d) % half) for d in range(half, devices)]
    )
    source_counts = swap_all(counts, "pen")

    misfit, _ = lax.optimization_barrier((misfit, sent_a))
    chunk_a, chunk_b = misfit_rows(misfit, row_forward, devices)
    chunk_a, got_b, edge, source_counts = lax.optimization_barrier((chunk_a, got_b, edge, source_counts))
    chunk_b, got_a, got_b, edge = lax.optimization_barrier((chunk_b, got_a, got_b, edge))
    columns_a = swap_all(chunk_a, both).reshape(n, 2 * LANES)
    columns_b = swap_all(chunk_b, both).reshape(n, LANES)
    pairs = pair_spec(flags, spec, got_a, got_b, edge)
    sums, edges = adjoint_columns_a(flags, columns_a, pairs, col_forward)
    fields = adjoint_columns_b(flags, columns_b, edges, sums, pairs, col_forward, col_inverse)
    gradient, outgoing = gradient_rows(
        counts, places, swap_all(fields, both), row_inverse, band, n, cap
    )
    outgoing, gradient = lax.optimization_barrier((outgoing, gradient))
    incoming = swap_all(outgoing, "pen")
    gradient, source_counts = lax.optimization_barrier((copied(gradient), source_counts))
    owned = (
        source_counts,
        incoming,
        model_vec.reshape(owner_length, LANES),
        weight_vec.reshape(owner_length, LANES),
    )
    updated = owner_call(owner_send_kernel, "owner_send", incoming.shape, *owned)
    updated, incoming = lax.optimization_barrier((updated, incoming))
    returned = swap_all(updated, "pen")
    model_chunks = model_rows(counts, places, returned, row_forward, band, n, devices)
    model_chunks, incoming = lax.optimization_barrier((model_chunks, incoming))
    moved = swap_all(model_chunks, both)
    model_new = owner_call(
        owner_keep_kernel, "owner_keep", (owner_length, LANES), owned[0], incoming, *owned[2:]
    )
    model_new, flags = lax.optimization_barrier((model_new, flags))
    out_b, edges, model = forward_columns_b(
        flags, moved, pairs, col_forward, col_inverse, n
    )
    back_b = swap_all(out_b.reshape(devices, rows, LANES), both)
    out_a = forward_columns_a(flags, model, edges, pairs, col_inverse)
    back_a = swap_all(out_a.reshape(devices, rows, 2 * LANES), both)
    predicted = predicted_rows(back_b, row_inverse, None, n)
    predicted = predicted_rows(back_a, row_inverse, predicted, n)
    return (gradient[None], model_new.reshape(model_vec.shape), predicted)


def local(misfit, kernel_spec, model_vec, weight_vec, active_list, send_counts):
    sizes = tuple(lax.axis_size(name) for name in ("pen", "dep", "chan"))
    if sizes == (16, 2, 1) and misfit.shape == (6, 64, RADIX * LANES) and kernel_spec.shape[1] == 2:
        plan = local_paired
    else:
        plan = local_general
    return plan(misfit, kernel_spec, model_vec, weight_vec, active_list, send_counts)


def solution(mesh):
    return jax.shard_map(
        local,
        mesh=mesh,
        in_specs=(
            P(("grp", "chan"), ("pen", "dep"), None),
            P("chan", None, ("pen", "dep"), None),
            P(("grp", "dep", "chan"), "pen", None, None),
            P(("grp", "dep", "chan"), "pen", None, None),
            P(("grp", "dep", "chan"), "pen", None),
            P(("grp", "dep", "chan"), "pen", None),
        ),
        out_specs=(
            P(("grp", "dep", "chan"), "pen", None),
            P(("grp", "dep", "chan"), "pen", None, None),
            P(("grp", "chan"), ("pen", "dep"), None),
        ),
        check_vma=False,
    )
```
